32 devices in a mesh: seq: 8 (over z, x), ch: 4 (over y, core).
Axes of the slice: x: 2, y: 2, z: 4, core: 2. Of those that a mesh axis runs over, the one named last changes fastest.
Arguments:
- tokens: float32 [8192, 1280], P('seq'), may hold values from -6 to 6
- cotangent: float32 [8192, 1280], P('seq', 'ch'), may hold values from -6 to 6
- lengths: int32 [16], replicated, may hold values from 30 to 1024, as said below
- valid_mask: int32 [8192], P('seq'), may hold values from 0 to 1, as said below
- weight_first: float32 [1280, 640], P(None, 'ch'), may hold values from -0.15625 to 0.15625
- weight_dilated: float32 [5, 640, 640], P(None, None, 'ch'), may hold values from -0.109375 to 0.109375
- weight_last: float32 [640, 1280], P('ch'), may hold values from -0.25 to 0.25
- momentum_first: float32 [1280, 640], P(None, 'ch'), may hold values from -320 to 320
- momentum_dilated: float32 [5, 640, 640], P(None, None, 'ch'), may hold values from -320 to 320
- momentum_last: float32 [640, 1280], P('ch'), may hold values from -320 to 320
- vector_params: float32 [7680], replicated, may hold values from -2 to 2
- vector_moment: float32 [7680], replicated, may hold values from -32 to 32
- vector_square: float32 [7680], replicated, may hold values from 2.94912 to 11.79648
Outputs:
- block_output: float32 [8192, 1280], P('seq', 'ch')
- tokens_grad: float32 [8192, 1280], P('seq', 'ch')
- first_weight: float32 [1280, 640], P(None, 'ch')
- dilated_weight: float32 [5, 640, 640], P(None, None, 'ch')
- last_weight: float32 [640, 1280], P('ch')
- first_momentum: float32 [1280, 640], P(None, 'ch')
- dilated_momentum: float32 [5, 640, 640], P(None, None, 'ch')
- last_momentum: float32 [640, 1280], P('ch')
- vector_first: float32 [7680], replicated
- vector_second: float32 [7680], replicated
- vector_values: float32 [7680], replicated
- root_means: float32 [2], replicated
The draws below stay inside these ranges and needn't reach their ends.
Inputs may be any that keep to these rules, and one draw needn't show every extreme that they name: The lengths sum to 8192; the largest is exactly 1024. `valid_mask`: position 0 is valid.
All inputs are finite; a program needn't handle non-finite values.
Results may differ from the reference program's by a relative error of at most 0.0081.
Values may be sent and summed in bfloat16 or wider, within the bound.
No kernel may reach another device: no remote copies, remote signals or barrier semaphores. Data moves between devices by JAX's collectives and lax.ppermute only.
A program may use at most 256 MiB of HBM per device.

```python
import math
import jax
import jax.numpy as jnp
from jax import lax

D = 1280
INNER = 640
KERNEL_TAPS = 5
DILATION_SPAN = 128
MAX_RESIDUE_SIZE = 1024
MIN_PROTEIN_SIZE = 30
STEP = 10
TOK_DEV = 1024
TOKENS = 8192
NPROT = 16
SMALL = 7680
N_SEQ = 8


def draw_lengths(key, part):
    weight_key = jax.random.fold_in(key, 11)
    place_key = jax.random.fold_in(key, 12)
    slots = jnp.arange(NPROT, dtype=jnp.int32)
    longest = jax.random.randint(place_key, (), 0, NPROT).astype(jnp.int32)
    foreign_lines = slots != longest
    shares = jnp.where(foreign_lines, jax.random.randint(weight_key, (NPROT,), 8, 17), 0).astype(jnp.int32)
    spare = TOKENS - MAX_RESIDUE_SIZE - (NPROT - 1) * MIN_PROTEIN_SIZE
    surplus_lines = spare * shares // jnp.sum(shares)
    remaining_lines = spare - jnp.sum(surplus_lines)
    worker_ordinal = jnp.cumsum(foreign_lines.astype(jnp.int32)) - 1
    surplus_count = (foreign_lines & (worker_ordinal < remaining_lines)).astype(jnp.int32)
    closing_output = jnp.where(foreign_lines, MIN_PROTEIN_SIZE + surplus_lines + surplus_count, MAX_RESIDUE_SIZE)
    return closing_output.astype(jnp.int32)


def draw_valid_mask(key, part):
    codes = jax.random.randint(key, (TOKENS,), 0, 8)
    marks = (codes < 7).astype(jnp.int32)
    return jnp.where(jnp.arange(TOKENS) == 0, 1, marks).astype(jnp.int32)


def draw_vector_params(key, part):
    keys = jax.random.split(key, 9)
    widths = [D, D, INNER, INNER, INNER, INNER, INNER, INNER, D]
    kinds = [1, 0, 0, 1, 0, 0, 1, 0, 0]
    pieces = []
    for index_piece in range(9):
        column_count = widths[index_piece]
        if kinds[index_piece] == 1:
            ramp = 0.5 + jnp.arange(column_count, dtype=jnp.float32) / column_count
            factor = jax.random.uniform(keys[index_piece], (column_count,), jnp.float32, 0.8, 1.2)
            pieces.append(ramp * factor)
        else:
            pieces.append(0.3 * jnp.clip(jax.random.normal(keys[index_piece], (column_count,), jnp.float32), -4.0, 4.0))
    return jnp.concatenate(pieces).astype(jnp.float32)


def levels(rng, shape, shards, low, largest):
    factor_of = 1.0
    for dim, shards_of in shards:
        draws = jax.random.uniform(jax.random.fold_in(jax.random.fold_in(rng, 6), dim), (shards_of,), jnp.float32, low / len(shards), largest / len(shards))
        factor_of = factor_of * jnp.repeat(jnp.exp(draws), shape[dim] // shards_of).reshape((-1,) + (1,) * (len(shape) - 1 - dim))
    return factor_of


def centred(own_key, shape, deviation, limit, cuts=(), kind=jnp.bfloat16):
    array = jax.random.normal(own_key, shape, jnp.float32) * deviation
    if len(cuts) > 0:
        array = levels(own_key, shape, cuts, -0.22, 0.18) * array
    return jnp.clip(array, min=-limit, max=limit).astype(kind)


def setup_inputs(seed: int = 0) -> dict:
    key_of = jax.random.split(jax.random.key(seed), 14)
    tokens = centred(key_of[0], (TOKENS, D), 1.0, 6.0, ((0, 8),), jnp.float32)
    cotangent = centred(key_of[1], (TOKENS, D), 1.0, 6.0, ((0, 8), (1, 4)), jnp.float32)
    lengths = draw_lengths(jax.random.fold_in(key_of[13], 71), 0)
    valid_mask = draw_valid_mask(jax.random.fold_in(key_of[13], 71), 0)
    weight_first = centred(key_of[4], (D, INNER), D ** -0.5, 0.15625, ((1, 4),), jnp.float32)
    weight_dilated = centred(key_of[5], (KERNEL_TAPS, INNER, INNER), (KERNEL_TAPS * INNER) ** -0.5, 0.109375, ((2, 4),), jnp.float32)
    weight_last = centred(key_of[6], (INNER, D), INNER ** -0.5, 0.25, ((0, 4),), jnp.float32)
    momentum_first = centred(key_of[7], (D, INNER), (0.6 * (TOK_DEV * N_SEQ) ** 0.5), 320.0, ((1, 4),), jnp.float32)
    momentum_dilated = centred(key_of[8], (KERNEL_TAPS, INNER, INNER), (0.6 * (TOK_DEV * N_SEQ) ** 0.5), 320.0, ((2, 4),), jnp.float32)
    momentum_last = centred(key_of[9], (INNER, D), (0.6 * (TOK_DEV * N_SEQ) ** 0.5), 320.0, ((0, 4),), jnp.float32)
    vector_params = draw_vector_params(jax.random.fold_in(key_of[13], 71), 0)
    vector_moment = centred(key_of[11], (SMALL,), (0.066 * (TOK_DEV * N_SEQ) ** 0.5), 32.0, (), jnp.float32)
    vector_square = jnp.clip(jnp.exp(jax.random.uniform(key_of[12], (SMALL,), jnp.float32, math.log(2.94912), math.log(11.79648))), 2.94912, 11.79648)
    return dict(tokens=tokens, cotangent=cotangent, lengths=lengths, valid_mask=valid_mask, weight_first=weight_first, weight_dilated=weight_dilated, weight_last=weight_last, momentum_first=momentum_first, momentum_dilated=momentum_dilated, momentum_last=momentum_last, vector_params=vector_params, vector_moment=vector_moment, vector_square=vector_square)


@jax.custom_vjp
def low(v):
    return lax.optimization_barrier(v.astype(jnp.bfloat16)).astype(jnp.float32)

@jax.custom_vjp
def low_back(v):
    return v

def low_keep(v):
    return (low(v), None)

def low_pass(kept, grad):
    return (grad,)

def back_keep(v):
    return (v, None)

def back_low(kept, grad):
    return (low(grad),)
low.defvjp(low_keep, low_pass)
low_back.defvjp(back_keep, back_low)
norm_eps = 1e-05
coef_first = 3.4445
coef_second = -4.775
coef_third = 2.0315
adam_rate = 0.4
adam_first = 0.9
adam_second = 0.999
adam_eps = 1e-08
decay_rate = 0.01
muon_rate = 0.1
muon_keep = 0.95
muon_scale = 0.2
highest = lax.Precision.HIGHEST

def smooth_gate(values):
    return jax.nn.gelu(values, approximate=False)

def norm_rows(values, gain, shift):
    center = lax.optimization_barrier(jnp.mean(values, axis=1, keepdims=True))
    square = lax.optimization_barrier(jnp.mean(values * values, axis=1, keepdims=True)) - center * center
    return (values - center) * lax.rsqrt(square + norm_eps) * gain + shift

def segment_of(lengths, positions):
    bounds = jnp.cumsum(lengths).astype(jnp.int32)
    return lax.optimization_barrier(jnp.sum((positions[:, None] >= bounds[None, :]).astype(jnp.int32), axis=1)).astype(jnp.int32)

def split_vector(vector):
    widths = [D, D, INNER, INNER, INNER, INNER, INNER, INNER, D]
    pieces = []
    tap_offset = 0
    for column_count in widths:
        pieces.append(vector[tap_offset:tap_offset + column_count])
        tap_offset = tap_offset + column_count
    return pieces

def tap_masks(lengths):
    positions = jnp.arange(TOKENS, dtype=jnp.int32)
    segment = segment_of(lengths, positions)
    masks = []
    for kernel_tap_index in range(KERNEL_TAPS):
        tap_offset = (kernel_tap_index - KERNEL_TAPS // 2) * DILATION_SPAN
        moved_rows = positions + tap_offset
        inside = (moved_rows >= 0) & (moved_rows < TOKENS)
        clipped = jnp.clip(moved_rows, 0, TOKENS - 1).astype(jnp.int32)
        masks.append((inside & (segment[clipped] == segment)).astype(jnp.float32))
    return masks

def forward(tokens, weight_first, weight_dilated, weight_last, vector_params, valid, masks):
    gain_one, shift_one, bias_one, gain_two, shift_two, bias_two, gain_three, shift_three, bias_three = split_vector(vector_params)
    hidden_one = low(smooth_gate(norm_rows(tokens, gain_one, shift_one)))
    inner_one = low_back(jnp.dot(hidden_one, low(weight_first), precision=highest, preferred_element_type=jnp.float32)) + bias_one
    hidden_two = low(smooth_gate(norm_rows(inner_one, gain_two, shift_two)) * valid[:, None])
    kernel = low(weight_dilated)
    neighbour_rows = KERNEL_TAPS // 2 * DILATION_SPAN
    padded = jnp.pad(hidden_two, ((neighbour_rows, neighbour_rows), (0, 0)))
    summed = jnp.zeros((TOKENS, INNER), jnp.float32)
    for kernel_tap_index in range(KERNEL_TAPS):
        tap_offset = neighbour_rows + (kernel_tap_index - KERNEL_TAPS // 2) * DILATION_SPAN
        product = jnp.dot(padded[tap_offset:tap_offset + TOKENS], kernel[kernel_tap_index], precision=highest, preferred_element_type=jnp.float32)
        summed = summed + masks[kernel_tap_index][:, None] * product
    inner_two = low_back(summed) + bias_two
    hidden_three = low(smooth_gate(norm_rows(inner_two, gain_three, shift_three)))
    branch = low_back(jnp.dot(hidden_three, low(weight_last), precision=highest, preferred_element_type=jnp.float32)) + bias_three
    return (tokens + branch, branch)

def orthogonal(matrix):
    rows_count, cols_count = matrix.shape
    work = matrix / (jnp.sqrt(jnp.sum(matrix * matrix)) + 1e-07)
    for sweep_index in range(5):
        if rows_count >= cols_count:
            gram = jnp.dot(work.T, work, precision=highest, preferred_element_type=jnp.float32)
            poly = coef_second * gram + coef_third * jnp.dot(gram, gram, precision=highest, preferred_element_type=jnp.float32)
            work = coef_first * work + jnp.dot(work, poly, precision=highest, preferred_element_type=jnp.float32)
        else:
            gram = jnp.dot(work, work.T, precision=highest, preferred_element_type=jnp.float32)
            poly = coef_second * gram + coef_third * jnp.dot(gram, gram, precision=highest, preferred_element_type=jnp.float32)
            work = coef_first * work + jnp.dot(poly, work, precision=highest, preferred_element_type=jnp.float32)
    return work * (muon_scale * math.sqrt(max(rows_count, cols_count)))

def reference(tokens, cotangent, lengths, valid_mask, weight_first, weight_dilated, weight_last, momentum_first, momentum_dilated, momentum_last, vector_params, vector_moment, vector_square):
    valid = valid_mask.astype(jnp.float32)
    masks = tap_masks(lengths)

    def closed(tokens_in, first_in, dilated_in, last_in, vector_in):
        return forward(tokens_in, first_in, dilated_in, last_in, vector_in, valid, masks)
    block_output, pullback, branch = jax.vjp(closed, tokens, weight_first, weight_dilated, weight_last, vector_params, has_aux=True)
    tokens_grad, grad_first, grad_dilated, grad_last, grad_vector = pullback(cotangent)
    keep_weight = 1.0 - muon_rate * decay_rate
    first_momentum = muon_keep * momentum_first + grad_first
    first_weight = weight_first * keep_weight - muon_rate * orthogonal(first_momentum)
    dilated_momentum = muon_keep * momentum_dilated + grad_dilated
    dilated_steps = jnp.stack([orthogonal(dilated_momentum[kernel_tap_index]) for kernel_tap_index in range(KERNEL_TAPS)])
    dilated_weight = weight_dilated * keep_weight - muon_rate * dilated_steps
    last_momentum = muon_keep * momentum_last + grad_last
    last_weight = weight_last * keep_weight - muon_rate * orthogonal(last_momentum)
    vector_first = adam_first * vector_moment + (1.0 - adam_first) * grad_vector
    vector_second = adam_second * vector_square + (1.0 - adam_second) * grad_vector * grad_vector
    corrected_first = vector_first / (1.0 - adam_first ** STEP)
    corrected_second = vector_second / (1.0 - adam_second ** STEP)
    vector_values = vector_params - adam_rate * (corrected_first / (jnp.sqrt(corrected_second) + adam_eps) + decay_rate * vector_params)
    count = jnp.sum(valid)
    output_square = jnp.sum(valid[:, None] * block_output * block_output)
    branch_square = jnp.sum(valid[:, None] * branch * branch)
    root_means = jnp.stack([jnp.sqrt(output_square / (count * D)), jnp.sqrt(branch_square / (count * D))])
    return (block_output, tokens_grad, first_weight, dilated_weight, last_weight, first_momentum, dilated_momentum, last_momentum, vector_first, vector_second, vector_values, root_means)
```

```python
import functools
import math

import jax
import jax.numpy as jnp
from jax import lax
from jax.experimental import pallas as pl
from jax.experimental.pallas import tpu as pltpu
from jax.sharding import PartitionSpec as P

D = 1280
INNER = 640
KERNEL_TAPS = 5
DILATION_SPAN = 128
STEP = 10

norm_eps = 1e-05
coef_first = 3.4445
coef_second = -4.775
coef_third = 2.0315
adam_rate = 0.4
adam_first = 0.9
adam_second = 0.999
adam_eps = 1e-08
decay_rate = 0.01
muon_rate = 0.1
muon_keep = 0.95
muon_scale = 0.2
REACH = KERNEL_TAPS // 2 * DILATION_SPAN
VECTOR = 3 * D + 6 * INNER
HALF_D = D // 2
MIB = 1024 * 1024

f32 = jnp.float32
bf16 = jnp.bfloat16
NN = (((1,), (0,)), ((), ()))
NT = (((1,), (1,)), ((), ()))
TN = (((0,), (0,)), ((), ()))


def mul(a, b, dims):
    return lax.dot_general(a, b, dims, preferred_element_type=f32)


def erf_parts(v):
    a = jnp.abs(v) * math.sqrt(0.5)
    t = pl.reciprocal(1.0 + 0.3275911 * a)
    e = jnp.exp(-a * a)
    p = t * (0.254829592 + t * (-0.284496736 + t * (1.421413741 + t * (-1.453152027 + t * 1.061405429))))
    tail = 0.5 * p * e
    return jnp.where(v >= 0, 1.0 - tail, tail), e


def gelu_pair(v):
    cdf, e = erf_parts(v)
    return v * cdf, cdf + v * e * (1.0 / math.sqrt(2.0 * math.pi))


VMEM = pl.BlockSpec(memory_space=pltpu.VMEM)
SMEM = pl.BlockSpec(memory_space=pltpu.SMEM)


def call(kernel, outs, scalars, arrays, scratch=(), limit=24, flops=10**8):
    shapes = [jax.ShapeDtypeStruct(shape, dtype) for shape, dtype in outs]
    size = sum(math.prod(shape) * jnp.dtype(dtype).itemsize for shape, dtype in outs)
    size += sum(a.size * a.dtype.itemsize for a in arrays)
    return pl.pallas_call(
        kernel,
        out_shape=shapes,
        in_specs=[SMEM] * len(scalars) + [VMEM] * len(arrays),
        out_specs=[VMEM] * len(outs),
        scratch_shapes=[pltpu.VMEM(shape, dtype) for shape, dtype in scratch],
        compiler_params=pltpu.CompilerParams(vmem_limit_bytes=limit * MIB),
        cost_estimate=pl.CostEstimate(flops=flops, bytes_accessed=size, transcendentals=0),
    )(*scalars, *arrays)


def chunks(count, step):
    return [pl.ds(i, step) for i in range(0, count, step)]


def at(index, count, step=32):
    return pl.ds(pl.multiple_of(index * count, step), count)


def prep_kernel(idx, w_ref, cot_ref, wo_ref, mine_ref, other_ref, sums_ref):
    k = idx[0]
    half = mine_ref.shape[1]
    for r in chunks(w_ref.shape[0], 32):
        wo_ref[r, :] = w_ref[r, :].astype(bf16)
    for r in chunks(cot_ref.shape[0], 32):
        v = cot_ref[r, :]
        sums_ref[r, :] = jnp.broadcast_to(jnp.sum(v, axis=1, keepdims=True), (32, 128))
        mine_ref[r, :] = cot_ref[r, at(k, half, 128)].astype(bf16)
        other_ref[r, :] = cot_ref[r, at(1 - k, half, 128)].astype(bf16)


def rest_kernel(last_ref, taps_ref, o_ref):
    for r in chunks(last_ref.shape[0], 32):
        o_ref[r, :D] = last_ref[r, :].astype(bf16)
        for j in range(KERNEL_TAPS):
            o_ref[r, D + j * INNER : D + (j + 1) * INNER] = taps_ref[j, r, :].astype(bf16)


def input_kernel(idx, tok_ref, gs_ref, hid_ref, hat_ref, slope_ref, scale_ref):
    for r in chunks(tok_ref.shape[0], 16):
        v = tok_ref[r, :]
        center = jnp.sum(v, axis=1, keepdims=True) * (1.0 / D)
        square = jnp.sum(v * v, axis=1, keepdims=True) * (1.0 / D)
        scale = lax.rsqrt(square - center * center + norm_eps)
        hat = (v - center) * scale
        hid, slope = gelu_pair(hat * gs_ref[0:1, :] + gs_ref[1:2, :])
        hid_ref[r, :] = hid.astype(bf16)
        hat_ref[r, :] = hat.astype(bf16)
        slope_ref[r, :] = slope.astype(bf16)
        scale_ref[r, :] = jnp.broadcast_to(scale, (16, 128))


def put_stats(ref, parts):
    for i, part in enumerate(parts):
        ref[i : i + 1, :] = part


def first_kernel(idx, own_ref, got_ref, hid_ref, cols_ref, w_ref, inner_ref, st_ref):
    k = idx[0]
    loc = own_ref.shape[0]
    w_ref[at(k, loc), :] = own_ref[...]
    w_ref[at(1 - k, loc), :] = got_ref[...]
    v = mul(w_ref[...], hid_ref[...], NT) + cols_ref[:, 0:1]
    inner_ref[...] = v
    put_stats(st_ref, (jnp.sum(v, axis=0, keepdims=True), jnp.sum(v * v, axis=0, keepdims=True)))


def center_scale(st_ref, got_ref):
    center = (st_ref[0:1, :] + got_ref[0:1, :]) * (1.0 / INNER)
    square = (st_ref[1:2, :] + got_ref[1:2, :]) * (1.0 / INNER)
    return center, lax.rsqrt(square - center * center + norm_eps)


def second_kernel(idx, inner_ref, st_ref, got_ref, cols_ref, valid_ref, hid_ref, hat_ref, slope_ref):
    center, scale = center_scale(st_ref, got_ref)
    valid = valid_ref[:, at(idx[0], hid_ref.shape[1], 128)].astype(f32)
    for r in chunks(inner_ref.shape[0], 32):
        hat = (inner_ref[r, :] - center) * scale
        hid, slope = gelu_pair(hat * cols_ref[r, 1:2] + cols_ref[r, 2:3])
        hid_ref[r, :] = (hid * valid).astype(bf16)
        hat_ref[r, :] = hat
        slope_ref[r, :] = slope * valid


def slabs_of(k, v_ref, row, in_ref, out_ref):
    half = v_ref.shape[1]
    rows = v_ref.shape[0]
    in_ref[row, :] = v_ref[:, at(1 - k, half - REACH, 128)]
    out_ref[row, :] = v_ref[:, at(k, half - REACH, 128)]


def slab_kernel(idx, own_ref, got_ref, in_ref, out_ref):
    k, y = idx[0], idx[1]
    wide = own_ref.shape[0]
    slabs_of(k, own_ref, at(y, wide), in_ref, out_ref)
    slabs_of(k, got_ref, at(1 - y, wide), in_ref, out_ref)


def fill_reach(k, ext_ref, in_ref, out_ref, half):
    @pl.when(k == 0)
    def _():
        ext_ref[:, :REACH] = out_ref[...]
        ext_ref[:, REACH + half :] = in_ref[...]

    @pl.when(k == 1)
    def _():
        ext_ref[:, :REACH] = in_ref[...]
        ext_ref[:, REACH + half :] = out_ref[...]


def conv_kernel(
    total, idx, lengths, own_ref, got_ref, in_ref, out_ref, wo_ref, wg_ref, cols_ref,
    ext_ref, inner_ref, st_ref, last_ref, taps_ref, mask_ref, stack,
):
    k, y = idx[0], idx[1]
    wide, half = own_ref.shape
    loc = wo_ref.shape[0]
    ext_ref[at(y, wide), REACH : REACH + half] = own_ref[...]
    ext_ref[at(1 - y, wide), REACH : REACH + half] = got_ref[...]
    fill_reach(k, ext_ref, in_ref, out_ref, half)
    last_ref[at(k, loc), :] = wo_ref[:, :D]
    last_ref[at(1 - k, loc), :] = wg_ref[:, :D]
    taps_ref[at(k, loc), :] = wo_ref[:, D:]
    taps_ref[at(1 - k, loc), :] = wg_ref[:, D:]
    positions = idx[5] - REACH + lax.broadcasted_iota(jnp.int32, (1, half + 2 * REACH), 1)
    segment = jnp.zeros_like(positions)
    bound = jnp.int32(0)
    for i in range(lengths.shape[0]):
        bound = bound + lengths[i]
        segment = segment + (positions >= bound).astype(jnp.int32)
    segment = jnp.where((positions >= 0) & (positions < total), segment, -1)
    centre = segment[:, REACH : REACH + half]
    for j in range(KERNEL_TAPS):
        lanes = slice(j * DILATION_SPAN, j * DILATION_SPAN + half)
        mask = (segment[:, lanes] == centre).astype(f32)
        mask_ref[j : j + 1, :] = mask
        low = mask.astype(bf16)
        for i in range(0, INNER, 160):
            stack[j * INNER + i : j * INNER + i + 160, :] = ext_ref[i : i + 160, lanes] * low
    v = mul(taps_ref[...], stack[...], NN) + cols_ref[:, 3:4]
    inner_ref[...] = v
    put_stats(st_ref, (jnp.sum(v, axis=0, keepdims=True), jnp.sum(v * v, axis=0, keepdims=True)))


def cotangent_kernel(idx, last_ref, mine_ref, sib_ref, opp_ref, diag_ref, gw_ref, g_ref):
    k, y = idx[0], idx[1]
    col = mine_ref.shape[0]
    gw_ref[at(2 * y + k, col), :] = mine_ref[...]
    gw_ref[at(2 * y + 1 - k, col), :] = sib_ref[...]
    gw_ref[at(2 * (1 - y) + k, col), :] = opp_ref[...]
    gw_ref[at(2 * (1 - y) + 1 - k, col), :] = diag_ref[...]
    g_ref[...] = mul(last_ref[...], gw_ref[...], NN)


def third_kernel(inner_ref, st_ref, got_ref, cols_ref, g_ref, hid_ref, e_ref, hat_ref, part_ref):
    center, scale = center_scale(st_ref, got_ref)
    plain = jnp.zeros_like(center)
    cross = jnp.zeros_like(center)
    for r in chunks(inner_ref.shape[0], 32):
        hat = (inner_ref[r, :] - center) * scale
        gain = cols_ref[r, 4:5]
        hid, slope = gelu_pair(hat * gain + cols_ref[r, 5:6])
        hid_ref[r, :] = hid.astype(bf16)
        hat_ref[r, :] = hat
        e = slope * g_ref[r, :]
        e_ref[r, :] = e
        eg = e * gain
        plain = plain + jnp.sum(eg, axis=0, keepdims=True)
        cross = cross + jnp.sum(eg * hat, axis=0, keepdims=True)
    put_stats(part_ref, (plain, cross, scale))


def norm_back(r, e_ref, hat_ref, part_ref, got_ref, scale, gain, sums_ref):
    plain = (part_ref[0:1, :] + got_ref[0:1, :]) * (1.0 / INNER)
    cross = (part_ref[1:2, :] + got_ref[1:2, :]) * (1.0 / INNER)
    e, hat = e_ref[r, :], hat_ref[r, :]
    grad = scale * (e * gain - plain - hat * cross)
    sums_ref[r, 0:1] = jnp.sum(e * hat, axis=1, keepdims=True)
    sums_ref[r, 1:2] = jnp.sum(e, axis=1, keepdims=True)
    sums_ref[r, 2:3] = jnp.sum(grad, axis=1, keepdims=True)
    return grad


def third_back_kernel(idx, e_ref, hat_ref, part_ref, got_ref, cols_ref, dz_ref, in_ref, out_ref, sums_ref):
    for r in chunks(e_ref.shape[0], 32):
        grad = norm_back(r, e_ref, hat_ref, part_ref, got_ref, part_ref[2:3, :], cols_ref[r, 4:5], sums_ref)
        dz_ref[r, :] = grad.astype(bf16)
    slabs_of(idx[0], dz_ref, slice(None), in_ref, out_ref)


def split_rows(k, full, own_ref, send_ref, lanes):
    loc = own_ref.shape[0]
    own_ref[:, lanes] = full[at(k, loc), lanes]
    send_ref[:, lanes] = full[at(1 - k, loc), lanes].astype(bf16)


def grads_kernel(idx, dz_ref, ext_ref, mask_ref, hid_ref, gw_ref, own_ref, send_ref, full):
    k = idx[0]
    half = dz_ref.shape[1]
    full[:, :D] = mul(hid_ref[...], gw_ref[...], NT)
    split_rows(k, full, own_ref, send_ref, slice(0, D))
    for j in range(KERNEL_TAPS):
        masked = dz_ref[...] * mask_ref[j : j + 1, :].astype(bf16)
        moved = ext_ref[:, j * DILATION_SPAN : j * DILATION_SPAN + half]
        lanes = slice(D + j * INNER, D + (j + 1) * INNER)
        full[:, lanes] = mul(masked, moved, NT)
        split_rows(k, full, own_ref, send_ref, lanes)


def conv_back_kernel(idx, dz_ref, in_ref, out_ref, mask_ref, taps_ref, own_ref, send_ref, ext, full):
    k, y = idx[0], idx[1]
    wide, half = dz_ref.shape
    ext[:, REACH : REACH + half] = dz_ref[...]
    fill_reach(k, ext, in_ref, out_ref, half)
    total = None
    for j in range(KERNEL_TAPS):
        begin = REACH - (j - KERNEL_TAPS // 2) * DILATION_SPAN
        mask = mask_ref[KERNEL_TAPS - 1 - j : KERNEL_TAPS - j, :].astype(bf16)
        part = mul(taps_ref[:, j * INNER : (j + 1) * INNER], ext[:, begin : begin + half] * mask, TN)
        total = part if total is None else total + part
    full[...] = total
    own_ref[...] = full[at(y, wide), :]
    send_ref[...] = full[at(1 - y, wide), :].astype(bf16)


def second_back_kernel(own_ref, got_ref, slope_ref, hat_ref, cols_ref, e_ref, part_ref):
    plain = jnp.zeros((1, own_ref.shape[1]), f32)
    cross = jnp.zeros_like(plain)
    for r in chunks(own_ref.shape[0], 32):
        e = slope_ref[r, :] * (own_ref[r, :] + got_ref[r, :].astype(f32))
        e_ref[r, :] = e
        eg = e * cols_ref[r, 1:2]
        plain = plain + jnp.sum(eg, axis=0, keepdims=True)
        cross = cross + jnp.sum(eg * hat_ref[r, :], axis=0, keepdims=True)
    put_stats(part_ref, (plain, cross))


def first_back_kernel(
    idx, e_ref, hat_ref, part_ref, got_ref, st_ref, stg_ref, cols_ref, hid_ref,
    dz_ref, own_ref, send_ref, sums_ref, full,
):
    _, scale = center_scale(st_ref, stg_ref)
    for r in chunks(e_ref.shape[0], 32):
        grad = norm_back(r, e_ref, hat_ref, part_ref, got_ref, scale, cols_ref[r, 1:2], sums_ref)
        dz_ref[r, :] = grad.astype(bf16)
    full[...] = mul(dz_ref[...], hid_ref[...], NN)
    split_rows(idx[0], full, own_ref, send_ref, slice(0, D))


def halves_kernel(idx, z_ref, w_ref, own_ref, send_ref, full):
    y = idx[1]
    full[...] = mul(z_ref[...], w_ref[...], TN)
    for r in chunks(full.shape[0], 64):
        own_ref[r, :] = full[r, at(y, HALF_D, 128)]
        send_ref[r, :] = full[r, at(1 - y, HALF_D, 128)].astype(bf16)


def column_halves(k, flipped, mine_ref, send_ref, full):
    col = mine_ref.shape[0]
    full[...] = flipped
    mine_ref[...] = full[at(k, col), :]
    send_ref[...] = full[at(1 - k, col), :]


def output_kernel(idx, own_ref, got_ref, tok_ref, bias_ref, valid_ref, mine_ref, send_ref, sq_ref, full):
    k, y = idx[0], idx[1]
    half = own_ref.shape[0]
    bias = bias_ref[:, at(y, HALF_D, 128)]
    branch = own_ref[...] + got_ref[...].astype(f32) + bias
    out = tok_ref[...] + branch
    valid = valid_ref[:, at(k, half, 128)].astype(f32)
    sq_ref[0:1, :] = jnp.sum(valid * mul_rows(out), axis=1, keepdims=True) * jnp.ones((1, 128), f32)
    sq_ref[1:2, :] = jnp.sum(valid * mul_rows(branch), axis=1, keepdims=True) * jnp.ones((1, 128), f32)
    sq_ref[2:3, :] = jnp.sum(valid, axis=1, keepdims=True) * jnp.full((1, 128), 0.5, f32)
    sq_ref[3:8, :] = jnp.zeros((5, 128), f32)
    column_halves(k, out.T, mine_ref, send_ref, full)


def mul_rows(v):
    rows = jnp.sum(v * v, axis=1, keepdims=True)
    return jnp.broadcast_to(rows, (v.shape[0], 128)).T[0:1, :]


def token_kernel(idx, own_ref, got_ref, slope_ref, hat_ref, gs_ref, e_ref, part_ref, sums_ref):
    y = idx[1]
    cols = at(y, HALF_D, 128)
    gain = gs_ref[0:1, cols]
    sum_cross = jnp.zeros((1, HALF_D), f32)
    sum_plain = jnp.zeros((1, HALF_D), f32)
    for r in chunks(own_ref.shape[0], 32):
        e = slope_ref[r, cols].astype(f32) * (own_ref[r, :] + got_ref[r, :].astype(f32))
        hat = hat_ref[r, cols].astype(f32)
        eg = e * gain
        e_ref[r, :] = eg
        part_ref[r, 0:1] = jnp.sum(eg, axis=1, keepdims=True)
        part_ref[r, 1:2] = jnp.sum(eg * hat, axis=1, keepdims=True)
        sum_cross = sum_cross + jnp.sum(e * hat, axis=0, keepdims=True)
        sum_plain = sum_plain + jnp.sum(e, axis=0, keepdims=True)
    put_stats(sums_ref, (sum_cross, sum_plain))


def flip_kernel(part_ref, o_ref):
    o_ref[...] = part_ref[...].T[0:8, :]


def token_back_kernel(idx, e_ref, hat_ref, scale_ref, part_ref, got_ref, mine_ref, send_ref, rows, full):
    cols = at(idx[1], HALF_D, 128)
    means = ((part_ref[...] + got_ref[...]) * (1.0 / D)).T
    for r in range(0, e_ref.shape[0], 64):
        s = slice(r, r + 64)
        hat = hat_ref[s, cols].astype(f32)
        rows[s, :] = scale_ref[s, 0:1] * (e_ref[s, :] - means[s, 0:1] - hat * means[s, 1:2])
    column_halves(idx[0], rows[...].T, mine_ref, send_ref, full)


def place_kernel(idx, mine_ref, got_ref, o_ref):
    half = mine_ref.shape[1]
    o_ref[:, at(idx[0], half, 128)] = mine_ref[...]
    o_ref[:, at(1 - idx[0], half, 128)] = got_ref[...]


def place_add_kernel(idx, mine_ref, got_ref, base_ref, o_ref):
    half = mine_ref.shape[1]
    mine, other = at(idx[0], half, 128), at(1 - idx[0], half, 128)
    o_ref[:, mine] = base_ref[:, mine] + mine_ref[...]
    o_ref[:, other] = base_ref[:, other] + got_ref[...]


TAIL = INNER // 2


def early_columns(b):
    taps = D
    return (
        (taps + b * INNER, INNER),
        (b * INNER, INNER),
        (taps + (2 + b) * INNER, INNER),
        (taps + 4 * INNER + b * TAIL, TAIL),
    )


def pair_kernel(idx, own_ref, got_ref, keep_ref, send_ref):
    for b in range(2):

        @pl.when(idx[2] == b)
        def _():
            to = 0
            for (mine, count), (other, _n) in zip(early_columns(b), early_columns(1 - b)):
                for r in chunks(own_ref.shape[0], 32):
                    keep_ref[r, to : to + count] = own_ref[r, mine : mine + count] + got_ref[
                        r, mine : mine + count
                    ].astype(f32)
                    send_ref[r, to : to + count] = (
                        own_ref[r, other : other + count] + got_ref[r, other : other + count].astype(f32)
                    ).astype(bf16)
                to += count


def across_x_kernel(idx, keep_ref, got_ref, sum_ref, send_ref):
    for r in chunks(keep_ref.shape[0], 32):
        sum_ref[r, :] = keep_ref[r, :] + got_ref[r, :].astype(f32)

    @pl.when(idx[3] % 2 == 0)
    def _():
        send_ref[:, : INNER + TAIL] = sum_ref[:, 2 * INNER :].astype(bf16)
        send_ref[:, INNER + TAIL :] = jnp.zeros_like(send_ref[:, INNER + TAIL :])

    @pl.when(idx[3] % 2 == 1)
    def _():
        send_ref[...] = sum_ref[:, : 2 * INNER].astype(bf16)


def along_z_kernel(idx, sum_ref, got_ref, keep_ref, send_ref):
    h = idx[3]

    @pl.when(h % 2 == 0)
    def _():
        for q in range(2):

            @pl.when(h // 2 % 2 == q)
            def _():
                mine = slice(q * INNER, (q + 1) * INNER)
                other = slice((1 - q) * INNER, (2 - q) * INNER)
                keep_ref[:, :INNER] = sum_ref[:, mine] + got_ref[:, mine].astype(f32)
                send_ref[:, :INNER] = (sum_ref[:, other] + got_ref[:, other].astype(f32)).astype(bf16)

        keep_ref[:, INNER:] = jnp.zeros_like(keep_ref[:, INNER:])
        send_ref[:, INNER:] = jnp.zeros_like(send_ref[:, INNER:])

    @pl.when(h % 2 == 1)
    def _():
        v = sum_ref[:, 2 * INNER :] + got_ref[:, : INNER + TAIL].astype(f32)
        keep_ref[...] = v
        send_ref[...] = v.astype(bf16)


def own_kernel(idx, first_ref, taps_ref, last_ref, unit_ref):
    h, b = idx[3], idx[2]
    unit_ref[:, INNER:] = jnp.zeros_like(unit_ref[:, INNER:])
    for i in range(2):

        @pl.when((h == 0) & (b == i))
        def _():
            unit_ref[:, :INNER] = taps_ref[i]

        @pl.when((h == 1) & (b == i))
        def _():
            unit_ref[:, :INNER] = first_ref[:, i * INNER : (i + 1) * INNER]

        @pl.when((h == 2) & (b == i))
        def _():
            unit_ref[:, :INNER] = last_ref[:, i * INNER : (i + 1) * INNER]

        @pl.when((h == 3) & (b == i))
        def _():
            unit_ref[:, :INNER] = taps_ref[2 + i]
            unit_ref[:, INNER:] = taps_ref[4, :, i * TAIL : (i + 1) * TAIL]

    @pl.when(h > 3)
    def _():
        unit_ref[...] = jnp.zeros_like(unit_ref)


def finish_kernel(idx, keep_ref, got_ref, head_ref, head_got_ref, old_ref, sum_ref, new_ref, cross_ref):
    h = idx[3]

    @pl.when(h == 1)
    def _():
        v = head_ref[...] + head_got_ref[...].astype(f32)
        sum_ref[:, :INNER] = v.astype(bf16)
        sum_ref[:, INNER:] = jnp.zeros_like(sum_ref[:, INNER:])
        new_ref[:, :INNER] = (muon_keep * old_ref[:, :INNER] + v).astype(bf16)
        new_ref[:, INNER:] = jnp.zeros_like(new_ref[:, INNER:])

    @pl.when(h != 1)
    def _():
        v = keep_ref[...] + got_ref[...].astype(f32)
        sum_ref[...] = v.astype(bf16)
        new_ref[...] = (muon_keep * old_ref[...] + v).astype(bf16)

    @pl.when(h == 3)
    def _():
        cross_ref[:, :TAIL] = new_ref[:, INNER:]
        cross_ref[:, TAIL:] = new_ref[:, INNER:]

    @pl.when(h != 3)
    def _():
        cross_ref[...] = new_ref[:, :INNER]


def block_kernel(idx, new_ref, got_ref, o_ref):
    h, b = idx[3], idx[2]
    long = (h == 1) | (h == 2)
    for i in range(2):

        @pl.when(long & (b == i))
        def _():
            o_ref[:, i * INNER : (i + 1) * INNER] = new_ref[:, :INNER]
            o_ref[:, (1 - i) * INNER : (2 - i) * INNER] = got_ref[...]

        @pl.when(jnp.logical_not(long) & (b == i))
        def _():
            o_ref[:, :INNER] = new_ref[:, :INNER]
            o_ref[:, INNER + i * TAIL : INNER + (i + 1) * TAIL] = new_ref[:, INNER:]
            o_ref[:, INNER + (1 - i) * TAIL : INNER + (2 - i) * TAIL] = got_ref[:, :TAIL]


def ortho_kernel(
    coarse, fine, idx, own_ref, sib_ref, opp_ref, diag_ref, mine_ref, theirs_ref,
    X, Xh, Xl, A, Ah, Al, Ph,
):
    R, C = X.shape
    k, y, h = idx[0], idx[1], idx[3]
    loc = own_ref.shape[0]
    MT = R // 2
    long = (h == 1) | (h == 2)
    fifth = (h == 3) & (k == 1)
    for place, ref in (
        (2 * y + k, own_ref),
        (2 * y + 1 - k, sib_ref),
        (2 * (1 - y) + k, opp_ref),
        (2 * (1 - y) + 1 - k, diag_ref),
    ):

        @pl.when(long)
        def _():
            X[at(place, loc), :] = ref[...].astype(f32)

        @pl.when(jnp.logical_not(long))
        def _():
            X[at(place, loc), INNER:] = jnp.zeros((loc, C - INNER), f32)

        @pl.when(jnp.logical_not(long) & jnp.logical_not(fifth))
        def _():
            X[at(place, loc), :INNER] = ref[:, :INNER].astype(f32)

        @pl.when(fifth)
        def _():
            X[at(place, loc), :INNER] = ref[:, INNER:].astype(f32)

    def square(i, acc):
        v = X[pl.ds(i * 16, 16), :]
        v = v * v
        return acc + v[:8] + v[8:]

    total = jnp.sum(lax.fori_loop(0, R // 16, square, jnp.zeros((8, C), f32)))
    inverse = 1.0 / (jnp.sqrt(total) + 1e-07)

    def scaled(i, _):
        r = pl.ds(i * 64, 64)
        X[r, :] = X[r, :] * inverse
        return 0

    lax.fori_loop(0, R // 64, scaled, 0)

    def split(low):
        def step(i, _):
            r = pl.ds(i * 32, 32)
            v = X[r, :]
            Xh[r, :] = v.astype(bf16)
            if low:
                Xl[r, :] = (v - Xh[r, :].astype(f32)).astype(bf16)
            return 0

        lax.fori_loop(0, R // 32, step, 0)

    def sweep_coarse(_, __):
        split(False)

        def gram(i, _):
            r = pl.ds(i * MT, MT)
            a = mul(Xh[r, :], Xh[...], NT)
            A[r, :] = a
            Ah[r, :] = a.astype(bf16)
            return 0

        lax.fori_loop(0, R // MT, gram, 0)

        def poly(i, _):
            r = pl.ds(i * MT, MT)
            Ph[r, :] = (coef_second * A[r, :] + coef_third * mul(Ah[r, :], Ah[...], NN)).astype(bf16)
            return 0

        lax.fori_loop(0, R // MT, poly, 0)

        def update(i, _):
            r = pl.ds(i * MT, MT)
            X[r, :] = coef_first * X[r, :] + mul(Ph[r, :], Xh[...], NN)
            return 0

        lax.fori_loop(0, R // MT, update, 0)
        return 0

    def sweep_fine(_, __):
        split(True)

        def gram(i, _):
            r = pl.ds(i * MT, MT)
            a = mul(Xh[r, :], Xh[...], NT) + (mul(Xh[r, :], Xl[...], NT) + mul(Xl[r, :], Xh[...], NT))
            A[r, :] = a
            Ah[r, :] = a.astype(bf16)
            Al[r, :] = (a - Ah[r, :].astype(f32)).astype(bf16)
            return 0

        lax.fori_loop(0, R // MT, gram, 0)

        def poly(i, _):
            r = pl.ds(i * MT, MT)
            p = coef_second * A[r, :] + coef_third * (
                mul(Ah[r, :], Ah[...], NN) + (mul(Ah[r, :], Al[...], NN) + mul(Al[r, :], Ah[...], NN))
            )
            Ph[r, :] = p.astype(bf16)
            A[r, :] = p - Ph[r, :].astype(f32)
            return 0

        lax.fori_loop(0, R // MT, poly, 0)

        def update(i, _):
            r = pl.ds(i * MT, MT)
            low = A[r, :].astype(bf16)
            X[r, :] = (
                coef_first * X[r, :]
                + mul(Ph[r, :], Xh[...], NN)
                + (mul(Ph[r, :], Xl[...], NN) + mul(low, Xh[...], NN))
            )
            return 0

        lax.fori_loop(0, R // MT, update, 0)
        return 0

    lax.fori_loop(0, coarse, sweep_coarse, 0)
    lax.fori_loop(0, fine, sweep_fine, 0)
    mine_ref[...] = X[at(2 * y + k, loc), :].astype(bf16)
    theirs_ref[...] = X[at(2 * y + 1 - k, loc), :INNER].astype(bf16)


def step_kernel(idx, mine_ref, got_ref, o_ref):
    h, b, k = idx[3], idx[2], idx[0]

    @pl.when((h == 0) | ((h == 3) & (k == 0)))
    def _():
        o_ref[:, :INNER] = mine_ref[:, :INNER]

    @pl.when((h == 3) & (k == 1))
    def _():
        o_ref[:, :INNER] = got_ref[...]

    for i in range(2):

        @pl.when(((h == 1) | (h == 2)) & (b == i))
        def _():
            o_ref[:, :INNER] = mine_ref[:, i * INNER : (i + 1) * INNER]

        @pl.when((h == 3) & (k == 0) & (b == i))
        def _():
            o_ref[:, INNER:] = got_ref[:, i * TAIL : (i + 1) * TAIL]

        @pl.when((h == 3) & (k == 1) & (b == i))
        def _():
            o_ref[:, INNER:] = mine_ref[:, i * TAIL : (i + 1) * TAIL]

    @pl.when(h != 3)
    def _():
        o_ref[:, INNER:] = jnp.zeros_like(o_ref[:, INNER:])

    @pl.when(h > 3)
    def _():
        o_ref[:, :INNER] = jnp.zeros_like(o_ref[:, :INNER])


def join_kernel(idx, own_ref, got_ref, o_ref):
    h = idx[3]
    for q in range(2):

        @pl.when(h // 2 % 2 == q)
        def _():
            o_ref[:, q * INNER : (q + 1) * INNER] = own_ref[:, :INNER]
            o_ref[:, (1 - q) * INNER : (2 - q) * INNER] = got_ref[:, :INNER]
            o_ref[:, 2 * INNER :] = (own_ref if q else got_ref)[:, INNER:]


def apply_kernel(
    keep, rate_long, rate_tap, idx, own_ref, x_ref, z_ref, zx_ref, first_ref, taps_ref, last_ref,
    of_ref, ot_ref, ol_ref,
):
    h, b = idx[3], idx[2]
    for odd in range(2):
        for i in range(2):

            @pl.when((h % 2 == odd) & (b == i))
            def _():
                even = (own_ref, x_ref) if odd == 0 else (z_ref, zx_ref)
                odds = (z_ref, zx_ref) if odd == 0 else (own_ref, x_ref)
                for r in chunks(first_ref.shape[0], 32):
                    for q in range(2):
                        e = even[q ^ i]
                        o = odds[q ^ i]
                        lanes = slice(q * INNER, (q + 1) * INNER)
                        tail = slice(q * TAIL, (q + 1) * TAIL)
                        of_ref[r, lanes] = keep * first_ref[r, lanes] + rate_long * o[r, :INNER].astype(f32)
                        ol_ref[r, lanes] = keep * last_ref[r, lanes] + rate_long * e[r, INNER : 2 * INNER].astype(f32)
                        ot_ref[q, r, :] = keep * taps_ref[q, r, :] + rate_tap * e[r, :INNER].astype(f32)
                        ot_ref[2 + q, r, :] = keep * taps_ref[2 + q, r, :] + rate_tap * o[
                            r, INNER : 2 * INNER
                        ].astype(f32)
                        ot_ref[4, r, tail] = keep * taps_ref[4, r, tail] + rate_tap * o[r, 2 * INNER :].astype(f32)


def body(
    tokens,
    cotangent,
    lengths,
    valid_mask,
    weight_first,
    weight_dilated,
    weight_last,
    momentum_first,
    momentum_dilated,
    momentum_last,
    vector_params,
    vector_moment,
    vector_square,
):
    C = lax.axis_size("ch")
    S = lax.axis_size("seq")
    c = lax.axis_index("ch")
    s = lax.axis_index("seq")
    k = c % 2
    y = c // 2
    T = tokens.shape[0]
    half = T // 2
    loc = weight_first.shape[1]
    wide = 2 * loc
    col = D // C
    H = S // 2
    b = s % 2
    h = s // 2
    idx = jnp.stack([k, y, b, h, s, s * T + k * half]).astype(jnp.int32)

    sib = [(i, i ^ 1) for i in range(C)]
    opp = [(i, i ^ 2) for i in range(C)]
    diag = [(i, i ^ 3) for i in range(C)]
    xsw = [(i, i ^ 1) for i in range(S)]

    def swap_core(v):
        return lax.ppermute(v, "ch", sib)

    def swap_y(v):
        return lax.ppermute(v, "ch", opp)

    def swap_x(v):
        return lax.ppermute(v, "seq", xsw)

    def along_h(v, pairs):
        return lax.ppermute(v, "seq", [(2 * i + q, 2 * j + q) for i, j in pairs for q in range(2)])

    outer_pairs = []
    for i in range(S):
        for j in range(C):
            if j % 2 == 0 and i >= 1:
                outer_pairs.append((i * C + j, (i - 1) * C + (j ^ 1)))
            if j % 2 == 1 and i + 1 < S:
                outer_pairs.append((i * C + j, (i + 1) * C + (j ^ 1)))

    def swap_outer(v):
        return lax.ppermute(v, ("seq", "ch"), outer_pairs)

    w_first, w_taps, w_last = weight_first.T, jnp.swapaxes(weight_dilated, 1, 2), weight_last
    m_first, m_taps, m_last = momentum_first.T, jnp.swapaxes(momentum_dilated, 1, 2), momentum_last
    cot = cotangent.T
    valid = valid_mask.reshape(1, T)
    gain_shift = vector_params[: 2 * D].reshape(2, D)
    inner_rows = vector_params[2 * D : 2 * D + 6 * INNER].reshape(6, INNER)
    cols = lax.dynamic_slice_in_dim(inner_rows, y * wide, wide, 1).T
    bias_three = vector_params[2 * D + 6 * INNER :].reshape(1, D)

    low_first, cot_mine, cot_other, cot_sums = call(
        prep_kernel,
        [((loc, D), bf16), ((col, half), bf16), ((col, half), bf16), ((col, 128), f32)],
        [idx],
        [w_first, cot],
    )
    got_first = swap_core(low_first)
    cot_opp = swap_y(cot_mine)
    cot_sib = swap_core(cot_other)
    cot_diag = lax.ppermute(cot_other, "ch", diag)

    rows = 128
    steps = half // rows
    hid_one, hat_one, slope_one, scale_one = pl.pallas_call(
        input_kernel,
        out_shape=[
            jax.ShapeDtypeStruct((half, D), bf16),
            jax.ShapeDtypeStruct((half, D), bf16),
            jax.ShapeDtypeStruct((half, D), bf16),
            jax.ShapeDtypeStruct((half, 128), f32),
        ],
        grid_spec=pltpu.PrefetchScalarGridSpec(
            num_scalar_prefetch=1,
            grid=(steps,),
            in_specs=[
                pl.BlockSpec((rows, D), lambda i, idx: (idx[0] * steps + i, 0)),
                pl.BlockSpec((2, D), lambda i, idx: (0, 0)),
            ],
            out_specs=[
                pl.BlockSpec((rows, D), lambda i, idx: (i, 0)),
                pl.BlockSpec((rows, D), lambda i, idx: (i, 0)),
                pl.BlockSpec((rows, D), lambda i, idx: (i, 0)),
                pl.BlockSpec((rows, 128), lambda i, idx: (i, 0)),
            ],
        ),
        compiler_params=pltpu.CompilerParams(vmem_limit_bytes=24 * MIB),
        cost_estimate=pl.CostEstimate(flops=5 * 10**9, bytes_accessed=8 * 10**6, transcendentals=10**6),
    )(idx, tokens, gain_shift)

    (low_rest,) = call(rest_kernel, [((loc, D + KERNEL_TAPS * INNER), bf16)], [], [w_last, w_taps])
    got_rest = swap_core(low_rest)

    full_first, inner_one, st_two = call(
        first_kernel,
        [((wide, D), bf16), ((wide, half), f32), ((8, half), f32)],
        [idx],
        [low_first, got_first, hid_one, cols],
    )
    st_two_got = swap_y(st_two)
    hid_two, hat_two, slope_two = call(
        second_kernel,
        [((wide, half), bf16), ((wide, half), f32), ((wide, half), f32)],
        [idx],
        [inner_one, st_two, st_two_got, cols, valid],
    )
    hid_two_got = swap_y(hid_two)
    slab_in, slab_out = call(
        slab_kernel, [((INNER, REACH), bf16)] * 2, [idx], [hid_two, hid_two_got]
    )
    got_in, got_out = swap_core(slab_in), swap_outer(slab_out)
    ext, inner_two, st_three, full_last, full_taps, masks = call(
        functools.partial(conv_kernel, S * T),
        [
            ((INNER, half + 2 * REACH), bf16),
            ((wide, half), f32),
            ((8, half), f32),
            ((wide, D), bf16),
            ((wide, KERNEL_TAPS * INNER), bf16),
            ((8, half), f32),
        ],
        [idx, lengths],
        [hid_two, hid_two_got, got_in, got_out, low_rest, got_rest, cols],
        scratch=[((KERNEL_TAPS * INNER, half), bf16)],
        flops=10**9,
    )
    st_three_got = swap_y(st_three)
    gw, g_three = call(
        cotangent_kernel,
        [((D, half), bf16), ((wide, half), f32)],
        [idx],
        [full_last, cot_mine, cot_sib, cot_opp, cot_diag],
        flops=4 * 10**8,
    )
    hid_three, e_three, hat_three, part_three = call(
        third_kernel,
        [((wide, half), bf16), ((wide, half), f32), ((wide, half), f32), ((8, half), f32)],
        [],
        [inner_two, st_three, st_three_got, cols, g_three],
    )
    part_three_got = swap_y(part_three)
    dz_two, slab_in, slab_out, sums_three = call(
        third_back_kernel,
        [((wide, half), bf16), ((wide, REACH), bf16), ((wide, REACH), bf16), ((wide, 8), f32)],
        [idx],
        [e_three, hat_three, part_three, part_three_got, cols],
    )
    got_in, got_out = swap_core(slab_in), swap_outer(slab_out)
    early_size = D + KERNEL_TAPS * INNER
    early_own, early_send = call(
        grads_kernel,
        [((loc, early_size), f32), ((loc, early_size), bf16)],
        [idx],
        [dz_two, ext, masks, hid_three, gw],
        scratch=[((wide, early_size), f32)],
        flops=16 * 10**8,
        limit=32,
    )
    early_got = swap_core(early_send)
    back_own, back_send = call(
        conv_back_kernel,
        [((wide, half), f32), ((wide, half), bf16)],
        [idx],
        [dz_two, got_in, got_out, masks, full_taps],
        scratch=[((wide, half + 2 * REACH), bf16), ((INNER, half), f32)],
        flops=10**9,
    )
    back_got = swap_y(back_send)
    early = 3 * INNER + TAIL
    keep, send = call(
        pair_kernel, [((loc, early), f32), ((loc, early), bf16)], [idx], [early_own, early_got]
    )
    x_got = swap_x(send)
    e_two, part_two = call(
        second_back_kernel,
        [((wide, half), f32), ((8, half), f32)],
        [],
        [back_own, back_got, slope_two, hat_two, cols],
    )
    part_two_got = swap_y(part_two)
    dz_one, first_own, first_send, sums_two = call(
        first_back_kernel,
        [((wide, half), bf16), ((loc, D), f32), ((loc, D), bf16), ((wide, 8), f32)],
        [idx],
        [e_two, hat_two, part_two, part_two_got, st_two, st_two_got, cols, hid_one],
        scratch=[((wide, D), f32)],
        flops=4 * 10**8,
    )
    first_got = swap_core(first_send)

    first_pair = first_own + first_got.astype(f32)
    head = lax.dynamic_slice_in_dim(first_pair, b * INNER, INNER, 1)
    head_send = lax.dynamic_slice_in_dim(first_pair, (1 - b) * INNER, INNER, 1).astype(bf16)
    head = head + swap_x(head_send).astype(f32)

    early_sum, send = call(
        across_x_kernel, [((loc, early), f32), ((loc, 2 * INNER), bf16)], [idx], [keep, x_got]
    )
    span = H
    while span > 4:
        span //= 2
        fold = [(i + span, i) for i in range(span)]
        early_sum = early_sum + along_h(early_sum.astype(bf16), fold).astype(f32)
        head = head + along_h(head.astype(bf16), fold).astype(f32)
        even = jnp.concatenate([early_sum[:, 2 * INNER :], jnp.zeros((loc, TAIL), f32)], axis=1)
        send = jnp.where(h % 2 == 0, even, early_sum[:, : 2 * INNER]).astype(bf16)
    z_got = along_h(send, [(i, i ^ 1) for i in range(4)])
    head = head + along_h(head.astype(bf16), [(0, 1), (2, 3)]).astype(f32)
    keep, send = call(
        along_z_kernel,
        [((loc, INNER + TAIL), f32), ((loc, INNER + TAIL), bf16)],
        [idx],
        [early_sum, z_got],
    )
    z_got = along_h(send, [(i, i ^ 2) for i in range(4)])
    head_got = along_h(head.astype(bf16), [(3, 1)])
    (old_unit,) = call(own_kernel, [((loc, INNER + TAIL), f32)], [idx], [m_first, m_taps, m_last])
    sum_unit, new_unit, cross = call(
        finish_kernel,
        [((loc, INNER + TAIL), bf16), ((loc, INNER + TAIL), bf16), ((loc, INNER), bf16)],
        [idx],
        [keep, z_got, head, head_got, old_unit],
    )
    cross_got = swap_x(cross)
    (block,) = call(block_kernel, [((loc, D), bf16)], [idx], [new_unit, cross_got])
    block_sib, block_opp = swap_core(block), swap_y(block)
    block_diag = swap_core(block_opp)

    def gather(unit):
        got = along_h(unit, [(i, i ^ 2) for i in range(4)])
        (joined,) = call(join_kernel, [((loc, 2 * INNER + TAIL), bf16)], [idx], [unit, got])
        joined_x = swap_x(joined)
        other = along_h(joined, [(i, i ^ 1) for i in range(4)])
        other_x = swap_x(other)
        result = [joined, joined_x, other, other_x]
        span = 4
        while span < H:
            spread = [(i, i + span) for i in range(span)]
            result = [jnp.where((h >= span) & (h < 2 * span), along_h(v, spread), v) for v in result]
            span *= 2
        return result

    def apply(keep, rate_long, rate_tap, parts, first, taps, last):
        return call(
            functools.partial(apply_kernel, keep, rate_long, rate_tap),
            [((loc, D), f32), ((KERNEL_TAPS, loc, INNER), f32), ((loc, D), f32)],
            [idx],
            [*parts, first, taps, last],
            limit=32,
        )

    new_first, new_taps, new_last = apply(muon_keep, 1.0, 1.0, gather(sum_unit), m_first, m_taps, m_last)

    mine, theirs = call(
        functools.partial(ortho_kernel, 3, 2),
        [((loc, D), bf16), ((loc, INNER), bf16)],
        [idx],
        [block, block_sib, block_opp, block_diag],
        scratch=[
            ((INNER, D), f32),
            ((INNER, D), bf16),
            ((INNER, D), bf16),
            ((INNER, INNER), f32),
            ((INNER, INNER), bf16),
            ((INNER, INNER), bf16),
            ((INNER, INNER), bf16),
        ],
        limit=32,
        flops=30 * 10**9,
    )
    theirs_got = swap_core(theirs)
    (step_unit,) = call(step_kernel, [((loc, INNER + TAIL), bf16)], [idx], [mine, theirs_got])
    keep_weight = 1.0 - muon_rate * decay_rate
    rate = muon_rate * muon_scale
    out_first, out_taps, out_last = apply(
        keep_weight,
        -rate * math.sqrt(D),
        -rate * math.sqrt(INNER),
        gather(step_unit),
        w_first,
        w_taps,
        w_last,
    )

    half_out = [((half, HALF_D), f32), ((half, HALF_D), bf16)]
    branch_own, branch_send = call(
        halves_kernel, half_out, [idx], [hid_three, full_last], scratch=[((half, D), f32)], flops=4 * 10**8
    )
    branch_got = swap_y(branch_send)
    own_tokens = lax.dynamic_slice(tokens, (k * half, y * HALF_D), (half, HALF_D))
    out_mine, out_send, squares = call(
        output_kernel,
        [((col, half), f32), ((col, half), f32), ((8, 128), f32)],
        [idx],
        [branch_own, branch_got, own_tokens, bias_three, valid],
        scratch=[((HALF_D, half), f32)],
    )
    (block_output,) = call(place_kernel, [((col, T), f32)], [idx], [out_mine, swap_core(out_send)])

    back_own, back_send = call(
        halves_kernel, half_out, [idx], [dz_one, full_first], scratch=[((half, D), f32)], flops=4 * 10**8
    )
    back_got = swap_y(back_send)
    e_one, part_one, sums_one = call(
        token_kernel,
        [((half, HALF_D), f32), ((half, 128), f32), ((8, HALF_D), f32)],
        [idx],
        [back_own, back_got, slope_one, hat_one, gain_shift],
    )
    (part_one,) = call(flip_kernel, [((8, half), f32)], [], [part_one])
    grad_mine, grad_send = call(
        token_back_kernel,
        [((col, half), f32), ((col, half), f32)],
        [idx],
        [e_one, hat_one, scale_one, part_one, swap_y(part_one)],
        scratch=[((half, HALF_D), f32), ((HALF_D, half), f32)],
    )
    (tokens_grad,) = call(
        place_add_kernel, [((col, T), f32)], [idx], [grad_mine, swap_core(grad_send), cot]
    )

    grid = jnp.zeros((6, INNER), f32)
    inner = jnp.concatenate([sums_two[:, 2:3], sums_two[:, 0:2], sums_three[:, 2:3], sums_three[:, 0:2]], axis=1)
    grid = lax.dynamic_update_slice(grid, inner.T, (0, y * wide))
    ones = jnp.zeros((2, D), f32)
    ones = lax.dynamic_update_slice(ones, sums_one[0:2], (0, y * HALF_D))
    bias = lax.dynamic_update_slice(jnp.zeros((D,), f32), cot_sums[:, 0], (c * col,))
    grad_vector = jnp.concatenate([ones.reshape(-1), grid.reshape(-1), bias, squares[:, 0], jnp.zeros((120,), f32)])
    grad_vector = grad_vector.reshape(-1, 128)
    grad_vector = grad_vector + swap_core(grad_vector)
    grad_vector = grad_vector + swap_y(grad_vector)
    bit = 1
    while bit < S:
        grad_vector = grad_vector + lax.ppermute(grad_vector, "seq", [(i, i ^ bit) for i in range(S)])
        bit *= 2
    grad_vector = grad_vector.reshape(-1)
    total_stats = grad_vector[VECTOR : VECTOR + 3]
    grad_vector = grad_vector[:VECTOR]
    vector_first = adam_first * vector_moment + (1.0 - adam_first) * grad_vector
    vector_second = adam_second * vector_square + (1.0 - adam_second) * grad_vector * grad_vector
    corrected_first = vector_first / (1.0 - adam_first**STEP)
    corrected_second = vector_second / (1.0 - adam_second**STEP)
    vector_values = vector_params - adam_rate * (
        corrected_first / (jnp.sqrt(corrected_second) + adam_eps) + decay_rate * vector_params
    )
    root_means = jnp.sqrt(total_stats[:2] / (total_stats[2] * D))
    return (
        block_output.T,
        tokens_grad.T,
        out_first.T,
        jnp.swapaxes(out_taps, 1, 2),
        out_last,
        new_first.T,
        jnp.swapaxes(new_taps, 1, 2),
        new_last,
        vector_first,
        vector_second,
        vector_values,
        root_means,
    )


def solution(mesh):
    placed = (
        P("seq", None),
        P("seq", "ch"),
        P(),
        P("seq"),
        P(None, "ch"),
        P(None, None, "ch"),
        P("ch", None),
        P(None, "ch"),
        P(None, None, "ch"),
        P("ch", None),
        P(),
        P(),
        P(),
    )
    return jax.shard_map(
        body,
        mesh=mesh,
        in_specs=placed,
        out_specs=(
            P("seq", "ch"),
            P("seq", "ch"),
            P(None, "ch"),
            P(None, None, "ch"),
            P("ch", None),
            P(None, "ch"),
            P(None, None, "ch"),
            P("ch", None),
            P(),
            P(),
            P(),
            P(),
        ),
        check_vma=False,
    )
```

```python
import functools
import math

import jax
import jax.numpy as jnp
from jax import lax
from jax.experimental import pallas as pl
from jax.experimental.pallas import tpu as pltpu
from jax.sharding import PartitionSpec as P

D = 1280
INNER = 640
KERNEL_TAPS = 5
DILATION_SPAN = 128
STEP = 10

norm_eps = 1e-05
coef_first = 3.4445
coef_second = -4.775
coef_third = 2.0315
adam_rate = 0.4
adam_first = 0.9
adam_second = 0.999
adam_eps = 1e-08
decay_rate = 0.01
muon_rate = 0.1
muon_keep = 0.95
muon_scale = 0.2
REACH = KERNEL_TAPS // 2 * DILATION_SPAN
VECTOR = 3 * D + 6 * INNER
HALF_D = D // 2
MIB = 1024 * 1024

f32 = jnp.float32
bf16 = jnp.bfloat16
NN = (((1,), (0,)), ((), ()))
NT = (((1,), (1,)), ((), ()))
TN = (((0,), (0,)), ((), ()))


def mul(a, b, dims):
    return lax.dot_general(a, b, dims, preferred_element_type=f32)


def erf_parts(v):
    a = jnp.abs(v) * math.sqrt(0.5)
    t = pl.reciprocal(1.0 + 0.3275911 * a)
    e = jnp.exp(-a * a)
    p = t * (0.254829592 + t * (-0.284496736 + t * (1.421413741 + t * (-1.453152027 + t * 1.061405429))))
    tail = 0.5 * p * e
    return jnp.where(v >= 0, 1.0 - tail, tail), e


def gelu_pair(v):
    cdf, e = erf_parts(v)
    return v * cdf, cdf + v * e * (1.0 / math.sqrt(2.0 * math.pi))


VMEM = pl.BlockSpec(memory_space=pltpu.VMEM)
SMEM = pl.BlockSpec(memory_space=pltpu.SMEM)


def call(kernel, outs, scalars, arrays, scratch=(), limit=24, flops=10**8):
    shapes = [jax.ShapeDtypeStruct(shape, dtype) for shape, dtype in outs]
    size = sum(math.prod(shape) * jnp.dtype(dtype).itemsize for shape, dtype in outs)
    size += sum(a.size * a.dtype.itemsize for a in arrays)
    return pl.pallas_call(
        kernel,
        out_shape=shapes,
        in_specs=[SMEM] * len(scalars) + [VMEM] * len(arrays),
        out_specs=[VMEM] * len(outs),
        scratch_shapes=[pltpu.VMEM(shape, dtype) for shape, dtype in scratch],
        compiler_params=pltpu.CompilerParams(vmem_limit_bytes=limit * MIB),
        cost_estimate=pl.CostEstimate(flops=flops, bytes_accessed=size, transcendentals=0),
    )(*scalars, *arrays)


def chunks(count, step):
    return [pl.ds(i, step) for i in range(0, count, step)]


def at(index, count, step=32):
    return pl.ds(pl.multiple_of(index * count, step), count)


def prep_kernel(idx, w_ref, cot_ref, wo_ref, mine_ref, other_ref, sums_ref):
    k = idx[0]
    half = mine_ref.shape[1]
    for r in chunks(w_ref.shape[0], 32):
        wo_ref[r, :] = w_ref[r, :].astype(bf16)
    for r in chunks(cot_ref.shape[0], 32):
        v = cot_ref[r, :]
        sums_ref[r, :] = jnp.broadcast_to(jnp.sum(v, axis=1, keepdims=True), (32, 128))
        mine_ref[r, :] = cot_ref[r, at(k, half, 128)].astype(bf16)
        other_ref[r, :] = cot_ref[r, at(1 - k, half, 128)].astype(bf16)


def rest_kernel(last_ref, taps_ref, o_ref):
    for r in chunks(last_ref.shape[0], 32):
        o_ref[r, :D] = last_ref[r, :].astype(bf16)
        for j in range(KERNEL_TAPS):
            o_ref[r, D + j * INNER : D + (j + 1) * INNER] = taps_ref[j, r, :].astype(bf16)


def input_kernel(idx, tok_ref, gs_ref, hid_ref, hat_ref, slope_ref, scale_ref):
    for r in chunks(tok_ref.shape[0], 16):
        v = tok_ref[r, :]
        center = jnp.sum(v, axis=1, keepdims=True) * (1.0 / D)
        square = jnp.sum(v * v, axis=1, keepdims=True) * (1.0 / D)
        scale = lax.rsqrt(square - center * center + norm_eps)
        hat = (v - center) * scale
        hid, slope = gelu_pair(hat * gs_ref[0:1, :] + gs_ref[1:2, :])
        hid_ref[r, :] = hid.astype(bf16)
        hat_ref[r, :] = hat.astype(bf16)
        slope_ref[r, :] = slope.astype(bf16)
        scale_ref[r, :] = jnp.broadcast_to(scale, (16, 128))


def put_stats(ref, parts):
    for i, part in enumerate(parts):
        ref[i : i + 1, :] = part


def first_kernel(idx, own_ref, got_ref, hid_ref, cols_ref, w_ref, inner_ref, st_ref):
    k = idx[0]
    loc = own_ref.shape[0]
    w_ref[at(k, loc), :] = own_ref[...]
    w_ref[at(1 - k, loc), :] = got_ref[...]
    v = mul(w_ref[...], hid_ref[...], NT) + cols_ref[:, 0:1]
    inner_ref[...] = v
    put_stats(st_ref, (jnp.sum(v, axis=0, keepdims=True), jnp.sum(v * v, axis=0, keepdims=True)))


def center_scale(st_ref, got_ref):
    center = (st_ref[0:1, :] + got_ref[0:1, :]) * (1.0 / INNER)
    square = (st_ref[1:2, :] + got_ref[1:2, :]) * (1.0 / INNER)
    return center, lax.rsqrt(square - center * center + norm_eps)


def second_kernel(idx, inner_ref, st_ref, got_ref, cols_ref, valid_ref, hid_ref, hat_ref, slope_ref):
    center, scale = center_scale(st_ref, got_ref)
    valid = valid_ref[:, at(idx[0], hid_ref.shape[1], 128)].astype(f32)
    for r in chunks(inner_ref.shape[0], 32):
        hat = (inner_ref[r, :] - center) * scale
        hid, slope = gelu_pair(hat * cols_ref[r, 1:2] + cols_ref[r, 2:3])
        hid_ref[r, :] = (hid * valid).astype(bf16)
        hat_ref[r, :] = hat
        slope_ref[r, :] = slope * valid


def slabs_of(k, v_ref, row, in_ref, out_ref):
    half = v_ref.shape[1]
    rows = v_ref.shape[0]
    in_ref[row, :] = v_ref[:, at(1 - k, half - REACH, 128)]
    out_ref[row, :] = v_ref[:, at(k, half - REACH, 128)]


def slab_kernel(idx, own_ref, got_ref, in_ref, out_ref):
    k, y = idx[0], idx[1]
    wide = own_ref.shape[0]
    slabs_of(k, own_ref, at(y, wide), in_ref, out_ref)
    slabs_of(k, got_ref, at(1 - y, wide), in_ref, out_ref)


def fill_reach(k, ext_ref, in_ref, out_ref, half):
    @pl.when(k == 0)
    def _():
        ext_ref[:, :REACH] = out_ref[...]
        ext_ref[:, REACH + half :] = in_ref[...]

    @pl.when(k == 1)
    def _():
        ext_ref[:, :REACH] = in_ref[...]
        ext_ref[:, REACH + half :] = out_ref[...]


def conv_kernel(
    total, idx, lengths, own_ref, got_ref, in_ref, out_ref, wo_ref, wg_ref, cols_ref,
    ext_ref, inner_ref, st_ref, last_ref, taps_ref, mask_ref, stack,
):
    k, y = idx[0], idx[1]
    wide, half = own_ref.shape
    loc = wo_ref.shape[0]
    ext_ref[at(y, wide), REACH : REACH + half] = own_ref[...]
    ext_ref[at(1 - y, wide), REACH : REACH + half] = got_ref[...]
    fill_reach(k, ext_ref, in_ref, out_ref, half)
    last_ref[at(k, loc), :] = wo_ref[:, :D]
    last_ref[at(1 - k, loc), :] = wg_ref[:, :D]
    taps_ref[at(k, loc), :] = wo_ref[:, D:]
    taps_ref[at(1 - k, loc), :] = wg_ref[:, D:]
    positions = idx[5] - REACH + lax.broadcasted_iota(jnp.int32, (1, half + 2 * REACH), 1)
    segment = jnp.zeros_like(positions)
    bound = jnp.int32(0)
    for i in range(lengths.shape[0]):
        bound = bound + lengths[i]
        segment = segment + (positions >= bound).astype(jnp.int32)
    segment = jnp.where((positions >= 0) & (positions < total), segment, -1)
    centre = segment[:, REACH : REACH + half]
    for j in range(KERNEL_TAPS):
        lanes = slice(j * DILATION_SPAN, j * DILATION_SPAN + half)
        mask = (segment[:, lanes] == centre).astype(f32)
        mask_ref[j : j + 1, :] = mask
        low = mask.astype(bf16)
        for i in range(0, INNER, 160):
            stack[j * INNER + i : j * INNER + i + 160, :] = ext_ref[i : i + 160, lanes] * low
    v = mul(taps_ref[...], stack[...], NN) + cols_ref[:, 3:4]
    inner_ref[...] = v
    put_stats(st_ref, (jnp.sum(v, axis=0, keepdims=True), jnp.sum(v * v, axis=0, keepdims=True)))


def cotangent_kernel(idx, last_ref, mine_ref, sib_ref, opp_ref, diag_ref, gw_ref, g_ref):
    k, y = idx[0], idx[1]
    col = mine_ref.shape[0]
    gw_ref[at(2 * y + k, col), :] = mine_ref[...]
    gw_ref[at(2 * y + 1 - k, col), :] = sib_ref[...]
    gw_ref[at(2 * (1 - y) + k, col), :] = opp_ref[...]
    gw_ref[at(2 * (1 - y) + 1 - k, col), :] = diag_ref[...]
    g_ref[...] = mul(last_ref[...], gw_ref[...], NN)


def third_kernel(inner_ref, st_ref, got_ref, cols_ref, g_ref, hid_ref, e_ref, hat_ref, part_ref):
    center, scale = center_scale(st_ref, got_ref)
    plain = jnp.zeros_like(center)
    cross = jnp.zeros_like(center)
    for r in chunks(inner_ref.shape[0], 32):
        hat = (inner_ref[r, :] - center) * scale
        gain = cols_ref[r, 4:5]
        hid, slope = gelu_pair(hat * gain + cols_ref[r, 5:6])
        hid_ref[r, :] = hid.astype(bf16)
        hat_ref[r, :] = hat
        e = slope * g_ref[r, :]
        e_ref[r, :] = e
        eg = e * gain
        plain = plain + jnp.sum(eg, axis=0, keepdims=True)
        cross = cross + jnp.sum(eg * hat, axis=0, keepdims=True)
    put_stats(part_ref, (plain, cross, scale))


def norm_back(r, e_ref, hat_ref, part_ref, got_ref, scale, gain, sums_ref):
    plain = (part_ref[0:1, :] + got_ref[0:1, :]) * (1.0 / INNER)
    cross = (part_ref[1:2, :] + got_ref[1:2, :]) * (1.0 / INNER)
    e, hat = e_ref[r, :], hat_ref[r, :]
    grad = scale * (e * gain - plain - hat * cross)
    sums_ref[r, 0:1] = jnp.sum(e * hat, axis=1, keepdims=True)
    sums_ref[r, 1:2] = jnp.sum(e, axis=1, keepdims=True)
    sums_ref[r, 2:3] = jnp.sum(grad, axis=1, keepdims=True)
    return grad


def third_back_kernel(idx, e_ref, hat_ref, part_ref, got_ref, cols_ref, dz_ref, in_ref, out_ref, sums_ref):
    for r in chunks(e_ref.shape[0], 32):
        grad = norm_back(r, e_ref, hat_ref, part_ref, got_ref, part_ref[2:3, :], cols_ref[r, 4:5], sums_ref)
        dz_ref[r, :] = grad.astype(bf16)
    slabs_of(idx[0], dz_ref, slice(None), in_ref, out_ref)


def split_rows(k, full, own_ref, send_ref, lanes):
    loc = own_ref.shape[0]
    own_ref[:, lanes] = full[at(k, loc), lanes]
    send_ref[:, lanes] = full[at(1 - k, loc), lanes].astype(bf16)


def grads_kernel(idx, dz_ref, ext_ref, mask_ref, hid_ref, gw_ref, own_ref, send_ref, full):
    k = idx[0]
    half = dz_ref.shape[1]
    full[:, :D] = mul(hid_ref[...], gw_ref[...], NT)
    split_rows(k, full, own_ref, send_ref, slice(0, D))
    for j in range(KERNEL_TAPS):
        masked = dz_ref[...] * mask_ref[j : j + 1, :].astype(bf16)
        moved = ext_ref[:, j * DILATION_SPAN : j * DILATION_SPAN + half]
        lanes = slice(D + j * INNER, D + (j + 1) * INNER)
        full[:, lanes] = mul(masked, moved, NT)
        split_rows(k, full, own_ref, send_ref, lanes)


def conv_back_kernel(idx, dz_ref, in_ref, out_ref, mask_ref, taps_ref, own_ref, send_ref, ext, full):
    k, y = idx[0], idx[1]
    wide, half = dz_ref.shape
    ext[:, REACH : REACH + half] = dz_ref[...]
    fill_reach(k, ext, in_ref, out_ref, half)
    total = None
    for j in range(KERNEL_TAPS):
        begin = REACH - (j - KERNEL_TAPS // 2) * DILATION_SPAN
        mask = mask_ref[KERNEL_TAPS - 1 - j : KERNEL_TAPS - j, :].astype(bf16)
        part = mul(taps_ref[:, j * INNER : (j + 1) * INNER], ext[:, begin : begin + half] * mask, TN)
        total = part if total is None else total + part
    full[...] = total
    own_ref[...] = full[at(y, wide), :]
    send_ref[...] = full[at(1 - y, wide), :].astype(bf16)


def second_back_kernel(own_ref, got_ref, slope_ref, hat_ref, cols_ref, e_ref, part_ref):
    plain = jnp.zeros((1, own_ref.shape[1]), f32)
    cross = jnp.zeros_like(plain)
    for r in chunks(own_ref.shape[0], 32):
        e = slope_ref[r, :] * (own_ref[r, :] + got_ref[r, :].astype(f32))
        e_ref[r, :] = e
        eg = e * cols_ref[r, 1:2]
        plain = plain + jnp.sum(eg, axis=0, keepdims=True)
        cross = cross + jnp.sum(eg * hat_ref[r, :], axis=0, keepdims=True)
    put_stats(part_ref, (plain, cross))


def first_back_kernel(
    idx, e_ref, hat_ref, part_ref, got_ref, st_ref, stg_ref, cols_ref, hid_ref,
    dz_ref, own_ref, send_ref, sums_ref, full,
):
    _, scale = center_scale(st_ref, stg_ref)
    for r in chunks(e_ref.shape[0], 32):
        grad = norm_back(r, e_ref, hat_ref, part_ref, got_ref, scale, cols_ref[r, 1:2], sums_ref)
        dz_ref[r, :] = grad.astype(bf16)
    full[...] = mul(dz_ref[...], hid_ref[...], NN)
    split_rows(idx[0], full, own_ref, send_ref, slice(0, D))


def halves_kernel(idx, z_ref, w_ref, own_ref, send_ref, full):
    y = idx[1]
    full[...] = mul(z_ref[...], w_ref[...], TN)
    for r in chunks(full.shape[0], 64):
        own_ref[r, :] = full[r, at(y, HALF_D, 128)]
        send_ref[r, :] = full[r, at(1 - y, HALF_D, 128)].astype(bf16)


def column_halves(k, flipped, mine_ref, send_ref, full):
    col = mine_ref.shape[0]
    full[...] = flipped
    mine_ref[...] = full[at(k, col), :]
    send_ref[...] = full[at(1 - k, col), :]


def output_kernel(idx, own_ref, got_ref, tok_ref, bias_ref, valid_ref, mine_ref, send_ref, sq_ref, full):
    k, y = idx[0], idx[1]
    half = own_ref.shape[0]
    bias = bias_ref[:, at(y, HALF_D, 128)]
    branch = own_ref[...] + got_ref[...].astype(f32) + bias
    out = tok_ref[...] + branch
    valid = valid_ref[:, at(k, half, 128)].astype(f32)
    sq_ref[0:1, :] = jnp.sum(valid * mul_rows(out), axis=1, keepdims=True) * jnp.ones((1, 128), f32)
    sq_ref[1:2, :] = jnp.sum(valid * mul_rows(branch), axis=1, keepdims=True) * jnp.ones((1, 128), f32)
    sq_ref[2:3, :] = jnp.sum(valid, axis=1, keepdims=True) * jnp.full((1, 128), 0.5, f32)
    sq_ref[3:8, :] = jnp.zeros((5, 128), f32)
    column_halves(k, out.T, mine_ref, send_ref, full)


def mul_rows(v):
    rows = jnp.sum(v * v, axis=1, keepdims=True)
    return jnp.broadcast_to(rows, (v.shape[0], 128)).T[0:1, :]


def token_kernel(idx, own_ref, got_ref, slope_ref, hat_ref, gs_ref, e_ref, part_ref, sums_ref):
    y = idx[1]
    cols = at(y, HALF_D, 128)
    gain = gs_ref[0:1, cols]
    sum_cross = jnp.zeros((1, HALF_D), f32)
    sum_plain = jnp.zeros((1, HALF_D), f32)
    for r in chunks(own_ref.shape[0], 32):
        e = slope_ref[r, cols].astype(f32) * (own_ref[r, :] + got_ref[r, :].astype(f32))
        hat = hat_ref[r, cols].astype(f32)
        eg = e * gain
        e_ref[r, :] = eg
        part_ref[r, 0:1] = jnp.sum(eg, axis=1, keepdims=True)
        part_ref[r, 1:2] = jnp.sum(eg * hat, axis=1, keepdims=True)
        sum_cross = sum_cross + jnp.sum(e * hat, axis=0, keepdims=True)
        sum_plain = sum_plain + jnp.sum(e, axis=0, keepdims=True)
    put_stats(sums_ref, (sum_cross, sum_plain))


def flip_kernel(part_ref, o_ref):
    o_ref[...] = part_ref[...].T[0:8, :]


def token_back_kernel(idx, e_ref, hat_ref, scale_ref, part_ref, got_ref, mine_ref, send_ref, rows, full):
    cols = at(idx[1], HALF_D, 128)
    means = ((part_ref[...] + got_ref[...]) * (1.0 / D)).T
    for r in range(0, e_ref.shape[0], 64):
        s = slice(r, r + 64)
        hat = hat_ref[s, cols].astype(f32)
        rows[s, :] = scale_ref[s, 0:1] * (e_ref[s, :] - means[s, 0:1] - hat * means[s, 1:2])
    column_halves(idx[0], rows[...].T, mine_ref, send_ref, full)


def place_kernel(idx, mine_ref, got_ref, o_ref):
    half = mine_ref.shape[1]
    o_ref[:, at(idx[0], half, 128)] = mine_ref[...]
    o_ref[:, at(1 - idx[0], half, 128)] = got_ref[...]


def place_add_kernel(idx, mine_ref, got_ref, base_ref, o_ref):
    half = mine_ref.shape[1]
    mine, other = at(idx[0], half, 128), at(1 - idx[0], half, 128)
    o_ref[:, mine] = base_ref[:, mine] + mine_ref[...]
    o_ref[:, other] = base_ref[:, other] + got_ref[...]


TAIL = INNER // 2


def tap_columns(b):
    return ((D + b * INNER, INNER), (D + (2 + b) * INNER, INNER), (D + 4 * INNER + b * TAIL, TAIL))


def pair_columns(own_ref, got_ref, keep_ref, send_ref, mine, other):
    to = 0
    for (m, count), (o, _n) in zip(mine, other):
        for r in chunks(own_ref.shape[0], 32):
            keep_ref[r, to : to + count] = own_ref[r, m : m + count] + got_ref[r, m : m + count].astype(f32)
            send_ref[r, to : to + count] = (
                own_ref[r, o : o + count] + got_ref[r, o : o + count].astype(f32)
            ).astype(bf16)
        to += count


def early_kernel(idx, own_ref, got_ref, keep_last, send_last, keep_taps, send_taps):
    for b in range(2):

        @pl.when(idx[2] == b)
        def _():
            pair_columns(own_ref, got_ref, keep_last, send_last, [(b * INNER, INNER)], [((1 - b) * INNER, INNER)])
            pair_columns(own_ref, got_ref, keep_taps, send_taps, tap_columns(b), tap_columns(1 - b))


def pair_kernel(idx, own_ref, got_ref, keep_ref, send_ref):
    for b in range(2):

        @pl.when(idx[2] == b)
        def _():
            pair_columns(own_ref, got_ref, keep_ref, send_ref, [(b * INNER, INNER)], [((1 - b) * INNER, INNER)])


def long_kernel(H, idx, keep_f, got_f, keep_l, got_l, part_ref, *send_refs):
    h = idx[3]
    for d, ref in enumerate((part_ref, *send_refs)):
        to = (h - d + H) % H
        for q, (keep, got) in enumerate(((keep_f, got_f), (keep_l, got_l))):

            @pl.when(to == q + 1)
            def _():
                ref[...] = (keep[...] + got[...].astype(f32)).astype(ref.dtype)

        @pl.when((to != 1) & (to != 2))
        def _():
            ref[...] = jnp.zeros_like(ref)


def taps_kernel(H, idx, keep_t, got_t, part_ref, *send_refs):
    h = idx[3]
    for d, ref in enumerate((part_ref, *send_refs)):
        to = (h - d + H) % H

        @pl.when(to == 0)
        def _():
            ref[:, :INNER] = (keep_t[:, :INNER] + got_t[:, :INNER].astype(f32)).astype(ref.dtype)
            ref[:, INNER:] = jnp.zeros_like(ref[:, INNER:])

        @pl.when(to == 3)
        def _():
            ref[...] = (keep_t[:, INNER:] + got_t[:, INNER:].astype(f32)).astype(ref.dtype)

        @pl.when((to != 0) & (to != 3))
        def _():
            ref[...] = jnp.zeros_like(ref)


def own_kernel(idx, first_ref, taps_ref, last_ref, unit_ref):
    h, b = idx[3], idx[2]
    unit_ref[:, INNER:] = jnp.zeros_like(unit_ref[:, INNER:])
    for i in range(2):

        @pl.when((h == 0) & (b == i))
        def _():
            unit_ref[:, :INNER] = taps_ref[i]

        @pl.when((h == 1) & (b == i))
        def _():
            unit_ref[:, :INNER] = first_ref[:, i * INNER : (i + 1) * INNER]

        @pl.when((h == 2) & (b == i))
        def _():
            unit_ref[:, :INNER] = last_ref[:, i * INNER : (i + 1) * INNER]

        @pl.when((h == 3) & (b == i))
        def _():
            unit_ref[:, :INNER] = taps_ref[2 + i]
            unit_ref[:, INNER:] = taps_ref[4, :, i * TAIL : (i + 1) * TAIL]

    @pl.when(h > 3)
    def _():
        unit_ref[...] = jnp.zeros_like(unit_ref)


def finish_kernel(H, idx, old_ref, part_long, part_taps, *refs):
    got_long, got_taps = refs[: H - 1], refs[H - 1 : 2 * (H - 1)]
    sum_ref, new_ref, cross_ref = refs[2 * (H - 1) :]
    h = idx[3]
    long = (h == 1) | (h == 2)

    @pl.when(long)
    def _():
        v = part_long[...]
        for got in got_long:
            v = v + got[...].astype(f32)
        sum_ref[:, :INNER] = v.astype(bf16)
        sum_ref[:, INNER:] = jnp.zeros_like(sum_ref[:, INNER:])
        new_ref[:, :INNER] = (muon_keep * old_ref[:, :INNER] + v).astype(bf16)
        new_ref[:, INNER:] = jnp.zeros_like(new_ref[:, INNER:])

    @pl.when(jnp.logical_not(long))
    def _():
        v = part_taps[...]
        for got in got_taps:
            v = v + got[...].astype(f32)
        sum_ref[...] = v.astype(bf16)
        new_ref[...] = (muon_keep * old_ref[...] + v).astype(bf16)

    @pl.when(h == 3)
    def _():
        cross_ref[:, :TAIL] = new_ref[:, INNER:]
        cross_ref[:, TAIL:] = new_ref[:, INNER:]

    @pl.when(h != 3)
    def _():
        cross_ref[...] = new_ref[:, :INNER]


def block_kernel(idx, new_ref, got_ref, o_ref):
    h, b = idx[3], idx[2]
    long = (h == 1) | (h == 2)
    for i in range(2):

        @pl.when(long & (b == i))
        def _():
            o_ref[:, i * INNER : (i + 1) * INNER] = new_ref[:, :INNER]
            o_ref[:, (1 - i) * INNER : (2 - i) * INNER] = got_ref[...]

        @pl.when(jnp.logical_not(long) & (b == i))
        def _():
            o_ref[:, :INNER] = new_ref[:, :INNER]
            o_ref[:, INNER + i * TAIL : INNER + (i + 1) * TAIL] = new_ref[:, INNER:]
            o_ref[:, INNER + (1 - i) * TAIL : INNER + (2 - i) * TAIL] = got_ref[:, :TAIL]


def sweep(X, Xh, Xl, A, Bh, Rh, width, low, last, carry):
    scale, squares = carry
    n = X.shape[0]
    alpha = squares * scale * scale * (1.0 / n)
    outer = scale * scale
    tile = n // 2
    rest = (coef_second + 2.0 * coef_third * alpha) * 1.0
    keep = (coef_first + coef_second * alpha + coef_third * alpha * alpha) * scale
    if low:
        Bl = mul(Xh[:, :width], Xl[:, :width], NT)
        A[...] = Bl + Bl.T
    for i in range(0, n, tile):
        r = slice(i, i + tile)
        a = mul(Xh[r, :width], Xh[:, :width], NT)
        if low:
            a = a + A[r, :]
        row = lax.broadcasted_iota(jnp.int32, (tile, n), 0) + i
        col = lax.broadcasted_iota(jnp.int32, (tile, n), 1)
        a = a * outer - jnp.where(row == col, alpha, 0.0)
        A[r, :] = a
        Bh[r, :] = a.astype(bf16)
    for i in range(0, n, tile):
        r = slice(i, i + tile)
        Rh[r, :] = (rest * A[r, :] + coef_third * mul(Bh[r, :], Bh[...], NN)).astype(bf16)
    total = jnp.zeros((8, 128), f32)
    for i in range(0, width, 256):
        c = slice(i, min(i + 256, width))
        v = keep * X[:, c] + scale * mul(Rh[...], Xh[:, c], NN)
        X[:, c] = v
        Xh[:, c] = v.astype(bf16)
        if last is not None:
            Xl[:, c] = (v - Xh[:, c].astype(f32)).astype(bf16)
        for q in range(0, c.stop - c.start, 128):
            w = v[:, q : q + 128]
            total = total + jnp.sum((w * w).reshape(n // 8, 8, 128), axis=0)
    return jnp.float32(1.0), jnp.sum(total)


def ortho_kernel(idx, own_ref, sib_ref, opp_ref, diag_ref, mine_ref, theirs_ref, X, Xh, Xl, A, Bh, Rh):
    n, C = X.shape
    k, y, h = idx[0], idx[1], idx[3]
    loc = own_ref.shape[0]
    long = (h == 1) | (h == 2)
    fifth = (h == 3) & (k == 1)
    blocks = (
        (2 * y + k, own_ref),
        (2 * y + 1 - k, sib_ref),
        (2 * (1 - y) + k, opp_ref),
        (2 * (1 - y) + 1 - k, diag_ref),
    )

    def load(first, count):
        total = jnp.zeros((8, count), f32)
        for place, ref in blocks:
            base = pl.multiple_of(place * loc, 32)
            for i in range(0, loc, 32):
                low = ref[i : i + 32, first : first + count]
                v = low.astype(f32)
                Xh[pl.ds(base + i, 32), :count] = low
                X[pl.ds(base + i, 32), :count] = v
                total = total + jnp.sum((v * v).reshape(4, 8, count), axis=0)
        squares = jnp.sum(total)
        return 1.0 / (jnp.sqrt(squares) + 1e-07), squares

    @pl.when(long)
    def _():
        carry = load(0, C)
        lax.fori_loop(0, 5, lambda i, c: sweep(X, Xh, Xl, A, Bh, Rh, C, False, None, c), carry)

    def taps(first):
        carry = load(first, INNER)
        carry = lax.fori_loop(0, 2, lambda i, c: sweep(X, Xh, Xl, A, Bh, Rh, INNER, False, True, c), carry)
        lax.fori_loop(0, 3, lambda i, c: sweep(X, Xh, Xl, A, Bh, Rh, INNER, True, True, c), carry)

    @pl.when(jnp.logical_not(long) & jnp.logical_not(fifth))
    def _():
        taps(0)

    @pl.when(fifth)
    def _():
        taps(INNER)

    mine_ref[...] = X[at(2 * y + k, loc), :].astype(bf16)
    theirs_ref[...] = X[at(2 * y + 1 - k, loc), :INNER].astype(bf16)


def step_kernel(idx, mine_ref, got_ref, o_ref):
    h, b, k = idx[3], idx[2], idx[0]

    @pl.when((h == 0) | ((h == 3) & (k == 0)))
    def _():
        o_ref[:, :INNER] = mine_ref[:, :INNER]

    @pl.when((h == 3) & (k == 1))
    def _():
        o_ref[:, :INNER] = got_ref[...]

    for i in range(2):

        @pl.when(((h == 1) | (h == 2)) & (b == i))
        def _():
            o_ref[:, :INNER] = mine_ref[:, i * INNER : (i + 1) * INNER]

        @pl.when((h == 3) & (k == 0) & (b == i))
        def _():
            o_ref[:, INNER:] = got_ref[:, i * TAIL : (i + 1) * TAIL]

        @pl.when((h == 3) & (k == 1) & (b == i))
        def _():
            o_ref[:, INNER:] = mine_ref[:, i * TAIL : (i + 1) * TAIL]

    @pl.when(h != 3)
    def _():
        o_ref[:, INNER:] = jnp.zeros_like(o_ref[:, INNER:])

    @pl.when(h > 3)
    def _():
        o_ref[:, :INNER] = jnp.zeros_like(o_ref[:, :INNER])


def join_kernel(idx, own_ref, got_ref, o_ref):
    h = idx[3]
    for q in range(2):

        @pl.when(h // 2 % 2 == q)
        def _():
            o_ref[:, q * INNER : (q + 1) * INNER] = own_ref[:, :INNER]
            o_ref[:, (1 - q) * INNER : (2 - q) * INNER] = got_ref[:, :INNER]
            o_ref[:, 2 * INNER :] = (own_ref if q else got_ref)[:, INNER:]


def apply_kernel(
    keep, rate_long, rate_tap, idx, own_ref, x_ref, z_ref, zx_ref, first_ref, taps_ref, last_ref,
    of_ref, ot_ref, ol_ref,
):
    h, b = idx[3], idx[2]
    for odd in range(2):
        for i in range(2):

            @pl.when((h % 2 == odd) & (b == i))
            def _():
                even = (own_ref, x_ref) if odd == 0 else (z_ref, zx_ref)
                odds = (z_ref, zx_ref) if odd == 0 else (own_ref, x_ref)
                for r in chunks(first_ref.shape[0], 32):
                    for q in range(2):
                        e = even[q ^ i]
                        o = odds[q ^ i]
                        lanes = slice(q * INNER, (q + 1) * INNER)
                        tail = slice(q * TAIL, (q + 1) * TAIL)
                        of_ref[r, lanes] = keep * first_ref[r, lanes] + rate_long * o[r, :INNER].astype(f32)
                        ol_ref[r, lanes] = keep * last_ref[r, lanes] + rate_long * e[r, INNER : 2 * INNER].astype(f32)
                        ot_ref[q, r, :] = keep * taps_ref[q, r, :] + rate_tap * e[r, :INNER].astype(f32)
                        ot_ref[2 + q, r, :] = keep * taps_ref[2 + q, r, :] + rate_tap * o[
                            r, INNER : 2 * INNER
                        ].astype(f32)
                        ot_ref[4, r, tail] = keep * taps_ref[4, r, tail] + rate_tap * o[r, 2 * INNER :].astype(f32)


ROWS = 24


def vector_kernel(idx, two_ref, three_ref, one_ref, cot_ref, sq_ref, o_ref):
    y, c = idx[1], 2 * idx[1] + idx[0]
    o_ref[...] = jnp.zeros_like(o_ref)
    o_ref[pl.ds(y, 1), :] = one_ref[0:1, :]
    o_ref[pl.ds(2 + y, 1), :] = one_ref[1:2, :]
    two = two_ref[...].T
    three = three_ref[...].T
    wide = two_ref.shape[0]
    pieces = (two[2:3], two[0:1], two[1:2], three[2:3], three[0:1], three[1:2])
    for i, piece in enumerate(pieces):
        o_ref[pl.ds(4 + 6 * y + i, 1), :wide] = piece
    cot = cot_ref[...].T
    o_ref[pl.ds(16 + c, 1), : cot_ref.shape[0]] = cot[0:1]
    for i in range(3):
        o_ref[20 + i : 21 + i, :128] = sq_ref[i : i + 1, :]


def adam_kernel(v_ref, par_ref, mom_ref, sqr_ref, first_ref, second_ref, value_ref, root_ref, g):
    wide = INNER // 2
    g[0:4, :] = v_ref[0:4, :]
    for i in range(6):
        g[4 + i : 5 + i, :wide] = v_ref[4 + i : 5 + i, :wide]
        g[4 + i : 5 + i, wide:] = v_ref[10 + i : 11 + i, :wide]
    for i in range(2):
        g[10 + i : 11 + i, :wide] = v_ref[16 + 2 * i : 17 + 2 * i, :wide]
        g[10 + i : 11 + i, wide:] = v_ref[17 + 2 * i : 18 + 2 * i, :wide]
    per = INNER // 128
    for r in range(12):
        for q in range(per):
            at_row = slice(r * per + q, r * per + q + 1)
            grad = g[r : r + 1, q * 128 : (q + 1) * 128]
            par = par_ref[at_row, :]
            first = adam_first * mom_ref[at_row, :] + (1.0 - adam_first) * grad
            second = adam_second * sqr_ref[at_row, :] + (1.0 - adam_second) * grad * grad
            first_ref[at_row, :] = first
            second_ref[at_row, :] = second
            value_ref[at_row, :] = par - adam_rate * (
                (first / (1.0 - adam_first**STEP)) / (jnp.sqrt(second / (1.0 - adam_second**STEP)) + adam_eps)
                + decay_rate * par
            )
    count = v_ref[22:23, :128] * D
    root_ref[...] = jnp.zeros_like(root_ref)
    for i in range(2):
        root_ref[i : i + 1, :] = jnp.sqrt(v_ref[20 + i : 21 + i, :128] / count)


def after(value, *others):
    return lax.optimization_barrier((value, *others))[0]


def body(
    tokens,
    cotangent,
    lengths,
    valid_mask,
    weight_first,
    weight_dilated,
    weight_last,
    momentum_first,
    momentum_dilated,
    momentum_last,
    vector_params,
    vector_moment,
    vector_square,
):
    C = lax.axis_size("ch")
    S = lax.axis_size("seq")
    c = lax.axis_index("ch")
    s = lax.axis_index("seq")
    k = c % 2
    y = c // 2
    T = tokens.shape[0]
    half = T // 2
    loc = weight_first.shape[1]
    wide = 2 * loc
    col = D // C
    H = S // 2
    b = s % 2
    h = s // 2
    idx = jnp.stack([k, y, b, h, s, s * T + k * half]).astype(jnp.int32)

    sib = [(i, i ^ 1) for i in range(C)]
    opp = [(i, i ^ 2) for i in range(C)]
    diag = [(i, i ^ 3) for i in range(C)]
    xsw = [(i, i ^ 1) for i in range(S)]

    def swap_core(v):
        return lax.ppermute(v, "ch", sib)

    def swap_y(v):
        return lax.ppermute(v, "ch", opp)

    def swap_x(v):
        return lax.ppermute(v, "seq", xsw)

    def along_h(v, pairs):
        return lax.ppermute(v, "seq", [(2 * i + q, 2 * j + q) for i, j in pairs for q in range(2)])

    outer_pairs = []
    for i in range(S):
        for j in range(C):
            if j % 2 == 0 and i >= 1:
                outer_pairs.append((i * C + j, (i - 1) * C + (j ^ 1)))
            if j % 2 == 1 and i + 1 < S:
                outer_pairs.append((i * C + j, (i + 1) * C + (j ^ 1)))

    def swap_outer(v):
        return lax.ppermute(v, ("seq", "ch"), outer_pairs)

    w_first, w_taps, w_last = weight_first.T, jnp.swapaxes(weight_dilated, 1, 2), weight_last
    m_first, m_taps, m_last = momentum_first.T, jnp.swapaxes(momentum_dilated, 1, 2), momentum_last
    cot = cotangent.T
    valid = valid_mask.reshape(1, T)
    gain_shift = vector_params[: 2 * D].reshape(2, D)
    inner_rows = vector_params[2 * D : 2 * D + 6 * INNER].reshape(6, INNER)
    cols = lax.dynamic_slice_in_dim(inner_rows, y * wide, wide, 1).T
    bias_three = vector_params[2 * D + 6 * INNER :].reshape(1, D)

    low_first, cot_mine, cot_other, cot_sums = call(
        prep_kernel,
        [((loc, D), bf16), ((col, half), bf16), ((col, half), bf16), ((col, 128), f32)],
        [idx],
        [w_first, cot],
    )
    got_first = swap_core(low_first)
    cot_opp = swap_y(cot_mine)
    cot_sib = swap_core(cot_other)
    cot_diag = lax.ppermute(cot_other, "ch", diag)

    rows = 128
    steps = half // rows
    hid_one, hat_one, slope_one, scale_one = pl.pallas_call(
        input_kernel,
        out_shape=[
            jax.ShapeDtypeStruct((half, D), bf16),
            jax.ShapeDtypeStruct((half, D), bf16),
            jax.ShapeDtypeStruct((half, D), bf16),
            jax.ShapeDtypeStruct((half, 128), f32),
        ],
        grid_spec=pltpu.PrefetchScalarGridSpec(
            num_scalar_prefetch=1,
            grid=(steps,),
            in_specs=[
                pl.BlockSpec((rows, D), lambda i, idx: (idx[0] * steps + i, 0)),
                pl.BlockSpec((2, D), lambda i, idx: (0, 0)),
            ],
            out_specs=[
                pl.BlockSpec((rows, D), lambda i, idx: (i, 0)),
                pl.BlockSpec((rows, D), lambda i, idx: (i, 0)),
                pl.BlockSpec((rows, D), lambda i, idx: (i, 0)),
                pl.BlockSpec((rows, 128), lambda i, idx: (i, 0)),
            ],
        ),
        compiler_params=pltpu.CompilerParams(vmem_limit_bytes=56 * MIB),
        cost_estimate=pl.CostEstimate(flops=5 * 10**9, bytes_accessed=8 * 10**6, transcendentals=10**6),
    )(idx, tokens, gain_shift)

    (low_rest,) = call(rest_kernel, [((loc, D + KERNEL_TAPS * INNER), bf16)], [], [w_last, w_taps])
    got_rest = swap_core(low_rest)

    full_first, inner_one, st_two = call(
        first_kernel,
        [((wide, D), bf16), ((wide, half), f32), ((8, half), f32)],
        [idx],
        [low_first, got_first, hid_one, cols],
    )
    st_two_got = after(swap_y(st_two), cot_sib, cot_opp, cot_diag)
    hid_two, hat_two, slope_two = call(
        second_kernel,
        [((wide, half), bf16), ((wide, half), f32), ((wide, half), f32)],
        [idx],
        [inner_one, st_two, st_two_got, cols, valid],
    )
    hid_two_got = swap_y(hid_two)
    slab_in, slab_out = call(
        slab_kernel, [((INNER, REACH), bf16)] * 2, [idx], [hid_two, hid_two_got]
    )
    got_in, got_out = swap_core(slab_in), swap_outer(slab_out)
    ext, inner_two, st_three, full_last, full_taps, masks = call(
        functools.partial(conv_kernel, S * T),
        [
            ((INNER, half + 2 * REACH), bf16),
            ((wide, half), f32),
            ((8, half), f32),
            ((wide, D), bf16),
            ((wide, KERNEL_TAPS * INNER), bf16),
            ((8, half), f32),
        ],
        [idx, lengths],
        [hid_two, hid_two_got, got_in, got_out, low_rest, got_rest, cols],
        scratch=[((KERNEL_TAPS * INNER, half), bf16)],
        flops=10**9,
    )
    st_three_got = swap_y(st_three)
    gw, g_three = call(
        cotangent_kernel,
        [((D, half), bf16), ((wide, half), f32)],
        [idx],
        [full_last, cot_mine, cot_sib, cot_opp, cot_diag],
        flops=4 * 10**8,
    )
    hid_three, e_three, hat_three, part_three = call(
        third_kernel,
        [((wide, half), bf16), ((wide, half), f32), ((wide, half), f32), ((8, half), f32)],
        [],
        [inner_two, st_three, st_three_got, cols, g_three],
    )
    part_three_got = swap_y(part_three)
    dz_two, slab_in, slab_out, sums_three = call(
        third_back_kernel,
        [((wide, half), bf16), ((wide, REACH), bf16), ((wide, REACH), bf16), ((wide, 128), f32)],
        [idx],
        [e_three, hat_three, part_three, part_three_got, cols],
    )
    got_in, got_out = swap_core(slab_in), swap_outer(slab_out)
    early_size = D + KERNEL_TAPS * INNER
    early_own, early_send = call(
        grads_kernel,
        [((loc, early_size), f32), ((loc, early_size), bf16)],
        [idx],
        [dz_two, ext, masks, hid_three, gw],
        scratch=[((wide, early_size), f32)],
        flops=16 * 10**8,
        limit=32,
    )
    early_got = swap_core(early_send)
    back_own, back_send = call(
        conv_back_kernel,
        [((wide, half), f32), ((wide, half), bf16)],
        [idx],
        [dz_two, got_in, got_out, masks, full_taps],
        scratch=[((wide, half + 2 * REACH), bf16), ((INNER, half), f32)],
        flops=10**9,
    )
    back_got = swap_y(back_send)
    unit, unit_low = ((loc, INNER), f32), ((loc, INNER), bf16)
    last_keep, last_send, taps_keep, taps_send = call(
        early_kernel,
        [unit, unit_low, ((loc, 2 * INNER + TAIL), f32), ((loc, 2 * INNER + TAIL), bf16)],
        [idx],
        [early_own, early_got],
    )
    last_got, taps_got = swap_x(last_send), swap_x(taps_send)
    e_two, part_two = call(
        second_back_kernel,
        [((wide, half), f32), ((8, half), f32)],
        [],
        [after(back_own, taps_send), back_got, slope_two, hat_two, cols],
    )
    part_two_got = swap_y(part_two)
    dz_one, first_own, first_send, sums_two = call(
        first_back_kernel,
        [((wide, half), bf16), ((loc, D), f32), ((loc, D), bf16), ((wide, 128), f32)],
        [idx],
        [e_two, hat_two, part_two, part_two_got, st_two, st_two_got, cols, hid_one],
        scratch=[((wide, D), f32)],
        flops=4 * 10**8,
    )
    first_got = swap_core(first_send)
    first_keep, first_low = call(pair_kernel, [unit, unit_low], [idx], [first_own, first_got])
    first_got = swap_x(first_low)

    span = H
    while span > 4:
        span //= 2
        fold = [(i + span, i) for i in range(span)]

        def folded(keep, got):
            total = keep + got.astype(f32)
            return total + along_h(total.astype(bf16), fold).astype(f32), jnp.zeros_like(got)

        first_keep, first_got = folded(first_keep, first_got)
        last_keep, last_got = folded(last_keep, last_got)
        taps_keep, taps_got = folded(taps_keep, taps_got)
    line = 4

    def to_owners(sends, owners):
        return [
            along_h(v, [((j + d + 1) % line, j) for j in owners]) for d, v in enumerate(sends)
        ]

    size_taps = (loc, INNER + TAIL)
    part_taps, *sends = call(
        functools.partial(taps_kernel, line),
        [(size_taps, f32)] + [(size_taps, bf16)] * (line - 1),
        [idx],
        [taps_keep, taps_got],
    )
    got_taps = to_owners(sends, (0, 3))
    part_long, *sends = call(
        functools.partial(long_kernel, line),
        [unit] + [unit_low] * (line - 1),
        [idx],
        [after(first_keep, part_taps), first_got, last_keep, last_got],
    )
    got_long = to_owners(sends, (1, 2))
    (old_unit,) = call(own_kernel, [(size_taps, f32)], [idx], [m_first, m_taps, m_last])
    sum_unit, new_unit, cross = call(
        functools.partial(finish_kernel, line),
        [(size_taps, bf16), (size_taps, bf16), unit_low],
        [idx],
        [old_unit, part_long, part_taps, *got_long, *got_taps],
    )
    cross_got = swap_x(cross)
    (block,) = call(block_kernel, [((loc, D), bf16)], [idx], [new_unit, cross_got])
    block_sib, block_opp = swap_core(block), swap_y(block)
    block_diag = swap_core(block_opp)

    def joined_with(unit):
        got = along_h(unit, [(i, i ^ 2) for i in range(4)])
        return call(join_kernel, [((loc, 2 * INNER + TAIL), bf16)], [idx], [unit, got])[0]

    def next_along_z(joined):
        return along_h(joined, [(i, i ^ 1) for i in range(4)])

    def spread(parts):
        span = 4
        while span < H:
            pairs = [(i, i + span) for i in range(span)]
            parts = [jnp.where((h >= span) & (h < 2 * span), along_h(v, pairs), v) for v in parts]
            span *= 2
        return parts

    def apply(keep, rate_long, rate_tap, parts, first, taps, last):
        return call(
            functools.partial(apply_kernel, keep, rate_long, rate_tap),
            [((loc, D), f32), ((KERNEL_TAPS, loc, INNER), f32), ((loc, D), f32)],
            [idx],
            [*parts, first, taps, last],
            limit=32,
        )

    half_out = [((half, HALF_D), f32), ((half, HALF_D), bf16)]
    back_own, back_send = call(
        halves_kernel, half_out, [idx], [dz_one, full_first], scratch=[((half, D), f32)], flops=4 * 10**8
    )
    back_got = swap_y(back_send)
    e_one, part_one, sums_one = call(
        token_kernel,
        [((half, HALF_D), f32), ((half, 128), f32), ((8, HALF_D), f32)],
        [idx],
        [back_own, back_got, slope_one, hat_one, gain_shift],
    )
    (part_one,) = call(flip_kernel, [((8, half), f32)], [], [part_one])

    joined = joined_with(sum_unit)
    mine, theirs = call(
        ortho_kernel,
        [((loc, D), bf16), ((loc, INNER), bf16)],
        [idx],
        [after(block, joined), block_sib, block_opp, block_diag],
        scratch=[
            ((INNER, D), f32),
            ((INNER, D), bf16),
            ((INNER, INNER), bf16),
            ((INNER, INNER), f32),
            ((INNER, INNER), bf16),
            ((INNER, INNER), bf16),
        ],
        limit=32,
        flops=14 * 10**9,
    )
    joined_x = swap_x(joined)
    other = next_along_z(joined)
    theirs_got = swap_core(theirs)
    (step_unit,) = call(step_kernel, [(size_taps, bf16)], [idx], [after(mine, joined_x, other), theirs_got])
    other_x = swap_x(other)
    new_first, new_taps, new_last = apply(
        muon_keep, 1.0, 1.0, spread([joined, joined_x, other, other_x]), m_first, m_taps, m_last
    )
    keep_weight = 1.0 - muon_rate * decay_rate
    rate = muon_rate * muon_scale
    joined = joined_with(step_unit)
    joined_x = swap_x(joined)
    other = next_along_z(joined)
    other_x = swap_x(other)
    out_first, out_taps, out_last = apply(
        keep_weight,
        -rate * math.sqrt(D),
        -rate * math.sqrt(INNER),
        spread([joined, joined_x, other, other_x]),
        w_first,
        w_taps,
        w_last,
    )

    branch_own, branch_send = call(
        halves_kernel,
        half_out,
        [idx],
        [after(hid_three, step_unit), full_last],
        scratch=[((half, D), f32)],
        flops=4 * 10**8,
    )
    branch_got = swap_y(branch_send)
    own_tokens = lax.dynamic_slice(tokens, (k * half, y * HALF_D), (half, HALF_D))
    out_mine, out_send, squares = call(
        output_kernel,
        [((col, half), f32), ((col, half), f32), ((8, 128), f32)],
        [idx],
        [branch_own, branch_got, own_tokens, bias_three, valid],
        scratch=[((HALF_D, half), f32)],
    )
    (block_output,) = call(place_kernel, [((col, T), f32)], [idx], [out_mine, swap_core(out_send)])

    grad_mine, grad_send = call(
        token_back_kernel,
        [((col, half), f32), ((col, half), f32)],
        [idx],
        [e_one, hat_one, scale_one, part_one, swap_y(part_one)],
        scratch=[((half, HALF_D), f32), ((HALF_D, half), f32)],
    )
    (tokens_grad,) = call(
        place_add_kernel, [((col, T), f32)], [idx], [grad_mine, swap_core(grad_send), cot]
    )

    (vector,) = call(
        vector_kernel, [((ROWS, INNER), f32)], [idx], [sums_two, sums_three, sums_one, cot_sums, squares]
    )
    vector = vector + swap_core(vector)
    vector = vector + swap_y(vector)
    bit = 1
    while bit < S:
        vector = vector + lax.ppermute(vector, "seq", [(i, i ^ bit) for i in range(S)])
        bit *= 2
    flat = (VECTOR // 128, 128)
    vector_first, vector_second, vector_values, root = call(
        adam_kernel,
        [(flat, f32)] * 3 + [((8, 128), f32)],
        [],
        [vector, vector_params.reshape(flat), vector_moment.reshape(flat), vector_square.reshape(flat)],
        scratch=[((12, INNER), f32)],
    )
    vector_first, vector_second, vector_values = (
        v.reshape(VECTOR) for v in (vector_first, vector_second, vector_values)
    )
    root_means = root[:2, 0]
    return (
        block_output.T,
        tokens_grad.T,
        out_first.T,
        jnp.swapaxes(out_taps, 1, 2),
        out_last,
        new_first.T,
        jnp.swapaxes(new_taps, 1, 2),
        new_last,
        vector_first,
        vector_second,
        vector_values,
        root_means,
    )


def solution(mesh):
    placed = (
        P("seq", None),
        P("seq", "ch"),
        P(),
        P("seq"),
        P(None, "ch"),
        P(None, None, "ch"),
        P("ch", None),
        P(None, "ch"),
        P(None, None, "ch"),
        P("ch", None),
        P(),
        P(),
        P(),
    )
    return jax.shard_map(
        body,
        mesh=mesh,
        in_specs=placed,
        out_specs=(
            P("seq", "ch"),
            P("seq", "ch"),
            P(None, "ch"),
            P(None, None, "ch"),
            P("ch", None),
            P(None, "ch"),
            P(None, None, "ch"),
            P("ch", None),
            P(),
            P(),
            P(),
            P(),
        ),
        check_vma=False,
    )
```

```python
import functools
import math

import jax
import jax.numpy as jnp
from jax import lax
from jax.experimental import pallas as pl
from jax.experimental.pallas import tpu as pltpu
from jax.sharding import PartitionSpec as P

D = 1280
INNER = 640
KERNEL_TAPS = 5
DILATION_SPAN = 128
STEP = 10

norm_eps = 1e-05
coef_first = 3.4445
coef_second = -4.775
coef_third = 2.0315
adam_rate = 0.4
adam_first = 0.9
adam_second = 0.999
adam_eps = 1e-08
decay_rate = 0.01
muon_rate = 0.1
muon_keep = 0.95
muon_scale = 0.2
REACH = KERNEL_TAPS // 2 * DILATION_SPAN
VECTOR = 3 * D + 6 * INNER
HALF_D = D // 2
MIB = 1024 * 1024

f32 = jnp.float32
bf16 = jnp.bfloat16
NN = (((1,), (0,)), ((), ()))
NT = (((1,), (1,)), ((), ()))
TN = (((0,), (0,)), ((), ()))


def mul(a, b, dims):
    return lax.dot_general(a, b, dims, preferred_element_type=f32)


def erf_parts(v):
    a = jnp.abs(v) * math.sqrt(0.5)
    t = pl.reciprocal(1.0 + 0.3275911 * a)
    e = jnp.exp(-a * a)
    p = t * (0.254829592 + t * (-0.284496736 + t * (1.421413741 + t * (-1.453152027 + t * 1.061405429))))
    tail = 0.5 * p * e
    return jnp.where(v >= 0, 1.0 - tail, tail), e


def gelu_pair(v):
    cdf, e = erf_parts(v)
    return v * cdf, cdf + v * e * (1.0 / math.sqrt(2.0 * math.pi))


VMEM = pl.BlockSpec(memory_space=pltpu.VMEM)
SMEM = pl.BlockSpec(memory_space=pltpu.SMEM)


def call(kernel, outs, scalars, arrays, scratch=(), limit=16, flops=1000):
    shapes = [jax.ShapeDtypeStruct(shape, dtype) for shape, dtype in outs]
    return pl.pallas_call(
        kernel,
        out_shape=shapes,
        in_specs=[SMEM] * len(scalars) + [VMEM] * len(arrays),
        out_specs=[VMEM] * len(outs),
        scratch_shapes=[pltpu.VMEM(shape, dtype) for shape, dtype in scratch],
        compiler_params=pltpu.CompilerParams(vmem_limit_bytes=limit * MIB),
        cost_estimate=pl.CostEstimate(flops=flops, bytes_accessed=1000, transcendentals=0),
    )(*scalars, *arrays)


def chunks(count, step):
    return [pl.ds(i, step) for i in range(0, count, step)]


def at(index, count, step=32):
    return pl.ds(pl.multiple_of(index * count, step), count)


def prep_kernel(idx, w_ref, cot_ref, wo_ref, all_ref, other_ref, sums_ref):
    half = other_ref.shape[1]
    for r in chunks(cot_ref.shape[0], 32):
        v = cot_ref[r, :]
        all_ref[r, :] = v.astype(bf16)
        other_ref[r, :] = cot_ref[r, at(1 - idx[0], half, 128)].astype(bf16)
        sums_ref[r, :] = jnp.broadcast_to(jnp.sum(v, axis=1, keepdims=True), (32, 128))
    for r in chunks(w_ref.shape[0], 32):
        wo_ref[r, :] = w_ref[r, :].astype(bf16)


def rest_kernel(last_ref, taps_ref, o_ref):
    for r in chunks(last_ref.shape[0], 32):
        o_ref[r, :D] = last_ref[r, :].astype(bf16)
        for j in range(KERNEL_TAPS):
            o_ref[r, D + j * INNER : D + (j + 1) * INNER] = taps_ref[j, r, :].astype(bf16)


def input_kernel(idx, tok_ref, gs_ref, hid_ref, hat_ref, slope_ref, scale_ref):
    for r in chunks(tok_ref.shape[0], 16):
        v = tok_ref[r, :]
        center = jnp.sum(v, axis=1, keepdims=True) * (1.0 / D)
        square = jnp.sum(v * v, axis=1, keepdims=True) * (1.0 / D)
        scale = lax.rsqrt(square - center * center + norm_eps)
        hat = (v - center) * scale
        hid, slope = gelu_pair(hat * gs_ref[0:1, :] + gs_ref[1:2, :])
        hid_ref[r, :] = hid.astype(bf16)
        hat_ref[r, :] = hat.astype(bf16)
        slope_ref[r, :] = slope.astype(bf16)
        scale_ref[r, :] = jnp.broadcast_to(scale, (16, 128))


def put_stats(ref, parts):
    for i, part in enumerate(parts):
        ref[i : i + 1, :] = part


def first_kernel(idx, own_ref, got_ref, hid_ref, cols_ref, w_ref, inner_ref, st_ref):
    k = idx[0]
    loc = own_ref.shape[0]
    w_ref[at(k, loc), :] = own_ref[...]
    w_ref[at(1 - k, loc), :] = got_ref[...]
    v = mul(w_ref[...], hid_ref[...], NT) + cols_ref[:, 0:1]
    inner_ref[...] = v
    put_stats(st_ref, (jnp.sum(v, axis=0, keepdims=True), jnp.sum(v * v, axis=0, keepdims=True)))


def center_scale(st_ref, got_ref):
    center = (st_ref[0:1, :] + got_ref[0:1, :]) * (1.0 / INNER)
    square = (st_ref[1:2, :] + got_ref[1:2, :]) * (1.0 / INNER)
    return center, lax.rsqrt(square - center * center + norm_eps)


def second_kernel(
    idx, inner_ref, st_ref, got_ref, cols_ref, valid_ref, in_ref, out_ref, hat_ref, slope_ref, hid_ref
):
    center, scale = center_scale(st_ref, got_ref)
    valid = valid_ref[:, at(idx[0], hid_ref.shape[1], 128)].astype(f32)
    for r in chunks(inner_ref.shape[0], 32):
        hat = (inner_ref[r, :] - center) * scale
        hid, slope = gelu_pair(hat * cols_ref[r, 1:2] + cols_ref[r, 2:3])
        hid_ref[r, :] = (hid * valid).astype(bf16)
        hat_ref[r, :] = hat
        slope_ref[r, :] = slope * valid
    slabs_of(idx[0], hid_ref, slice(None), in_ref, out_ref)


def slabs_of(k, v_ref, row, in_ref, out_ref):
    half = v_ref.shape[1]
    rows = v_ref.shape[0]
    in_ref[row, :] = v_ref[:, at(1 - k, half - REACH, 128)]
    out_ref[row, :] = v_ref[:, at(k, half - REACH, 128)]


def fill_reach(k, ext_ref, in_ref, out_ref, half):
    @pl.when(k == 0)
    def _():
        ext_ref[:, :REACH] = out_ref[...]
        ext_ref[:, REACH + half :] = in_ref[...]

    @pl.when(k == 1)
    def _():
        ext_ref[:, :REACH] = in_ref[...]
        ext_ref[:, REACH + half :] = out_ref[...]


def conv_kernel(
    total, idx, lengths, own_in, own_out, opp_in, opp_out, sib_in, sib_opp_in, seq_out, seq_opp_out,
    wo_ref, wg_ref, cols_ref, ext_ref, inner_ref, st_ref, last_ref, taps_ref, mask_ref, stack,
):
    k, y = idx[0], idx[1]
    wide, reach = own_in.shape
    half = 2 * reach
    loc = wo_ref.shape[0]
    for q in range(2):
        @pl.when(k == q)
        def _():
            for place, (mine, other) in enumerate(
                ((seq_out, seq_opp_out), (own_out, opp_out), (own_in, opp_in), (sib_in, sib_opp_in))
            ):
                place = 3 - place if q else place
                lanes = slice(place * reach, (place + 1) * reach)
                ext_ref[at(y, wide), lanes] = mine[...]
                ext_ref[at(1 - y, wide), lanes] = other[...]

    last_ref[at(k, loc), :] = wo_ref[:, :D]
    last_ref[at(1 - k, loc), :] = wg_ref[:, :D]
    taps_ref[at(k, loc), :] = wo_ref[:, D:]
    taps_ref[at(1 - k, loc), :] = wg_ref[:, D:]
    positions = idx[5] - REACH + lax.broadcasted_iota(jnp.int32, (1, half + 2 * REACH), 1)
    segment = jnp.zeros_like(positions)
    bound = jnp.int32(0)
    for i in range(lengths.shape[0]):
        bound = bound + lengths[i]
        segment = segment + (positions >= bound).astype(jnp.int32)
    segment = jnp.where((positions >= 0) & (positions < total), segment, -1)
    centre = segment[:, REACH : REACH + half]
    for j in range(KERNEL_TAPS):
        lanes = slice(j * DILATION_SPAN, j * DILATION_SPAN + half)
        mask = (segment[:, lanes] == centre).astype(f32)
        mask_ref[j : j + 1, :] = mask
        low = mask.astype(bf16)
        for i in range(0, INNER, 160):
            stack[j * INNER + i : j * INNER + i + 160, :] = ext_ref[i : i + 160, lanes] * low
    v = mul(taps_ref[...], stack[...], NN) + cols_ref[:, 3:4]
    inner_ref[...] = v
    put_stats(st_ref, (jnp.sum(v, axis=0, keepdims=True), jnp.sum(v * v, axis=0, keepdims=True)))


def cotangent_kernel(idx, last_ref, all_ref, sib_ref, opp_ref, diag_ref, gw_ref, g_ref):
    k, y = idx[0], idx[1]
    col, half = sib_ref.shape
    mine = at(k, half, 128)
    gw_ref[at(2 * y + k, col), :] = all_ref[:, mine]
    gw_ref[at(2 * y + 1 - k, col), :] = sib_ref[...]
    gw_ref[at(2 * (1 - y) + k, col), :] = opp_ref[:, mine]
    gw_ref[at(2 * (1 - y) + 1 - k, col), :] = diag_ref[...]
    g_ref[...] = mul(last_ref[...], gw_ref[...], NN)


def other_half_kernel(idx, all_ref, o_ref):
    o_ref[...] = all_ref[:, at(1 - idx[0], o_ref.shape[1], 128)]


def third_kernel(inner_ref, st_ref, got_ref, cols_ref, g_ref, hid_ref, e_ref, hat_ref, part_ref):
    center, scale = center_scale(st_ref, got_ref)
    plain = jnp.zeros_like(center)
    cross = jnp.zeros_like(center)
    for r in chunks(inner_ref.shape[0], 32):
        hat = (inner_ref[r, :] - center) * scale
        gain = cols_ref[r, 4:5]
        hid, slope = gelu_pair(hat * gain + cols_ref[r, 5:6])
        hid_ref[r, :] = hid.astype(bf16)
        hat_ref[r, :] = hat
        e = slope * g_ref[r, :]
        e_ref[r, :] = e
        eg = e * gain
        plain = plain + jnp.sum(eg, axis=0, keepdims=True)
        cross = cross + jnp.sum(eg * hat, axis=0, keepdims=True)
    put_stats(part_ref, (plain, cross, scale))


def norm_back(r, e_ref, hat_ref, part_ref, got_ref, scale, gain, sums_ref):
    plain = (part_ref[0:1, :] + got_ref[0:1, :]) * (1.0 / INNER)
    cross = (part_ref[1:2, :] + got_ref[1:2, :]) * (1.0 / INNER)
    e, hat = e_ref[r, :], hat_ref[r, :]
    grad = scale * (e * gain - plain - hat * cross)
    sums_ref[r, 0:1] = jnp.sum(e * hat, axis=1, keepdims=True)
    sums_ref[r, 1:2] = jnp.sum(e, axis=1, keepdims=True)
    sums_ref[r, 2:3] = jnp.sum(grad, axis=1, keepdims=True)
    return grad


def third_back_kernel(idx, e_ref, hat_ref, part_ref, got_ref, cols_ref, dz_ref, in_ref, out_ref, sums_ref):
    for r in chunks(e_ref.shape[0], 32):
        grad = norm_back(r, e_ref, hat_ref, part_ref, got_ref, part_ref[2:3, :], cols_ref[r, 4:5], sums_ref)
        dz_ref[r, :] = grad.astype(bf16)
    slabs_of(idx[0], dz_ref, slice(None), in_ref, out_ref)


def split_rows(k, full, own_ref, send_ref, lanes):
    loc = own_ref.shape[0]
    own_ref[:, lanes] = full[at(k, loc), lanes]
    send_ref[:, lanes] = full[at(1 - k, loc), lanes].astype(bf16)


def grads_kernel(idx, dz_ref, ext_ref, mask_ref, hid_ref, gw_ref, own_ref, send_ref, full):
    k = idx[0]
    half = dz_ref.shape[1]
    full[:, :D] = mul(hid_ref[...], gw_ref[...], NT)
    split_rows(k, full, own_ref, send_ref, slice(0, D))
    for j in range(KERNEL_TAPS):
        masked = dz_ref[...] * mask_ref[j : j + 1, :].astype(bf16)
        moved = ext_ref[:, j * DILATION_SPAN : j * DILATION_SPAN + half]
        lanes = slice(D + j * INNER, D + (j + 1) * INNER)
        full[:, lanes] = mul(masked, moved, NT)
        split_rows(k, full, own_ref, send_ref, lanes)


def conv_back_kernel(idx, dz_ref, in_ref, out_ref, mask_ref, taps_ref, own_ref, send_ref, ext, full):
    k, y = idx[0], idx[1]
    wide, half = dz_ref.shape
    ext[:, REACH : REACH + half] = dz_ref[...]
    fill_reach(k, ext, in_ref, out_ref, half)
    total = None
    for j in range(KERNEL_TAPS):
        begin = REACH - (j - KERNEL_TAPS // 2) * DILATION_SPAN
        mask = mask_ref[KERNEL_TAPS - 1 - j : KERNEL_TAPS - j, :].astype(bf16)
        part = mul(taps_ref[:, j * INNER : (j + 1) * INNER], ext[:, begin : begin + half] * mask, TN)
        total = part if total is None else total + part
    full[...] = total
    own_ref[...] = full[at(y, wide), :]
    send_ref[...] = full[at(1 - y, wide), :].astype(bf16)


def second_back_kernel(own_ref, got_ref, slope_ref, hat_ref, cols_ref, e_ref, part_ref):
    plain = jnp.zeros((1, own_ref.shape[1]), f32)
    cross = jnp.zeros_like(plain)
    for r in chunks(own_ref.shape[0], 32):
        e = slope_ref[r, :] * (own_ref[r, :] + got_ref[r, :].astype(f32))
        e_ref[r, :] = e
        eg = e * cols_ref[r, 1:2]
        plain = plain + jnp.sum(eg, axis=0, keepdims=True)
        cross = cross + jnp.sum(eg * hat_ref[r, :], axis=0, keepdims=True)
    put_stats(part_ref, (plain, cross))


def first_back_kernel(
    idx, e_ref, hat_ref, part_ref, got_ref, st_ref, stg_ref, cols_ref, hid_ref,
    dz_ref, own_ref, send_ref, sums_ref, full,
):
    _, scale = center_scale(st_ref, stg_ref)
    for r in chunks(e_ref.shape[0], 32):
        grad = norm_back(r, e_ref, hat_ref, part_ref, got_ref, scale, cols_ref[r, 1:2], sums_ref)
        dz_ref[r, :] = grad.astype(bf16)
    full[...] = mul(dz_ref[...], hid_ref[...], NN)
    split_rows(idx[0], full, own_ref, send_ref, slice(0, D))


def halves_kernel(idx, z_ref, w_ref, own_ref, send_ref, full):
    y = idx[1]
    full[...] = mul(z_ref[...], w_ref[...], TN)
    for r in chunks(full.shape[0], 64):
        own_ref[r, :] = full[r, at(y, HALF_D, 128)]
        send_ref[r, :] = full[r, at(1 - y, HALF_D, 128)].astype(bf16)


def column_halves(k, flipped, mine_ref, send_ref, full):
    col = mine_ref.shape[0]
    full[...] = flipped
    mine_ref[...] = full[at(k, col), :]
    send_ref[...] = full[at(1 - k, col), :]


def output_kernel(idx, own_ref, got_ref, tok_ref, bias_ref, valid_ref, mine_ref, send_ref, sq_ref, full):
    k, y = idx[0], idx[1]
    half = own_ref.shape[0]
    bias = bias_ref[:, at(y, HALF_D, 128)]
    branch = own_ref[...] + got_ref[...].astype(f32) + bias
    out = tok_ref[...] + branch
    valid = valid_ref[:, at(k, half, 128)].astype(f32)
    sq_ref[0:1, :] = jnp.sum(valid * mul_rows(out), axis=1, keepdims=True) * jnp.ones((1, 128), f32)
    sq_ref[1:2, :] = jnp.sum(valid * mul_rows(branch), axis=1, keepdims=True) * jnp.ones((1, 128), f32)
    sq_ref[2:3, :] = jnp.sum(valid, axis=1, keepdims=True) * jnp.full((1, 128), 0.5, f32)
    sq_ref[3:8, :] = jnp.zeros((5, 128), f32)
    column_halves(k, out.T, mine_ref, send_ref, full)


def mul_rows(v):
    rows = jnp.sum(v * v, axis=1, keepdims=True)
    return jnp.broadcast_to(rows, (v.shape[0], 128)).T[0:1, :]


def token_kernel(idx, own_ref, got_ref, slope_ref, hat_ref, gs_ref, e_ref, part_ref, sums_ref):
    y = idx[1]
    cols = at(y, HALF_D, 128)
    gain = gs_ref[0:1, cols]
    sum_cross = jnp.zeros((1, HALF_D), f32)
    sum_plain = jnp.zeros((1, HALF_D), f32)
    for r in chunks(own_ref.shape[0], 32):
        e = slope_ref[r, cols].astype(f32) * (own_ref[r, :] + got_ref[r, :].astype(f32))
        hat = hat_ref[r, cols].astype(f32)
        eg = e * gain
        e_ref[r, :] = eg
        part_ref[r, 0:1] = jnp.sum(eg, axis=1, keepdims=True)
        part_ref[r, 1:2] = jnp.sum(eg * hat, axis=1, keepdims=True)
        sum_cross = sum_cross + jnp.sum(e * hat, axis=0, keepdims=True)
        sum_plain = sum_plain + jnp.sum(e, axis=0, keepdims=True)
    put_stats(sums_ref, (sum_cross, sum_plain))


def flip_kernel(part_ref, o_ref):
    o_ref[...] = part_ref[...].T[0:8, :]


def token_back_kernel(idx, e_ref, hat_ref, scale_ref, part_ref, got_ref, mine_ref, send_ref, rows, full):
    cols = at(idx[1], HALF_D, 128)
    means = ((part_ref[...] + got_ref[...]) * (1.0 / D)).T
    for r in range(0, e_ref.shape[0], 64):
        s = slice(r, r + 64)
        hat = hat_ref[s, cols].astype(f32)
        rows[s, :] = scale_ref[s, 0:1] * (e_ref[s, :] - means[s, 0:1] - hat * means[s, 1:2])
    column_halves(idx[0], rows[...].T, mine_ref, send_ref, full)


def place_kernel(idx, mine_ref, got_ref, o_ref):
    half = mine_ref.shape[1]
    o_ref[:, at(idx[0], half, 128)] = mine_ref[...]
    o_ref[:, at(1 - idx[0], half, 128)] = got_ref[...]


def place_add_kernel(idx, mine_ref, got_ref, base_ref, o_ref):
    half = mine_ref.shape[1]
    mine, other = at(idx[0], half, 128), at(1 - idx[0], half, 128)
    o_ref[:, mine] = base_ref[:, mine] + mine_ref[...]
    o_ref[:, other] = base_ref[:, other] + got_ref[...]


TAIL = INNER // 2


def tap_columns(b):
    return ((D + b * INNER, INNER), (D + (2 + b) * INNER, INNER), (D + 4 * INNER + b * TAIL, TAIL))


def pair_columns(own_ref, got_ref, keep_ref, send_ref, mine, other):
    to = 0
    for (m, count), (o, _n) in zip(mine, other):
        for r in chunks(own_ref.shape[0], 32):
            keep_ref[r, to : to + count] = own_ref[r, m : m + count] + got_ref[r, m : m + count].astype(f32)
            send_ref[r, to : to + count] = (
                own_ref[r, o : o + count] + got_ref[r, o : o + count].astype(f32)
            ).astype(bf16)
        to += count


def early_kernel(idx, own_ref, got_ref, keep_last, send_last, keep_taps, send_taps):
    for b in range(2):

        @pl.when(idx[2] == b)
        def _():
            pair_columns(own_ref, got_ref, keep_last, send_last, [(b * INNER, INNER)], [((1 - b) * INNER, INNER)])
            pair_columns(own_ref, got_ref, keep_taps, send_taps, tap_columns(b), tap_columns(1 - b))


def pair_kernel(idx, own_ref, got_ref, keep_ref, send_ref):
    for b in range(2):

        @pl.when(idx[2] == b)
        def _():
            pair_columns(own_ref, got_ref, keep_ref, send_ref, [(b * INNER, INNER)], [((1 - b) * INNER, INNER)])


def long_kernel(H, idx, keep_f, got_f, keep_l, got_l, part_ref, *send_refs):
    h = idx[3]
    for d, ref in enumerate((part_ref, *send_refs)):
        to = (h - d + H) % H
        for q, (keep, got) in enumerate(((keep_f, got_f), (keep_l, got_l))):

            @pl.when(to == q + 1)
            def _():
                ref[...] = (keep[...] + got[...].astype(f32)).astype(ref.dtype)

        @pl.when((to != 1) & (to != 2))
        def _():
            ref[...] = jnp.zeros_like(ref)


def taps_kernel(idx, keep_ref, got_ref, sum_ref, send_ref):
    for r in chunks(keep_ref.shape[0], 32):
        sum_ref[r, :] = keep_ref[r, :] + got_ref[r, :].astype(f32)

    @pl.when(idx[3] % 2 == 0)
    def _():
        send_ref[...] = sum_ref[:, INNER:].astype(bf16)

    @pl.when(idx[3] % 2 == 1)
    def _():
        send_ref[:, :INNER] = sum_ref[:, :INNER].astype(bf16)
        send_ref[:, INNER:] = jnp.zeros_like(send_ref[:, INNER:])


def taps_next_kernel(idx, sum_ref, got_ref, part_ref, send_ref):
    @pl.when(idx[3] % 2 == 0)
    def _():
        part_ref[:, :INNER] = sum_ref[:, :INNER] + got_ref[:, :INNER].astype(f32)
        part_ref[:, INNER:] = jnp.zeros_like(part_ref[:, INNER:])

    @pl.when(idx[3] % 2 == 1)
    def _():
        part_ref[...] = sum_ref[:, INNER:] + got_ref[...].astype(f32)

    send_ref[...] = part_ref[...].astype(bf16)


def own_kernel(idx, first_ref, taps_ref, last_ref, unit_ref):
    h, b = idx[3], idx[2]
    unit_ref[:, INNER:] = jnp.zeros_like(unit_ref[:, INNER:])
    for i in range(2):

        @pl.when((h == 0) & (b == i))
        def _():
            unit_ref[:, :INNER] = taps_ref[i]

        @pl.when((h == 1) & (b == i))
        def _():
            unit_ref[:, :INNER] = first_ref[:, i * INNER : (i + 1) * INNER]

        @pl.when((h == 2) & (b == i))
        def _():
            unit_ref[:, :INNER] = last_ref[:, i * INNER : (i + 1) * INNER]

        @pl.when((h == 3) & (b == i))
        def _():
            unit_ref[:, :INNER] = taps_ref[2 + i]
            unit_ref[:, INNER:] = taps_ref[4, :, i * TAIL : (i + 1) * TAIL]

    @pl.when(h > 3)
    def _():
        unit_ref[...] = jnp.zeros_like(unit_ref)


def finish_kernel(H, idx, old_ref, part_long, part_taps, *refs):
    got_long, got_taps = refs[: H - 1], refs[H - 1 : H]
    sum_ref, new_ref, cross_ref = refs[H:]
    h = idx[3]
    long = (h == 1) | (h == 2)

    @pl.when(long)
    def _():
        v = part_long[...]
        for got in got_long:
            v = v + got[...].astype(f32)
        sum_ref[:, :INNER] = v.astype(bf16)
        sum_ref[:, INNER:] = jnp.zeros_like(sum_ref[:, INNER:])
        new_ref[:, :INNER] = (muon_keep * old_ref[:, :INNER] + v).astype(bf16)
        new_ref[:, INNER:] = jnp.zeros_like(new_ref[:, INNER:])

    @pl.when(jnp.logical_not(long))
    def _():
        v = part_taps[...]
        for got in got_taps:
            v = v + got[...].astype(f32)
        sum_ref[...] = v.astype(bf16)
        new_ref[...] = (muon_keep * old_ref[...] + v).astype(bf16)

    @pl.when(h == 3)
    def _():
        cross_ref[:, :TAIL] = new_ref[:, INNER:]
        cross_ref[:, TAIL:] = new_ref[:, INNER:]

    @pl.when(h != 3)
    def _():
        cross_ref[...] = new_ref[:, :INNER]


def block_kernel(idx, new_ref, got_ref, o_ref):
    h, b = idx[3], idx[2]
    long = (h == 1) | (h == 2)
    for i in range(2):

        @pl.when(long & (b == i))
        def _():
            o_ref[:, i * INNER : (i + 1) * INNER] = new_ref[:, :INNER]
            o_ref[:, (1 - i) * INNER : (2 - i) * INNER] = got_ref[...]

        @pl.when(jnp.logical_not(long) & (b == i))
        def _():
            o_ref[:, :INNER] = new_ref[:, :INNER]
            o_ref[:, INNER + i * TAIL : INNER + (i + 1) * TAIL] = new_ref[:, INNER:]
            o_ref[:, INNER + (1 - i) * TAIL : INNER + (2 - i) * TAIL] = got_ref[:, :TAIL]


def sweep(X, Xh, Xl, A, Bh, Rh, width, low, last, carry):
    scale, squares = carry
    n = X.shape[0]
    alpha = squares * scale * scale * (1.0 / n)
    outer = scale * scale
    tile = n // 2
    rest = (coef_second + 2.0 * coef_third * alpha) * 1.0
    keep = (coef_first + coef_second * alpha + coef_third * alpha * alpha) * scale
    if low:
        Bl = mul(Xh[:, :width], Xl[:, :width], NT)
        A[...] = Bl + Bl.T
    for i in range(0, n, tile):
        r = slice(i, i + tile)
        a = mul(Xh[r, :width], Xh[:, :width], NT)
        if low:
            a = a + A[r, :]
        row = lax.broadcasted_iota(jnp.int32, (tile, n), 0) + i
        col = lax.broadcasted_iota(jnp.int32, (tile, n), 1)
        a = a * outer - jnp.where(row == col, alpha, 0.0)
        A[r, :] = a
        Bh[r, :] = a.astype(bf16)
    for i in range(0, n, tile):
        r = slice(i, i + tile)
        Rh[r, :] = (rest * A[r, :] + coef_third * mul(Bh[r, :], Bh[...], NN)).astype(bf16)
    total = jnp.zeros((8, 128), f32)
    for i in range(0, width, 256):
        c = slice(i, min(i + 256, width))
        v = keep * X[:, c] + scale * mul(Rh[...], Xh[:, c], NN)
        X[:, c] = v
        Xh[:, c] = v.astype(bf16)
        if last is not None:
            Xl[:, c] = (v - Xh[:, c].astype(f32)).astype(bf16)
        for q in range(0, c.stop - c.start, 128):
            w = v[:, q : q + 128]
            total = total + jnp.sum((w * w).reshape(n // 8, 8, 128), axis=0)
    return jnp.float32(1.0), jnp.sum(total)


def ortho_kernel(idx, own_ref, sib_ref, opp_ref, diag_ref, mine_ref, theirs_ref, X, Xh, Xl, A, Bh, Rh):
    n, C = X.shape
    k, y, h = idx[0], idx[1], idx[3]
    loc = own_ref.shape[0]
    long = (h == 1) | (h == 2)
    fifth = (h == 3) & (k == 1)
    blocks = (
        (2 * y + k, own_ref),
        (2 * y + 1 - k, sib_ref),
        (2 * (1 - y) + k, opp_ref),
        (2 * (1 - y) + 1 - k, diag_ref),
    )

    def load(first, count):
        total = jnp.zeros((8, count), f32)
        for place, ref in blocks:
            base = pl.multiple_of(place * loc, 32)
            for i in range(0, loc, 32):
                low = ref[i : i + 32, first : first + count]
                v = low.astype(f32)
                Xh[pl.ds(base + i, 32), :count] = low
                X[pl.ds(base + i, 32), :count] = v
                total = total + jnp.sum((v * v).reshape(4, 8, count), axis=0)
        squares = jnp.sum(total)
        return 1.0 / (jnp.sqrt(squares) + 1e-07), squares

    @pl.when(long)
    def _():
        carry = load(0, C)
        lax.fori_loop(0, 5, lambda i, c: sweep(X, Xh, Xl, A, Bh, Rh, C, False, None, c), carry)

    def taps(first):
        carry = load(first, INNER)
        carry = lax.fori_loop(0, 2, lambda i, c: sweep(X, Xh, Xl, A, Bh, Rh, INNER, False, True, c), carry)
        lax.fori_loop(0, 3, lambda i, c: sweep(X, Xh, Xl, A, Bh, Rh, INNER, True, True, c), carry)

    @pl.when(jnp.logical_not(long) & jnp.logical_not(fifth))
    def _():
        taps(0)

    @pl.when(fifth)
    def _():
        taps(INNER)

    mine_ref[...] = X[at(2 * y + k, loc), :].astype(bf16)
    theirs_ref[...] = X[at(2 * y + 1 - k, loc), :INNER].astype(bf16)


def step_kernel(idx, mine_ref, got_ref, o_ref):
    h, b, k = idx[3], idx[2], idx[0]

    @pl.when((h == 0) | ((h == 3) & (k == 0)))
    def _():
        o_ref[:, :INNER] = mine_ref[:, :INNER]

    @pl.when((h == 3) & (k == 1))
    def _():
        o_ref[:, :INNER] = got_ref[...]

    for i in range(2):

        @pl.when(((h == 1) | (h == 2)) & (b == i))
        def _():
            o_ref[:, :INNER] = mine_ref[:, i * INNER : (i + 1) * INNER]

        @pl.when((h == 3) & (k == 0) & (b == i))
        def _():
            o_ref[:, INNER:] = got_ref[:, i * TAIL : (i + 1) * TAIL]

        @pl.when((h == 3) & (k == 1) & (b == i))
        def _():
            o_ref[:, INNER:] = mine_ref[:, i * TAIL : (i + 1) * TAIL]

    @pl.when(h != 3)
    def _():
        o_ref[:, INNER:] = jnp.zeros_like(o_ref[:, INNER:])

    @pl.when(h > 3)
    def _():
        o_ref[:, :INNER] = jnp.zeros_like(o_ref[:, :INNER])


def join_kernel(idx, own_ref, got_ref, o_ref):
    h = idx[3]
    for q in range(2):

        @pl.when(h // 2 % 2 == q)
        def _():
            o_ref[:, q * INNER : (q + 1) * INNER] = own_ref[:, :INNER]
            o_ref[:, (1 - q) * INNER : (2 - q) * INNER] = got_ref[:, :INNER]
            o_ref[:, 2 * INNER :] = (own_ref if q else got_ref)[:, INNER:]


def apply_kernel(
    keep, rate_long, rate_tap, idx, own_ref, x_ref, z_ref, zx_ref, first_ref, taps_ref, last_ref,
    of_ref, ot_ref, ol_ref,
):
    h, b = idx[3], idx[2]
    for odd in range(2):
        for i in range(2):

            @pl.when((h % 2 == odd) & (b == i))
            def _():
                even = (own_ref, x_ref) if odd == 0 else (z_ref, zx_ref)
                odds = (z_ref, zx_ref) if odd == 0 else (own_ref, x_ref)
                for r in chunks(first_ref.shape[0], 32):
                    for q in range(2):
                        e = even[q ^ i]
                        o = odds[q ^ i]
                        lanes = slice(q * INNER, (q + 1) * INNER)
                        tail = slice(q * TAIL, (q + 1) * TAIL)
                        of_ref[r, lanes] = keep * first_ref[r, lanes] + rate_long * o[r, :INNER].astype(f32)
                        ol_ref[r, lanes] = keep * last_ref[r, lanes] + rate_long * e[r, INNER : 2 * INNER].astype(f32)
                        ot_ref[q, r, :] = keep * taps_ref[q, r, :] + rate_tap * e[r, :INNER].astype(f32)
                        ot_ref[2 + q, r, :] = keep * taps_ref[2 + q, r, :] + rate_tap * o[
                            r, INNER : 2 * INNER
                        ].astype(f32)
                        ot_ref[4, r, tail] = keep * taps_ref[4, r, tail] + rate_tap * o[r, 2 * INNER :].astype(f32)


ROWS = 24


def vector_kernel(idx, two_ref, three_ref, one_ref, cot_ref, sq_ref, o_ref):
    y, c = idx[1], 2 * idx[1] + idx[0]
    o_ref[...] = jnp.zeros_like(o_ref)
    o_ref[pl.ds(y, 1), :] = one_ref[0:1, :]
    o_ref[pl.ds(2 + y, 1), :] = one_ref[1:2, :]
    two = two_ref[...].T
    three = three_ref[...].T
    wide = two_ref.shape[0]
    pieces = (two[2:3], two[0:1], two[1:2], three[2:3], three[0:1], three[1:2])
    for i, piece in enumerate(pieces):
        o_ref[pl.ds(4 + 6 * y + i, 1), :wide] = piece
    cot = cot_ref[...].T
    o_ref[pl.ds(16 + c, 1), : cot_ref.shape[0]] = cot[0:1]
    for i in range(3):
        o_ref[20 + i : 21 + i, :128] = sq_ref[i : i + 1, :]


def adam_kernel(v_ref, par_ref, mom_ref, sqr_ref, first_ref, second_ref, value_ref, root_ref, g):
    wide = INNER // 2
    g[0:4, :] = v_ref[0:4, :]
    for i in range(6):
        g[4 + i : 5 + i, :wide] = v_ref[4 + i : 5 + i, :wide]
        g[4 + i : 5 + i, wide:] = v_ref[10 + i : 11 + i, :wide]
    for i in range(2):
        g[10 + i : 11 + i, :wide] = v_ref[16 + 2 * i : 17 + 2 * i, :wide]
        g[10 + i : 11 + i, wide:] = v_ref[17 + 2 * i : 18 + 2 * i, :wide]
    per = INNER // 128
    for r in range(12):
        for q in range(per):
            at_row = slice(r * per + q, r * per + q + 1)
            grad = g[r : r + 1, q * 128 : (q + 1) * 128]
            par = par_ref[at_row, :]
            first = adam_first * mom_ref[at_row, :] + (1.0 - adam_first) * grad
            second = adam_second * sqr_ref[at_row, :] + (1.0 - adam_second) * grad * grad
            first_ref[at_row, :] = first
            second_ref[at_row, :] = second
            value_ref[at_row, :] = par - adam_rate * (
                (first / (1.0 - adam_first**STEP)) / (jnp.sqrt(second / (1.0 - adam_second**STEP)) + adam_eps)
                + decay_rate * par
            )
    count = v_ref[22:23, :128] * D
    root_ref[...] = jnp.zeros_like(root_ref)
    for i in range(2):
        root_ref[i : i + 1, :] = jnp.sqrt(v_ref[20 + i : 21 + i, :128] / count)


def after(value, *others):
    return lax.optimization_barrier((value, *others))[0]


def body(
    tokens,
    cotangent,
    lengths,
    valid_mask,
    weight_first,
    weight_dilated,
    weight_last,
    momentum_first,
    momentum_dilated,
    momentum_last,
    vector_params,
    vector_moment,
    vector_square,
):
    C = lax.axis_size("ch")
    S = lax.axis_size("seq")
    c = lax.axis_index("ch")
    s = lax.axis_index("seq")
    k = c % 2
    y = c // 2
    T = tokens.shape[0]
    half = T // 2
    loc = weight_first.shape[1]
    wide = 2 * loc
    col = D // C
    H = S // 2
    b = s % 2
    h = s // 2
    idx = jnp.stack([k, y, b, h, s, s * T + k * half]).astype(jnp.int32)

    sib = [(i, i ^ 1) for i in range(C)]
    opp = [(i, i ^ 2) for i in range(C)]
    xsw = [(i, i ^ 1) for i in range(S)]

    def swap_core(v):
        return lax.ppermute(v, "ch", sib)

    def swap_y(v):
        return lax.ppermute(v, "ch", opp)

    def swap_x(v):
        return lax.ppermute(v, "seq", xsw)

    def along_h(v, pairs):
        return lax.ppermute(v, "seq", [(2 * i + q, 2 * j + q) for i, j in pairs for q in range(2)])

    outer_pairs = []
    for i in range(S):
        for j in range(C):
            if j % 2 == 0 and i >= 1:
                outer_pairs.append((i * C + j, (i - 1) * C + (j ^ 1)))
            if j % 2 == 1 and i + 1 < S:
                outer_pairs.append((i * C + j, (i + 1) * C + (j ^ 1)))

    def swap_outer(v):
        return lax.ppermute(v, ("seq", "ch"), outer_pairs)

    w_first, w_taps, w_last = weight_first.T, jnp.swapaxes(weight_dilated, 1, 2), weight_last
    m_first, m_taps, m_last = momentum_first.T, jnp.swapaxes(momentum_dilated, 1, 2), momentum_last
    cot = cotangent.T
    valid = valid_mask.reshape(1, T)
    gain_shift = vector_params[: 2 * D].reshape(2, D)
    inner_rows = vector_params[2 * D : 2 * D + 6 * INNER].reshape(6, INNER)
    cols = lax.dynamic_slice_in_dim(inner_rows, y * wide, wide, 1).T
    bias_three = vector_params[2 * D + 6 * INNER :].reshape(1, D)

    low_first, cot_all, cot_other, cot_sums = call(
        prep_kernel,
        [((loc, D), bf16), ((col, T), bf16), ((col, half), bf16), ((col, 128), f32)],
        [idx],
        [w_first, cot],
    )
    got_first = swap_core(low_first)
    cot_opp = swap_y(cot_all)
    cot_sib = swap_core(cot_other)

    rows = 128
    steps = half // rows
    hid_one, hat_one, slope_one, scale_one = pl.pallas_call(
        input_kernel,
        out_shape=[
            jax.ShapeDtypeStruct((half, D), bf16),
            jax.ShapeDtypeStruct((half, D), bf16),
            jax.ShapeDtypeStruct((half, D), bf16),
            jax.ShapeDtypeStruct((half, 128), f32),
        ],
        grid_spec=pltpu.PrefetchScalarGridSpec(
            num_scalar_prefetch=1,
            grid=(steps,),
            in_specs=[
                pl.BlockSpec((rows, D), lambda i, idx: (idx[0] * steps + i, 0)),
                pl.BlockSpec((2, D), lambda i, idx: (0, 0)),
            ],
            out_specs=[
                pl.BlockSpec((rows, D), lambda i, idx: (i, 0)),
                pl.BlockSpec((rows, D), lambda i, idx: (i, 0)),
                pl.BlockSpec((rows, D), lambda i, idx: (i, 0)),
                pl.BlockSpec((rows, 128), lambda i, idx: (i, 0)),
            ],
        ),
        compiler_params=pltpu.CompilerParams(vmem_limit_bytes=16 * MIB),
        cost_estimate=pl.CostEstimate(flops=5000000000, bytes_accessed=1000, transcendentals=0),
    )(idx, tokens, gain_shift)

    (low_rest,) = call(
        rest_kernel, [((loc, D + KERNEL_TAPS * INNER), bf16)], [], [after(w_last, hid_one), w_taps]
    )
    got_rest = swap_core(low_rest)

    full_first, inner_one, st_two = call(
        first_kernel,
        [((wide, D), bf16), ((wide, half), f32), ((8, half), f32)],
        [idx],
        [low_first, got_first, hid_one, cols],
    )
    st_two_got = after(swap_y(st_two), cot_sib, cot_opp)
    (cot_diag,) = call(other_half_kernel, [((col, half), bf16)], [idx], [cot_opp])
    cot_diag = swap_core(cot_diag)
    slab = ((wide, REACH), bf16)
    own_in, own_out, hat_two, slope_two = call(
        second_kernel,
        [slab, slab, ((wide, half), f32), ((wide, half), f32)],
        [idx],
        [inner_one, st_two, st_two_got, cols, valid],
        scratch=[((wide, half), bf16)],
    )
    opp_in, opp_out = swap_y(own_in), swap_y(own_out)
    sib_in, seq_out = swap_core(own_in), swap_outer(own_out)
    sib_opp_in, seq_opp_out = swap_core(opp_in), swap_y(seq_out)
    ext, inner_two, st_three, full_last, full_taps, masks = call(
        functools.partial(conv_kernel, S * T),
        [
            ((INNER, half + 2 * REACH), bf16),
            ((wide, half), f32),
            ((8, half), f32),
            ((wide, D), bf16),
            ((wide, KERNEL_TAPS * INNER), bf16),
            ((8, half), f32),
        ],
        [idx, lengths],
        [
            own_in, own_out, opp_in, opp_out, sib_in, sib_opp_in, seq_out, seq_opp_out,
            low_rest, got_rest, cols,
        ],
        scratch=[((KERNEL_TAPS * INNER, half), bf16)],
    )
    st_three_got = swap_y(st_three)
    gw, g_three = call(
        cotangent_kernel,
        [((D, half), bf16), ((wide, half), f32)],
        [idx],
        [full_last, cot_all, cot_sib, cot_opp, cot_diag],
    )
    hid_three, e_three, hat_three, part_three = call(
        third_kernel,
        [((wide, half), bf16), ((wide, half), f32), ((wide, half), f32), ((8, half), f32)],
        [],
        [inner_two, st_three, st_three_got, cols, g_three],
    )
    part_three_got = swap_y(part_three)
    dz_two, slab_in, slab_out, sums_three = call(
        third_back_kernel,
        [((wide, half), bf16), ((wide, REACH), bf16), ((wide, REACH), bf16), ((wide, 128), f32)],
        [idx],
        [e_three, hat_three, part_three, part_three_got, cols],
    )
    got_in, got_out = swap_core(slab_in), swap_outer(slab_out)
    back_own, back_send = call(
        conv_back_kernel,
        [((wide, half), f32), ((wide, half), bf16)],
        [idx],
        [dz_two, got_in, got_out, masks, full_taps],
        scratch=[((wide, half + 2 * REACH), bf16), ((INNER, half), f32)],
    )
    back_got = swap_y(back_send)
    early_size = D + KERNEL_TAPS * INNER
    early_own, early_send = call(
        grads_kernel,
        [((loc, early_size), f32), ((loc, early_size), bf16)],
        [idx],
        [after(dz_two, back_send), ext, masks, hid_three, gw],
        scratch=[((wide, early_size), f32)],
        limit=32,
    )
    early_got = swap_core(early_send)
    unit, unit_low = ((loc, INNER), f32), ((loc, INNER), bf16)
    last_keep, last_send, taps_keep, taps_send = call(
        early_kernel,
        [unit, unit_low, ((loc, 2 * INNER + TAIL), f32), ((loc, 2 * INNER + TAIL), bf16)],
        [idx],
        [early_own, early_got],
    )
    last_got, taps_got = swap_x(last_send), swap_x(taps_send)
    e_two, part_two = call(
        second_back_kernel,
        [((wide, half), f32), ((8, half), f32)],
        [],
        [after(back_own, taps_send), back_got, slope_two, hat_two, cols],
    )
    half_out = [((half, HALF_D), f32), ((half, HALF_D), bf16)]
    branch_own, branch_send = call(
        halves_kernel, half_out, [idx], [after(hid_three, back_send), full_last], scratch=[((half, D), f32)]
    )
    part_two_got = after(swap_y(part_two), branch_send)
    branch_got = swap_y(after(branch_send, part_two_got))
    dz_one, first_own, first_send, sums_two = call(
        first_back_kernel,
        [((wide, half), bf16), ((loc, D), f32), ((loc, D), bf16), ((wide, 128), f32)],
        [idx],
        [e_two, hat_two, part_two, part_two_got, st_two, st_two_got, cols, hid_one],
        scratch=[((wide, D), f32)],
    )
    first_got = swap_core(first_send)
    first_keep, first_low = call(pair_kernel, [unit, unit_low], [idx], [first_own, first_got])
    first_got = swap_x(first_low)

    span = H
    while span > 4:
        span //= 2
        fold = [(i + span, i) for i in range(span)]

        def folded(keep, got):
            total = keep + got.astype(f32)
            return total + along_h(total.astype(bf16), fold).astype(f32), jnp.zeros_like(got)

        first_keep, first_got = folded(first_keep, first_got)
        last_keep, last_got = folded(last_keep, last_got)
        taps_keep, taps_got = folded(taps_keep, taps_got)
    line = 4

    def to_owners(sends, owners):
        return [
            along_h(v, [((j + d + 1) % line, j) for j in owners]) for d, v in enumerate(sends)
        ]

    size_taps = (loc, INNER + TAIL)
    sum_taps, send_taps = call(
        taps_kernel, [((loc, 2 * INNER + TAIL), f32), (size_taps, bf16)], [idx], [taps_keep, taps_got]
    )
    got_taps = along_h(send_taps, [(i, i ^ 1) for i in range(line)])
    part_long, *sends = call(
        functools.partial(long_kernel, line),
        [unit] + [unit_low] * (line - 1),
        [idx],
        [after(first_keep, send_taps), first_got, last_keep, last_got],
    )
    got_long = to_owners(sends, (1, 2))
    part_taps, send_taps = call(
        taps_next_kernel, [(size_taps, f32), (size_taps, bf16)], [idx], [sum_taps, got_taps]
    )
    got_taps = along_h(send_taps, [(2, 0), (1, 3)])
    back_own, back_send = call(
        halves_kernel, half_out, [idx], [after(dz_one, first_low), full_first], scratch=[((half, D), f32)]
    )
    back_got = swap_y(back_send)
    own_tokens = lax.dynamic_slice(tokens, (k * half, y * HALF_D), (half, HALF_D))
    out_mine, out_send, squares = call(
        output_kernel,
        [((col, half), f32), ((col, half), f32), ((8, 128), f32)],
        [idx],
        [branch_own, branch_got, own_tokens, bias_three, valid],
        scratch=[((HALF_D, half), f32)],
    )
    e_one, part_one, sums_one = call(
        token_kernel,
        [((half, HALF_D), f32), ((half, 128), f32), ((8, HALF_D), f32)],
        [idx],
        [back_own, back_got, slope_one, hat_one, gain_shift],
    )
    (part_one,) = call(flip_kernel, [((8, half), f32)], [], [part_one])
    (vector,) = call(
        vector_kernel, [((ROWS, INNER), f32)], [idx], [sums_two, sums_three, sums_one, cot_sums, squares]
    )
    (old_unit,) = call(own_kernel, [(size_taps, f32)], [idx], [m_first, m_taps, m_last])
    sum_unit, new_unit, cross = call(
        functools.partial(finish_kernel, line),
        [(size_taps, bf16), (size_taps, bf16), unit_low],
        [idx],
        [old_unit, part_long, part_taps, *got_long, got_taps],
    )
    cross_got = swap_x(after(cross, squares, sums_one))
    (block,) = call(block_kernel, [((loc, D), bf16)], [idx], [new_unit, cross_got])
    sum_far = along_h(sum_unit, [(i, i ^ 2) for i in range(4)])
    block_sib, block_opp = swap_core(block), swap_y(block)
    block_diag = swap_core(after(block_opp, sum_far))

    def joined_with(unit, got):
        return call(join_kernel, [((loc, 2 * INNER + TAIL), bf16)], [idx], [unit, got])[0]

    def next_along_z(joined):
        return along_h(joined, [(i, i ^ 1) for i in range(4)])

    def spread(parts):
        span = 4
        while span < H:
            pairs = [(i, i + span) for i in range(span)]
            parts = [jnp.where((h >= span) & (h < 2 * span), along_h(v, pairs), v) for v in parts]
            span *= 2
        return parts

    def apply(keep, rate_long, rate_tap, parts, first, taps, last):
        return call(
            functools.partial(apply_kernel, keep, rate_long, rate_tap),
            [((loc, D), f32), ((KERNEL_TAPS, loc, INNER), f32), ((loc, D), f32)],
            [idx],
            [*parts, first, taps, last],
            limit=32,
        )

    joined = joined_with(sum_unit, sum_far)
    mine, theirs = call(
        ortho_kernel,
        [((loc, D), bf16), ((loc, INNER), bf16)],
        [idx],
        [after(block, joined), block_sib, block_opp, block_diag],
        scratch=[
            ((INNER, D), f32),
            ((INNER, D), bf16),
            ((INNER, INNER), bf16),
            ((INNER, INNER), f32),
            ((INNER, INNER), bf16),
            ((INNER, INNER), bf16),
        ],
        limit=32,
        flops=14 * 10**9,
    )
    joined_x = swap_x(joined)
    other = next_along_z(joined)
    theirs_got = swap_core(theirs)
    (step_unit,) = call(step_kernel, [(size_taps, bf16)], [idx], [after(mine, joined_x, other), theirs_got])
    other_x = swap_x(after(other, step_unit))
    mom_parts = spread([joined, joined_x, other, other_x])

    vector = after(vector, step_unit)
    vector = vector + swap_core(vector)
    vector = vector + swap_y(vector)
    vector = vector + swap_x(vector)
    step_far = along_h(step_unit, [(i, i ^ 2) for i in range(4)])
    joined = joined_with(after(step_unit, vector, other_x), step_far)
    joined_x = swap_x(joined)
    other = after(next_along_z(joined), joined_x)

    grad_mine, grad_send = call(
        token_back_kernel,
        [((col, half), f32), ((col, half), f32)],
        [idx],
        [after(e_one, joined), hat_one, scale_one, part_one, swap_y(part_one)],
        scratch=[((half, HALF_D), f32), ((HALF_D, half), f32)],
    )
    grad_got, out_got = swap_core(grad_send), swap_core(out_send)
    other, vector, grad_got, out_got = lax.optimization_barrier((other, vector, grad_got, out_got))
    other_x = swap_x(other)
    bit = 2
    while bit < S:
        vector = vector + lax.ppermute(vector, "seq", [(i, i ^ bit) for i in range(S)])
        bit *= 2
    (block_output,) = call(place_kernel, [((col, T), f32)], [idx], [out_mine, out_got])
    (tokens_grad,) = call(place_add_kernel, [((col, T), f32)], [idx], [grad_mine, grad_got, cot])
    flat = (VECTOR // 128, 128)
    vector_first, vector_second, vector_values, root = call(
        adam_kernel,
        [(flat, f32)] * 3 + [((8, 128), f32)],
        [],
        [vector, vector_params.reshape(flat), vector_moment.reshape(flat), vector_square.reshape(flat)],
        scratch=[((12, INNER), f32)],
    )
    vector_first, vector_second, vector_values = (
        v.reshape(VECTOR) for v in (vector_first, vector_second, vector_values)
    )
    root_means = root[:2, 0]
    new_first, new_taps, new_last = apply(
        muon_keep, 1.0, 1.0, [after(mom_parts[0], other), *mom_parts[1:]], m_first, m_taps, m_last
    )
    keep_weight = 1.0 - muon_rate * decay_rate
    rate = muon_rate * muon_scale
    out_first, out_taps, out_last = apply(
        keep_weight,
        -rate * math.sqrt(D),
        -rate * math.sqrt(INNER),
        spread([joined, joined_x, other, other_x]),
        w_first,
        w_taps,
        w_last,
    )
    return (
        block_output.T,
        tokens_grad.T,
        out_first.T,
        jnp.swapaxes(out_taps, 1, 2),
        out_last,
        new_first.T,
        jnp.swapaxes(new_taps, 1, 2),
        new_last,
        vector_first,
        vector_second,
        vector_values,
        root_means,
    )


def solution(mesh):
    placed = (
        P("seq", None),
        P("seq", "ch"),
        P(),
        P("seq"),
        P(None, "ch"),
        P(None, None, "ch"),
        P("ch", None),
        P(None, "ch"),
        P(None, None, "ch"),
        P("ch", None),
        P(),
        P(),
        P(),
    )
    return jax.shard_map(
        body,
        mesh=mesh,
        in_specs=placed,
        out_specs=(
            P("seq", "ch"),
            P("seq", "ch"),
            P(None, "ch"),
            P(None, None, "ch"),
            P("ch", None),
            P(None, "ch"),
            P(None, None, "ch"),
            P("ch", None),
            P(),
            P(),
            P(),
            P(),
        ),
        check_vma=False,
    )
```

```python
import functools
import math

import jax
import jax.numpy as jnp
from jax import lax
from jax.experimental import pallas as pl
from jax.experimental.pallas import tpu as pltpu
from jax.sharding import PartitionSpec as P

D = 1280
INNER = 640
KERNEL_TAPS = 5
DILATION_SPAN = 128
STEP = 10

norm_eps = 1e-05
coef_first = 3.4445
coef_second = -4.775
coef_third = 2.0315
adam_rate = 0.4
adam_first = 0.9
adam_second = 0.999
adam_eps = 1e-08
decay_rate = 0.01
muon_rate = 0.1
muon_keep = 0.95
muon_scale = 0.2
REACH = KERNEL_TAPS // 2 * DILATION_SPAN
VECTOR = 3 * D + 6 * INNER
HALF_D = D // 2
MIB = 1024 * 1024

f32 = jnp.float32
bf16 = jnp.bfloat16
NN = (((1,), (0,)), ((), ()))
NT = (((1,), (1,)), ((), ()))
TN = (((0,), (0,)), ((), ()))


def mul(a, b, dims):
    return lax.dot_general(a, b, dims, preferred_element_type=f32)


def erf_parts(v):
    a = jnp.abs(v) * math.sqrt(0.5)
    t = pl.reciprocal(1.0 + 0.3275911 * a)
    e = jnp.exp(-a * a)
    p = t * (0.254829592 + t * (-0.284496736 + t * (1.421413741 + t * (-1.453152027 + t * 1.061405429))))
    tail = 0.5 * p * e
    return jnp.where(v >= 0, 1.0 - tail, tail), e


def gelu_pair(v):
    cdf, e = erf_parts(v)
    return v * cdf, cdf + v * e * (1.0 / math.sqrt(2.0 * math.pi))


VMEM = pl.BlockSpec(memory_space=pltpu.VMEM)
SMEM = pl.BlockSpec(memory_space=pltpu.SMEM)


def call(kernel, outs, scalars, arrays, scratch=(), limit=16, flops=1000):
    shapes = [jax.ShapeDtypeStruct(shape, dtype) for shape, dtype in outs]
    return pl.pallas_call(
        kernel,
        out_shape=shapes,
        in_specs=[SMEM] * len(scalars) + [VMEM] * len(arrays),
        out_specs=[VMEM] * len(outs),
        scratch_shapes=[pltpu.VMEM(shape, dtype) for shape, dtype in scratch],
        compiler_params=pltpu.CompilerParams(vmem_limit_bytes=limit * MIB),
        cost_estimate=pl.CostEstimate(flops=flops, bytes_accessed=1000, transcendentals=0),
    )(*scalars, *arrays)


def chunks(count, step):
    return [pl.ds(i, step) for i in range(0, count, step)]


def at(index, count, step=32):
    return pl.ds(pl.multiple_of(index * count, step), count)


def prep_kernel(idx, w_ref, cot_ref, wo_ref, all_ref, other_ref, sums_ref):
    half = other_ref.shape[1]
    for r in chunks(cot_ref.shape[0], 32):
        v = cot_ref[r, :]
        all_ref[r, :] = v.astype(bf16)
        other_ref[r, :] = cot_ref[r, at(1 - idx[0], half, 128)].astype(bf16)
        sums_ref[r, :] = jnp.broadcast_to(jnp.sum(v, axis=1, keepdims=True), (32, 128))
    for r in chunks(w_ref.shape[0], 32):
        wo_ref[r, :] = w_ref[r, :].astype(bf16)


def rest_kernel(last_ref, taps_ref, o_ref):
    for r in chunks(last_ref.shape[0], 32):
        o_ref[r, :D] = last_ref[r, :].astype(bf16)
        for j in range(KERNEL_TAPS):
            o_ref[r, D + j * INNER : D + (j + 1) * INNER] = taps_ref[j, r, :].astype(bf16)


def input_kernel(idx, tok_ref, gs_ref, hid_ref, hat_ref, slope_ref, scale_ref):
    for r in chunks(tok_ref.shape[0], 16):
        v = tok_ref[r, :]
        center = jnp.sum(v, axis=1, keepdims=True) * (1.0 / D)
        square = jnp.sum(v * v, axis=1, keepdims=True) * (1.0 / D)
        scale = lax.rsqrt(square - center * center + norm_eps)
        hat = (v - center) * scale
        hid, slope = gelu_pair(hat * gs_ref[0:1, :] + gs_ref[1:2, :])
        hid_ref[r, :] = hid.astype(bf16)
        hat_ref[r, :] = hat.astype(bf16)
        slope_ref[r, :] = slope.astype(bf16)
        scale_ref[r, :] = jnp.broadcast_to(scale, (16, 128))


def put_stats(ref, parts):
    for i, part in enumerate(parts):
        ref[i : i + 1, :] = part


def first_kernel(idx, own_ref, got_ref, hid_ref, cols_ref, w_ref, inner_ref, st_ref):
    k = idx[0]
    loc = own_ref.shape[0]
    w_ref[at(k, loc), :] = own_ref[...]
    w_ref[at(1 - k, loc), :] = got_ref[...]
    v = mul(w_ref[...], hid_ref[...], NT) + cols_ref[:, 0:1]
    inner_ref[...] = v
    put_stats(st_ref, (jnp.sum(v, axis=0, keepdims=True), jnp.sum(v * v, axis=0, keepdims=True)))


def center_scale(st_ref, got_ref):
    center = (st_ref[0:1, :] + got_ref[0:1, :]) * (1.0 / INNER)
    square = (st_ref[1:2, :] + got_ref[1:2, :]) * (1.0 / INNER)
    return center, lax.rsqrt(square - center * center + norm_eps)


def second_kernel(
    idx, inner_ref, st_ref, got_ref, cols_ref, valid_ref, in_ref, out_ref, hat_ref, slope_ref, hid_ref
):
    center, scale = center_scale(st_ref, got_ref)
    valid = valid_ref[:, at(idx[0], hid_ref.shape[1], 128)].astype(f32)
    for r in chunks(inner_ref.shape[0], 32):
        hat = (inner_ref[r, :] - center) * scale
        hid, slope = gelu_pair(hat * cols_ref[r, 1:2] + cols_ref[r, 2:3])
        hid_ref[r, :] = (hid * valid).astype(bf16)
        hat_ref[r, :] = hat
        slope_ref[r, :] = slope * valid
    slabs_of(idx[0], hid_ref, slice(None), in_ref, out_ref)


def slabs_of(k, v_ref, row, in_ref, out_ref):
    half = v_ref.shape[1]
    rows = v_ref.shape[0]
    in_ref[row, :] = v_ref[:, at(1 - k, half - REACH, 128)]
    out_ref[row, :] = v_ref[:, at(k, half - REACH, 128)]


def fill_reach(k, ext_ref, in_ref, out_ref, half):
    @pl.when(k == 0)
    def _():
        ext_ref[:, :REACH] = out_ref[...]
        ext_ref[:, REACH + half :] = in_ref[...]

    @pl.when(k == 1)
    def _():
        ext_ref[:, :REACH] = in_ref[...]
        ext_ref[:, REACH + half :] = out_ref[...]


def conv_kernel(
    total, idx, lengths, own_in, own_out, opp_in, opp_out, sib_in, sib_opp_in, seq_out, seq_opp_out,
    wo_ref, wg_ref, cols_ref, ext_ref, inner_ref, st_ref, last_ref, taps_ref, mask_ref, stack,
):
    k, y = idx[0], idx[1]
    wide, reach = own_in.shape
    half = 2 * reach
    loc = wo_ref.shape[0]
    for q in range(2):
        @pl.when(k == q)
        def _():
            for place, (mine, other) in enumerate(
                ((seq_out, seq_opp_out), (own_out, opp_out), (own_in, opp_in), (sib_in, sib_opp_in))
            ):
                place = 3 - place if q else place
                lanes = slice(place * reach, (place + 1) * reach)
                ext_ref[at(y, wide), lanes] = mine[...]
                ext_ref[at(1 - y, wide), lanes] = other[...]

    last_ref[at(k, loc), :] = wo_ref[:, :D]
    last_ref[at(1 - k, loc), :] = wg_ref[:, :D]
    taps_ref[at(k, loc), :] = wo_ref[:, D:]
    taps_ref[at(1 - k, loc), :] = wg_ref[:, D:]
    positions = idx[5] - REACH + lax.broadcasted_iota(jnp.int32, (1, half + 2 * REACH), 1)
    segment = jnp.zeros_like(positions)
    bound = jnp.int32(0)
    for i in range(lengths.shape[0]):
        bound = bound + lengths[i]
        segment = segment + (positions >= bound).astype(jnp.int32)
    segment = jnp.where((positions >= 0) & (positions < total), segment, -1)
    centre = segment[:, REACH : REACH + half]
    for j in range(KERNEL_TAPS):
        lanes = slice(j * DILATION_SPAN, j * DILATION_SPAN + half)
        mask = (segment[:, lanes] == centre).astype(f32)
        mask_ref[j : j + 1, :] = mask
        low = mask.astype(bf16)
        for i in range(0, INNER, 160):
            stack[j * INNER + i : j * INNER + i + 160, :] = ext_ref[i : i + 160, lanes] * low
    v = mul(taps_ref[...], stack[...], NN) + cols_ref[:, 3:4]
    inner_ref[...] = v
    put_stats(st_ref, (jnp.sum(v, axis=0, keepdims=True), jnp.sum(v * v, axis=0, keepdims=True)))


def cotangent_kernel(idx, last_ref, all_ref, sib_ref, opp_ref, diag_ref, gw_ref, g_ref):
    k, y = idx[0], idx[1]
    col, half = sib_ref.shape
    mine = at(k, half, 128)
    gw_ref[at(2 * y + k, col), :] = all_ref[:, mine]
    gw_ref[at(2 * y + 1 - k, col), :] = sib_ref[...]
    gw_ref[at(2 * (1 - y) + k, col), :] = opp_ref[:, mine]
    gw_ref[at(2 * (1 - y) + 1 - k, col), :] = diag_ref[...]
    g_ref[...] = mul(last_ref[...], gw_ref[...], NN)


def other_half_kernel(idx, all_ref, o_ref):
    o_ref[...] = all_ref[:, at(1 - idx[0], o_ref.shape[1], 128)]


def third_kernel(inner_ref, st_ref, got_ref, cols_ref, g_ref, hid_ref, e_ref, hat_ref, part_ref):
    center, scale = center_scale(st_ref, got_ref)
    plain = jnp.zeros_like(center)
    cross = jnp.zeros_like(center)
    for r in chunks(inner_ref.shape[0], 32):
        hat = (inner_ref[r, :] - center) * scale
        gain = cols_ref[r, 4:5]
        hid, slope = gelu_pair(hat * gain + cols_ref[r, 5:6])
        hid_ref[r, :] = hid.astype(bf16)
        hat_ref[r, :] = hat
        e = slope * g_ref[r, :]
        e_ref[r, :] = e
        eg = e * gain
        plain = plain + jnp.sum(eg, axis=0, keepdims=True)
        cross = cross + jnp.sum(eg * hat, axis=0, keepdims=True)
    put_stats(part_ref, (plain, cross, scale))


def norm_back(r, e_ref, hat_ref, part_ref, got_ref, scale, gain, sums_ref):
    plain = (part_ref[0:1, :] + got_ref[0:1, :]) * (1.0 / INNER)
    cross = (part_ref[1:2, :] + got_ref[1:2, :]) * (1.0 / INNER)
    e, hat = e_ref[r, :], hat_ref[r, :]
    grad = scale * (e * gain - plain - hat * cross)
    sums_ref[r, 0:1] = jnp.sum(e * hat, axis=1, keepdims=True)
    sums_ref[r, 1:2] = jnp.sum(e, axis=1, keepdims=True)
    sums_ref[r, 2:3] = jnp.sum(grad, axis=1, keepdims=True)
    return grad


def third_back_kernel(idx, e_ref, hat_ref, part_ref, got_ref, cols_ref, dz_ref, in_ref, out_ref, sums_ref):
    for r in chunks(e_ref.shape[0], 32):
        grad = norm_back(r, e_ref, hat_ref, part_ref, got_ref, part_ref[2:3, :], cols_ref[r, 4:5], sums_ref)
        dz_ref[r, :] = grad.astype(bf16)
    slabs_of(idx[0], dz_ref, slice(None), in_ref, out_ref)


def split_rows(k, full, own_ref, send_ref, lanes):
    loc = own_ref.shape[0]
    own_ref[:, lanes] = full[at(k, loc), lanes]
    send_ref[:, lanes] = full[at(1 - k, loc), lanes].astype(bf16)


def grads_kernel(idx, dz_ref, ext_ref, mask_ref, hid_ref, gw_ref, own_ref, send_ref, full):
    k = idx[0]
    half = dz_ref.shape[1]
    full[:, :D] = mul(hid_ref[...], gw_ref[...], NT)
    split_rows(k, full, own_ref, send_ref, slice(0, D))
    for j in range(KERNEL_TAPS):
        masked = dz_ref[...] * mask_ref[j : j + 1, :].astype(bf16)
        moved = ext_ref[:, j * DILATION_SPAN : j * DILATION_SPAN + half]
        lanes = slice(D + j * INNER, D + (j + 1) * INNER)
        full[:, lanes] = mul(masked, moved, NT)
        split_rows(k, full, own_ref, send_ref, lanes)


def conv_back_kernel(idx, dz_ref, in_ref, out_ref, mask_ref, taps_ref, own_ref, send_ref, ext, full):
    k, y = idx[0], idx[1]
    wide, half = dz_ref.shape
    ext[:, REACH : REACH + half] = dz_ref[...]
    fill_reach(k, ext, in_ref, out_ref, half)
    total = None
    for j in range(KERNEL_TAPS):
        begin = REACH - (j - KERNEL_TAPS // 2) * DILATION_SPAN
        mask = mask_ref[KERNEL_TAPS - 1 - j : KERNEL_TAPS - j, :].astype(bf16)
        part = mul(taps_ref[:, j * INNER : (j + 1) * INNER], ext[:, begin : begin + half] * mask, TN)
        total = part if total is None else total + part
    full[...] = total
    own_ref[...] = full[at(y, wide), :]
    send_ref[...] = full[at(1 - y, wide), :].astype(bf16)


def second_back_kernel(own_ref, got_ref, slope_ref, hat_ref, cols_ref, e_ref, part_ref):
    plain = jnp.zeros((1, own_ref.shape[1]), f32)
    cross = jnp.zeros_like(plain)
    for r in chunks(own_ref.shape[0], 32):
        e = slope_ref[r, :] * (own_ref[r, :] + got_ref[r, :].astype(f32))
        e_ref[r, :] = e
        eg = e * cols_ref[r, 1:2]
        plain = plain + jnp.sum(eg, axis=0, keepdims=True)
        cross = cross + jnp.sum(eg * hat_ref[r, :], axis=0, keepdims=True)
    put_stats(part_ref, (plain, cross))


def first_back_kernel(
    idx, e_ref, hat_ref, part_ref, got_ref, st_ref, stg_ref, cols_ref, hid_ref,
    dz_ref, own_ref, send_ref, sums_ref, full,
):
    _, scale = center_scale(st_ref, stg_ref)
    for r in chunks(e_ref.shape[0], 32):
        grad = norm_back(r, e_ref, hat_ref, part_ref, got_ref, scale, cols_ref[r, 1:2], sums_ref)
        dz_ref[r, :] = grad.astype(bf16)
    full[...] = mul(dz_ref[...], hid_ref[...], NN)
    split_rows(idx[0], full, own_ref, send_ref, slice(0, D))


def halves_kernel(idx, z_ref, w_ref, own_ref, send_ref, full):
    y = idx[1]
    full[...] = mul(z_ref[...], w_ref[...], TN)
    for r in chunks(full.shape[0], 64):
        own_ref[r, :] = full[r, at(y, HALF_D, 128)]
        send_ref[r, :] = full[r, at(1 - y, HALF_D, 128)].astype(bf16)


def column_halves(k, flipped, mine_ref, send_ref, full):
    col = mine_ref.shape[0]
    full[...] = flipped
    mine_ref[...] = full[at(k, col), :]
    send_ref[...] = full[at(1 - k, col), :]


def output_kernel(idx, own_ref, got_ref, tok_ref, flat_ref, valid_ref, mine_ref, send_ref, sq_ref, full):
    k, y = idx[0], idx[1]
    half = own_ref.shape[0]
    per = HALF_D // 128
    first = (2 * D + 6 * INNER) // 128 + per * y
    bias = jnp.concatenate([flat_ref[pl.ds(first + q, 1), :] for q in range(per)], axis=1)
    branch = own_ref[...] + got_ref[...].astype(f32) + bias
    out = tok_ref[...] + branch
    valid = valid_ref[:, at(k, half, 128)].astype(f32)
    sq_ref[0:1, :] = jnp.sum(valid * mul_rows(out), axis=1, keepdims=True) * jnp.ones((1, 128), f32)
    sq_ref[1:2, :] = jnp.sum(valid * mul_rows(branch), axis=1, keepdims=True) * jnp.ones((1, 128), f32)
    sq_ref[2:3, :] = jnp.sum(valid, axis=1, keepdims=True) * jnp.full((1, 128), 0.5, f32)
    sq_ref[3:8, :] = jnp.zeros((5, 128), f32)
    column_halves(k, out.T, mine_ref, send_ref, full)


def mul_rows(v):
    rows = jnp.sum(v * v, axis=1, keepdims=True)
    return jnp.broadcast_to(rows, (v.shape[0], 128)).T[0:1, :]


def token_kernel(idx, own_ref, got_ref, slope_ref, hat_ref, gs_ref, e_ref, part_ref, sums_ref):
    y = idx[1]
    cols = at(y, HALF_D, 128)
    gain = gs_ref[0:1, cols]
    sum_cross = jnp.zeros((1, HALF_D), f32)
    sum_plain = jnp.zeros((1, HALF_D), f32)
    for r in chunks(own_ref.shape[0], 32):
        e = slope_ref[r, cols].astype(f32) * (own_ref[r, :] + got_ref[r, :].astype(f32))
        hat = hat_ref[r, cols].astype(f32)
        eg = e * gain
        e_ref[r, :] = eg
        part_ref[r, 0:1] = jnp.sum(eg, axis=1, keepdims=True)
        part_ref[r, 1:2] = jnp.sum(eg * hat, axis=1, keepdims=True)
        sum_cross = sum_cross + jnp.sum(e * hat, axis=0, keepdims=True)
        sum_plain = sum_plain + jnp.sum(e, axis=0, keepdims=True)
    put_stats(sums_ref, (sum_cross, sum_plain))


def flip_kernel(part_ref, o_ref):
    o_ref[...] = part_ref[...].T[0:8, :]


def token_back_kernel(idx, e_ref, hat_ref, scale_ref, part_ref, got_ref, mine_ref, send_ref, rows, full):
    cols = at(idx[1], HALF_D, 128)
    means = ((part_ref[...] + got_ref[...]) * (1.0 / D)).T
    for r in range(0, e_ref.shape[0], 64):
        s = slice(r, r + 64)
        hat = hat_ref[s, cols].astype(f32)
        rows[s, :] = scale_ref[s, 0:1] * (e_ref[s, :] - means[s, 0:1] - hat * means[s, 1:2])
    column_halves(idx[0], rows[...].T, mine_ref, send_ref, full)


def place_kernel(idx, mine_ref, got_ref, o_ref):
    half = mine_ref.shape[1]
    o_ref[:, at(idx[0], half, 128)] = mine_ref[...]
    o_ref[:, at(1 - idx[0], half, 128)] = got_ref[...]


def place_add_kernel(idx, mine_ref, got_ref, base_ref, o_ref):
    half = mine_ref.shape[1]
    mine, other = at(idx[0], half, 128), at(1 - idx[0], half, 128)
    o_ref[:, mine] = base_ref[:, mine] + mine_ref[...]
    o_ref[:, other] = base_ref[:, other] + got_ref[...]


TAIL = INNER // 2


def tap_columns(b):
    return ((D + b * INNER, INNER), (D + (2 + b) * INNER, INNER), (D + 4 * INNER + b * TAIL, TAIL))


def pair_columns(own_ref, got_ref, keep_ref, send_ref, mine, other):
    to = 0
    for (m, count), (o, _n) in zip(mine, other):
        for r in chunks(own_ref.shape[0], 32):
            keep_ref[r, to : to + count] = own_ref[r, m : m + count] + got_ref[r, m : m + count].astype(f32)
            send_ref[r, to : to + count] = (
                own_ref[r, o : o + count] + got_ref[r, o : o + count].astype(f32)
            ).astype(bf16)
        to += count


def early_kernel(idx, own_ref, got_ref, keep_last, send_last, keep_taps, send_taps):
    for b in range(2):

        @pl.when(idx[2] == b)
        def _():
            pair_columns(own_ref, got_ref, keep_last, send_last, [(b * INNER, INNER)], [((1 - b) * INNER, INNER)])
            pair_columns(own_ref, got_ref, keep_taps, send_taps, tap_columns(b), tap_columns(1 - b))


def pair_kernel(idx, own_ref, got_ref, keep_ref, send_ref):
    for b in range(2):

        @pl.when(idx[2] == b)
        def _():
            pair_columns(own_ref, got_ref, keep_ref, send_ref, [(b * INNER, INNER)], [((1 - b) * INNER, INNER)])


def taps_kernel(idx, keep_ref, got_ref, sum_ref, send_ref):
    for r in chunks(keep_ref.shape[0], 32):
        sum_ref[r, :] = keep_ref[r, :] + got_ref[r, :].astype(f32)

    @pl.when(idx[3] % 2 == 0)
    def _():
        send_ref[...] = sum_ref[:, INNER:].astype(bf16)

    @pl.when(idx[3] % 2 == 1)
    def _():
        send_ref[:, :INNER] = sum_ref[:, :INNER].astype(bf16)
        send_ref[:, INNER:] = jnp.zeros_like(send_ref[:, INNER:])


def line_kernel(
    H, idx, keep_f, got_f, keep_l, got_l, taps_ref, taps_got, part_ref, *send_refs
):
    h = idx[3]
    taps_part, taps_send = send_refs[H - 1 :]
    for d, ref in enumerate((part_ref, *send_refs[: H - 1])):
        to = (h - d + H) % H
        for q, (keep, got) in enumerate(((keep_f, got_f), (keep_l, got_l))):

            @pl.when(to == q + 1)
            def _():
                ref[...] = (keep[...] + got[...].astype(f32)).astype(ref.dtype)

        @pl.when((to != 1) & (to != 2))
        def _():
            ref[...] = jnp.zeros_like(ref)

    @pl.when(h % 2 == 0)
    def _():
        taps_part[:, :INNER] = taps_ref[:, :INNER] + taps_got[:, :INNER].astype(f32)
        taps_part[:, INNER:] = jnp.zeros_like(taps_part[:, INNER:])

    @pl.when(h % 2 == 1)
    def _():
        taps_part[...] = taps_ref[:, INNER:] + taps_got[...].astype(f32)

    taps_send[...] = taps_part[...].astype(bf16)


def own_kernel(idx, first_ref, taps_ref, last_ref, unit_ref):
    h, b = idx[3], idx[2]
    unit_ref[:, INNER:] = jnp.zeros_like(unit_ref[:, INNER:])
    for i in range(2):

        @pl.when((h == 0) & (b == i))
        def _():
            unit_ref[:, :INNER] = taps_ref[i]

        @pl.when((h == 1) & (b == i))
        def _():
            unit_ref[:, :INNER] = first_ref[:, i * INNER : (i + 1) * INNER]

        @pl.when((h == 2) & (b == i))
        def _():
            unit_ref[:, :INNER] = last_ref[:, i * INNER : (i + 1) * INNER]

        @pl.when((h == 3) & (b == i))
        def _():
            unit_ref[:, :INNER] = taps_ref[2 + i]
            unit_ref[:, INNER:] = taps_ref[4, :, i * TAIL : (i + 1) * TAIL]

    @pl.when(h > 3)
    def _():
        unit_ref[...] = jnp.zeros_like(unit_ref)


def finish_kernel(H, idx, old_ref, part_long, part_taps, *refs):
    got_long, got_taps = refs[: H - 1], refs[H - 1 : H]
    sum_ref, new_ref, cross_ref = refs[H:]
    h = idx[3]
    long = (h == 1) | (h == 2)

    @pl.when(long)
    def _():
        v = part_long[...]
        for got in got_long:
            v = v + got[...].astype(f32)
        sum_ref[:, :INNER] = v.astype(bf16)
        sum_ref[:, INNER:] = jnp.zeros_like(sum_ref[:, INNER:])
        new_ref[:, :INNER] = (muon_keep * old_ref[:, :INNER] + v).astype(bf16)
        new_ref[:, INNER:] = jnp.zeros_like(new_ref[:, INNER:])

    @pl.when(jnp.logical_not(long))
    def _():
        v = part_taps[...]
        for got in got_taps:
            v = v + got[...].astype(f32)
        sum_ref[...] = v.astype(bf16)
        new_ref[...] = (muon_keep * old_ref[...] + v).astype(bf16)

    @pl.when(h == 3)
    def _():
        cross_ref[:, :TAIL] = new_ref[:, INNER:]
        cross_ref[:, TAIL:] = new_ref[:, INNER:]

    @pl.when(h != 3)
    def _():
        cross_ref[...] = new_ref[:, :INNER]


def block_kernel(idx, new_ref, got_ref, o_ref):
    h, b = idx[3], idx[2]
    long = (h == 1) | (h == 2)
    for i in range(2):

        @pl.when(long & (b == i))
        def _():
            o_ref[:, i * INNER : (i + 1) * INNER] = new_ref[:, :INNER]
            o_ref[:, (1 - i) * INNER : (2 - i) * INNER] = got_ref[...]

        @pl.when(jnp.logical_not(long) & (b == i))
        def _():
            o_ref[:, :INNER] = new_ref[:, :INNER]
            o_ref[:, INNER + i * TAIL : INNER + (i + 1) * TAIL] = new_ref[:, INNER:]
            o_ref[:, INNER + (1 - i) * TAIL : INNER + (2 - i) * TAIL] = got_ref[:, :TAIL]


def sweep(X, Xh, Xl, A, Bh, Rh, width, low, last, carry):
    scale, squares = carry
    n = X.shape[0]
    alpha = squares * scale * scale * (1.0 / n)
    outer = scale * scale
    tile = n // 2
    rest = (coef_second + 2.0 * coef_third * alpha) * 1.0
    keep = (coef_first + coef_second * alpha + coef_third * alpha * alpha) * scale
    if low:
        Bl = mul(Xh[:, :width], Xl[:, :width], NT)
        A[...] = Bl + Bl.T
    for i in range(0, n, tile):
        r = slice(i, i + tile)
        a = mul(Xh[r, :width], Xh[:, :width], NT)
        if low:
            a = a + A[r, :]
        row = lax.broadcasted_iota(jnp.int32, (tile, n), 0) + i
        col = lax.broadcasted_iota(jnp.int32, (tile, n), 1)
        a = a * outer - jnp.where(row == col, alpha, 0.0)
        A[r, :] = a
        Bh[r, :] = a.astype(bf16)
    for i in range(0, n, tile):
        r = slice(i, i + tile)
        Rh[r, :] = (rest * A[r, :] + coef_third * mul(Bh[r, :], Bh[...], NN)).astype(bf16)
    total = jnp.zeros((8, 128), f32)
    for i in range(0, width, 256):
        c = slice(i, min(i + 256, width))
        v = keep * X[:, c] + scale * mul(Rh[...], Xh[:, c], NN)
        X[:, c] = v
        Xh[:, c] = v.astype(bf16)
        if last is not None:
            Xl[:, c] = (v - Xh[:, c].astype(f32)).astype(bf16)
        for q in range(0, c.stop - c.start, 128):
            w = v[:, q : q + 128]
            total = total + jnp.sum((w * w).reshape(n // 8, 8, 128), axis=0)
    return jnp.float32(1.0), jnp.sum(total)


def ortho_kernel(idx, own_ref, sib_ref, opp_ref, diag_ref, mine_ref, theirs_ref, X, Xh, Xl, A, Bh, Rh):
    n, C = X.shape
    k, y, h = idx[0], idx[1], idx[3]
    loc = own_ref.shape[0]
    long = (h == 1) | (h == 2)
    fifth = (h == 3) & (k == 1)
    blocks = (
        (2 * y + k, own_ref),
        (2 * y + 1 - k, sib_ref),
        (2 * (1 - y) + k, opp_ref),
        (2 * (1 - y) + 1 - k, diag_ref),
    )

    def load(first, count):
        total = jnp.zeros((8, count), f32)
        for place, ref in blocks:
            base = pl.multiple_of(place * loc, 32)
            for i in range(0, loc, 32):
                low = ref[i : i + 32, first : first + count]
                v = low.astype(f32)
                Xh[pl.ds(base + i, 32), :count] = low
                X[pl.ds(base + i, 32), :count] = v
                total = total + jnp.sum((v * v).reshape(4, 8, count), axis=0)
        squares = jnp.sum(total)
        return 1.0 / (jnp.sqrt(squares) + 1e-07), squares

    @pl.when(long)
    def _():
        carry = load(0, C)
        lax.fori_loop(0, 5, lambda i, c: sweep(X, Xh, Xl, A, Bh, Rh, C, False, None, c), carry)

    def taps(first):
        carry = load(first, INNER)
        carry = lax.fori_loop(0, 2, lambda i, c: sweep(X, Xh, Xl, A, Bh, Rh, INNER, False, True, c), carry)
        lax.fori_loop(0, 3, lambda i, c: sweep(X, Xh, Xl, A, Bh, Rh, INNER, True, True, c), carry)

    @pl.when(jnp.logical_not(long) & jnp.logical_not(fifth))
    def _():
        taps(0)

    @pl.when(fifth)
    def _():
        taps(INNER)

    mine_ref[...] = X[at(2 * y + k, loc), :].astype(bf16)
    theirs_ref[...] = X[at(2 * y + 1 - k, loc), :INNER].astype(bf16)


def step_kernel(idx, mine_ref, got_ref, o_ref):
    h, b, k = idx[3], idx[2], idx[0]

    @pl.when((h == 0) | ((h == 3) & (k == 0)))
    def _():
        o_ref[:, :INNER] = mine_ref[:, :INNER]

    @pl.when((h == 3) & (k == 1))
    def _():
        o_ref[:, :INNER] = got_ref[...]

    for i in range(2):

        @pl.when(((h == 1) | (h == 2)) & (b == i))
        def _():
            o_ref[:, :INNER] = mine_ref[:, i * INNER : (i + 1) * INNER]

        @pl.when((h == 3) & (k == 0) & (b == i))
        def _():
            o_ref[:, INNER:] = got_ref[:, i * TAIL : (i + 1) * TAIL]

        @pl.when((h == 3) & (k == 1) & (b == i))
        def _():
            o_ref[:, INNER:] = mine_ref[:, i * TAIL : (i + 1) * TAIL]

    @pl.when(h != 3)
    def _():
        o_ref[:, INNER:] = jnp.zeros_like(o_ref[:, INNER:])

    @pl.when(h > 3)
    def _():
        o_ref[:, :INNER] = jnp.zeros_like(o_ref[:, :INNER])


def join_kernel(idx, own_ref, got_ref, o_ref):
    h = idx[3]
    for q in range(2):

        @pl.when(h // 2 % 2 == q)
        def _():
            o_ref[:, q * INNER : (q + 1) * INNER] = own_ref[:, :INNER]
            o_ref[:, (1 - q) * INNER : (2 - q) * INNER] = got_ref[:, :INNER]
            o_ref[:, 2 * INNER :] = (own_ref if q else got_ref)[:, INNER:]


def apply_kernel(
    keep, rate_long, rate_tap, idx, own_ref, x_ref, z_ref, zx_ref, first_ref, taps_ref, last_ref,
    of_ref, ot_ref, ol_ref,
):
    h, b = idx[3], idx[2]
    for odd in range(2):
        for i in range(2):

            @pl.when((h % 2 == odd) & (b == i))
            def _():
                even = (own_ref, x_ref) if odd == 0 else (z_ref, zx_ref)
                odds = (z_ref, zx_ref) if odd == 0 else (own_ref, x_ref)
                for r in chunks(first_ref.shape[0], 32):
                    for q in range(2):
                        e = even[q ^ i]
                        o = odds[q ^ i]
                        lanes = slice(q * INNER, (q + 1) * INNER)
                        tail = slice(q * TAIL, (q + 1) * TAIL)
                        of_ref[r, lanes] = keep * first_ref[r, lanes] + rate_long * o[r, :INNER].astype(f32)
                        ol_ref[r, lanes] = keep * last_ref[r, lanes] + rate_long * e[r, INNER : 2 * INNER].astype(f32)
                        ot_ref[q, r, :] = keep * taps_ref[q, r, :] + rate_tap * e[r, :INNER].astype(f32)
                        ot_ref[2 + q, r, :] = keep * taps_ref[2 + q, r, :] + rate_tap * o[
                            r, INNER : 2 * INNER
                        ].astype(f32)
                        ot_ref[4, r, tail] = keep * taps_ref[4, r, tail] + rate_tap * o[r, 2 * INNER :].astype(f32)


ROWS = 24


def vector_kernel(idx, two_ref, three_ref, one_ref, cot_ref, sq_ref, o_ref):
    y, c = idx[1], 2 * idx[1] + idx[0]
    o_ref[...] = jnp.zeros_like(o_ref)
    o_ref[pl.ds(y, 1), :] = one_ref[0:1, :]
    o_ref[pl.ds(2 + y, 1), :] = one_ref[1:2, :]
    two = two_ref[...].T
    three = three_ref[...].T
    wide = two_ref.shape[0]
    pieces = (two[2:3], two[0:1], two[1:2], three[2:3], three[0:1], three[1:2])
    for i, piece in enumerate(pieces):
        o_ref[pl.ds(4 + 6 * y + i, 1), :wide] = piece
    cot = cot_ref[...].T
    o_ref[pl.ds(16 + c, 1), : cot_ref.shape[0]] = cot[0:1]
    for i in range(3):
        o_ref[20 + i : 21 + i, :128] = sq_ref[i : i + 1, :]


def adam_kernel(v_ref, par_ref, mom_ref, sqr_ref, first_ref, second_ref, value_ref, root_ref, g):
    wide = INNER // 2
    g[0:4, :] = v_ref[0:4, :]
    for i in range(6):
        g[4 + i : 5 + i, :wide] = v_ref[4 + i : 5 + i, :wide]
        g[4 + i : 5 + i, wide:] = v_ref[10 + i : 11 + i, :wide]
    for i in range(2):
        g[10 + i : 11 + i, :wide] = v_ref[16 + 2 * i : 17 + 2 * i, :wide]
        g[10 + i : 11 + i, wide:] = v_ref[17 + 2 * i : 18 + 2 * i, :wide]
    per = INNER // 128
    for r in range(12):
        for q in range(per):
            at_row = slice(r * per + q, r * per + q + 1)
            grad = g[r : r + 1, q * 128 : (q + 1) * 128]
            par = par_ref[at_row, :]
            first = adam_first * mom_ref[at_row, :] + (1.0 - adam_first) * grad
            second = adam_second * sqr_ref[at_row, :] + (1.0 - adam_second) * grad * grad
            first_ref[at_row, :] = first
            second_ref[at_row, :] = second
            value_ref[at_row, :] = par - adam_rate * (
                (first / (1.0 - adam_first**STEP)) / (jnp.sqrt(second / (1.0 - adam_second**STEP)) + adam_eps)
                + decay_rate * par
            )
    count = v_ref[22:23, :128] * D
    root_ref[...] = jnp.zeros_like(root_ref)
    for i in range(2):
        root_ref[i : i + 1, :] = jnp.sqrt(v_ref[20 + i : 21 + i, :128] / count)


def after(value, *others):
    return lax.optimization_barrier((value, *others))[0]


def body(
    tokens,
    cotangent,
    lengths,
    valid_mask,
    weight_first,
    weight_dilated,
    weight_last,
    momentum_first,
    momentum_dilated,
    momentum_last,
    vector_params,
    vector_moment,
    vector_square,
):
    C = lax.axis_size("ch")
    S = lax.axis_size("seq")
    c = lax.axis_index("ch")
    s = lax.axis_index("seq")
    k = c % 2
    y = c // 2
    T = tokens.shape[0]
    half = T // 2
    loc = weight_first.shape[1]
    wide = 2 * loc
    col = D // C
    H = S // 2
    b = s % 2
    h = s // 2
    idx = jnp.stack([k, y, b, h, s, s * T + k * half]).astype(jnp.int32)

    sib = [(i, i ^ 1) for i in range(C)]
    opp = [(i, i ^ 2) for i in range(C)]
    xsw = [(i, i ^ 1) for i in range(S)]

    def swap_core(v):
        return lax.ppermute(v, "ch", sib)

    def swap_y(v):
        return lax.ppermute(v, "ch", opp)

    def swap_x(v):
        return lax.ppermute(v, "seq", xsw)

    def along_h(v, pairs):
        return lax.ppermute(v, "seq", [(2 * i + q, 2 * j + q) for i, j in pairs for q in range(2)])

    outer_pairs = []
    for i in range(S):
        for j in range(C):
            if j % 2 == 0 and i >= 1:
                outer_pairs.append((i * C + j, (i - 1) * C + (j ^ 1)))
            if j % 2 == 1 and i + 1 < S:
                outer_pairs.append((i * C + j, (i + 1) * C + (j ^ 1)))

    def swap_outer(v):
        return lax.ppermute(v, ("seq", "ch"), outer_pairs)

    w_first, w_taps, w_last = weight_first.T, jnp.swapaxes(weight_dilated, 1, 2), weight_last
    m_first, m_taps, m_last = momentum_first.T, jnp.swapaxes(momentum_dilated, 1, 2), momentum_last
    cot = cotangent.T
    valid = valid_mask.reshape(1, T)
    gain_shift = vector_params[: 2 * D].reshape(2, D)
    inner_rows = vector_params[2 * D : 2 * D + 6 * INNER].reshape(6, INNER)
    cols = lax.dynamic_slice_in_dim(inner_rows, y * wide, wide, 1).T
    flat = (VECTOR // 128, 128)
    flat_params = vector_params.reshape(flat)

    low_first, cot_all, cot_other, cot_sums = call(
        prep_kernel,
        [((loc, D), bf16), ((col, T), bf16), ((col, half), bf16), ((col, 128), f32)],
        [idx],
        [w_first, cot],
    )
    got_first = swap_core(low_first)
    cot_opp = swap_y(cot_all)
    cot_sib = swap_core(cot_other)

    rows = 128
    steps = half // rows
    hid_one, hat_one, slope_one, scale_one = pl.pallas_call(
        input_kernel,
        out_shape=[
            jax.ShapeDtypeStruct((half, D), bf16),
            jax.ShapeDtypeStruct((half, D), bf16),
            jax.ShapeDtypeStruct((half, D), bf16),
            jax.ShapeDtypeStruct((half, 128), f32),
        ],
        grid_spec=pltpu.PrefetchScalarGridSpec(
            num_scalar_prefetch=1,
            grid=(steps,),
            in_specs=[
                pl.BlockSpec((rows, D), lambda i, idx: (idx[0] * steps + i, 0)),
                pl.BlockSpec((2, D), lambda i, idx: (0, 0)),
            ],
            out_specs=[
                pl.BlockSpec((rows, D), lambda i, idx: (i, 0)),
                pl.BlockSpec((rows, D), lambda i, idx: (i, 0)),
                pl.BlockSpec((rows, D), lambda i, idx: (i, 0)),
                pl.BlockSpec((rows, 128), lambda i, idx: (i, 0)),
            ],
        ),
        compiler_params=pltpu.CompilerParams(vmem_limit_bytes=16 * MIB),
        cost_estimate=pl.CostEstimate(flops=5000000000, bytes_accessed=1000, transcendentals=0),
    )(idx, tokens, gain_shift)

    (low_rest,) = call(
        rest_kernel, [((loc, D + KERNEL_TAPS * INNER), bf16)], [], [after(w_last, hid_one), w_taps]
    )
    got_rest = swap_core(low_rest)

    full_first, inner_one, st_two = call(
        first_kernel,
        [((wide, D), bf16), ((wide, half), f32), ((8, half), f32)],
        [idx],
        [low_first, got_first, hid_one, cols],
    )
    st_two_got = after(swap_y(st_two), cot_sib, cot_opp)
    (cot_diag,) = call(other_half_kernel, [((col, half), bf16)], [idx], [cot_opp])
    cot_diag = swap_core(cot_diag)
    slab = ((wide, REACH), bf16)
    own_in, own_out, hat_two, slope_two = call(
        second_kernel,
        [slab, slab, ((wide, half), f32), ((wide, half), f32)],
        [idx],
        [inner_one, st_two, st_two_got, cols, valid],
        scratch=[((wide, half), bf16)],
    )
    opp_in, opp_out = swap_y(own_in), swap_y(own_out)
    sib_in, seq_out = swap_core(own_in), swap_outer(own_out)
    sib_opp_in, seq_opp_out = swap_core(opp_in), swap_y(seq_out)
    ext, inner_two, st_three, full_last, full_taps, masks = call(
        functools.partial(conv_kernel, S * T),
        [
            ((INNER, half + 2 * REACH), bf16),
            ((wide, half), f32),
            ((8, half), f32),
            ((wide, D), bf16),
            ((wide, KERNEL_TAPS * INNER), bf16),
            ((8, half), f32),
        ],
        [idx, lengths],
        [
            own_in, own_out, opp_in, opp_out, sib_in, sib_opp_in, seq_out, seq_opp_out,
            low_rest, got_rest, cols,
        ],
        scratch=[((KERNEL_TAPS * INNER, half), bf16)],
    )
    st_three_got = swap_y(st_three)
    gw, g_three = call(
        cotangent_kernel,
        [((D, half), bf16), ((wide, half), f32)],
        [idx],
        [full_last, cot_all, cot_sib, cot_opp, cot_diag],
    )
    hid_three, e_three, hat_three, part_three = call(
        third_kernel,
        [((wide, half), bf16), ((wide, half), f32), ((wide, half), f32), ((8, half), f32)],
        [],
        [inner_two, st_three, st_three_got, cols, g_three],
    )
    part_three_got = swap_y(part_three)
    dz_two, slab_in, slab_out, sums_three = call(
        third_back_kernel,
        [((wide, half), bf16), ((wide, REACH), bf16), ((wide, REACH), bf16), ((wide, 128), f32)],
        [idx],
        [e_three, hat_three, part_three, part_three_got, cols],
    )
    got_in, got_out = swap_core(slab_in), swap_outer(slab_out)
    back_own, back_send = call(
        conv_back_kernel,
        [((wide, half), f32), ((wide, half), bf16)],
        [idx],
        [dz_two, got_in, got_out, masks, full_taps],
        scratch=[((wide, half + 2 * REACH), bf16), ((INNER, half), f32)],
    )
    back_got = swap_y(back_send)
    early_size = D + KERNEL_TAPS * INNER
    early_own, early_send = call(
        grads_kernel,
        [((loc, early_size), f32), ((loc, early_size), bf16)],
        [idx],
        [after(dz_two, back_send), ext, masks, hid_three, gw],
        scratch=[((wide, early_size), f32)],
        limit=32,
    )
    early_got = swap_core(early_send)
    unit, unit_low = ((loc, INNER), f32), ((loc, INNER), bf16)
    last_keep, last_send, taps_keep, taps_send = call(
        early_kernel,
        [unit, unit_low, ((loc, 2 * INNER + TAIL), f32), ((loc, 2 * INNER + TAIL), bf16)],
        [idx],
        [early_own, early_got],
    )
    last_got, taps_got = swap_x(last_send), swap_x(taps_send)
    e_two, part_two = call(
        second_back_kernel,
        [((wide, half), f32), ((8, half), f32)],
        [],
        [after(back_own, taps_send), back_got, slope_two, hat_two, cols],
    )
    half_out = [((half, HALF_D), f32), ((half, HALF_D), bf16)]
    branch_own, branch_send = call(
        halves_kernel, half_out, [idx], [after(hid_three, back_send), full_last], scratch=[((half, D), f32)]
    )
    part_two_got = after(swap_y(part_two), branch_send)
    branch_got = swap_y(after(branch_send, part_two_got))
    dz_one, first_own, first_send, sums_two = call(
        first_back_kernel,
        [((wide, half), bf16), ((loc, D), f32), ((loc, D), bf16), ((wide, 128), f32)],
        [idx],
        [e_two, hat_two, part_two, part_two_got, st_two, st_two_got, cols, hid_one],
        scratch=[((wide, D), f32)],
    )
    first_got = swap_core(first_send)
    first_keep, first_low = call(pair_kernel, [unit, unit_low], [idx], [first_own, first_got])
    first_low = after(first_low, taps_got)
    first_got = swap_x(first_low)

    span = H
    while span > 4:
        span //= 2
        fold = [(i + span, i) for i in range(span)]

        def folded(keep, got):
            total = keep + got.astype(f32)
            return total + along_h(total.astype(bf16), fold).astype(f32), jnp.zeros_like(got)

        first_keep, first_got = folded(first_keep, first_got)
        last_keep, last_got = folded(last_keep, last_got)
        taps_keep, taps_got = folded(taps_keep, taps_got)
    line = 4

    def to_owners(sends, owners):
        return [
            along_h(v, [((j + d + 1) % line, j) for j in owners]) for d, v in enumerate(sends)
        ]

    size_taps = (loc, INNER + TAIL)
    sum_taps, send_taps = call(
        taps_kernel, [((loc, 2 * INNER + TAIL), f32), (size_taps, bf16)], [idx], [taps_keep, taps_got]
    )
    got_taps = along_h(send_taps, [(i, i ^ 1) for i in range(line)])
    part_long, *sends, part_taps, send_taps = call(
        functools.partial(line_kernel, line),
        [unit] + [unit_low] * (line - 1) + [(size_taps, f32), (size_taps, bf16)],
        [idx],
        [first_keep, first_got, last_keep, last_got, sum_taps, got_taps],
    )
    got_long = to_owners(sends, (1, 2))
    got_taps = along_h(send_taps, [(2, 0), (1, 3)])
    back_own, back_send = call(
        halves_kernel, half_out, [idx], [after(dz_one, part_long), full_first], scratch=[((half, D), f32)]
    )
    back_got = swap_y(back_send)
    def whole_block(shape):
        return pl.BlockSpec(shape, lambda i, idx: (0, 0))

    out_mine, out_send, squares = pl.pallas_call(
        output_kernel,
        out_shape=[
            jax.ShapeDtypeStruct((col, half), f32),
            jax.ShapeDtypeStruct((col, half), f32),
            jax.ShapeDtypeStruct((8, 128), f32),
        ],
        grid_spec=pltpu.PrefetchScalarGridSpec(
            num_scalar_prefetch=1,
            grid=(1,),
            in_specs=[
                whole_block((half, HALF_D)),
                whole_block((half, HALF_D)),
                pl.BlockSpec((half, HALF_D), lambda i, idx: (idx[0], idx[1])),
                whole_block((VECTOR // 128, 128)),
                whole_block((1, T)),
            ],
            out_specs=[whole_block((col, half)), whole_block((col, half)), whole_block((8, 128))],
            scratch_shapes=[pltpu.VMEM((HALF_D, half), f32)],
        ),
        compiler_params=pltpu.CompilerParams(vmem_limit_bytes=24 * MIB),
        cost_estimate=pl.CostEstimate(flops=1000, bytes_accessed=1000, transcendentals=0),
    )(idx, branch_own, branch_got, tokens, flat_params, valid)
    e_one, part_one, sums_one = call(
        token_kernel,
        [((half, HALF_D), f32), ((half, 128), f32), ((8, HALF_D), f32)],
        [idx],
        [back_own, back_got, slope_one, hat_one, gain_shift],
    )
    (part_one,) = call(flip_kernel, [((8, half), f32)], [], [part_one])
    (vector,) = call(
        vector_kernel, [((ROWS, INNER), f32)], [idx], [sums_two, sums_three, sums_one, cot_sums, squares]
    )
    (old_unit,) = call(own_kernel, [(size_taps, f32)], [idx], [m_first, m_taps, m_last])
    sum_unit, new_unit, cross = call(
        functools.partial(finish_kernel, line),
        [(size_taps, bf16), (size_taps, bf16), unit_low],
        [idx],
        [old_unit, part_long, part_taps, *got_long, got_taps],
    )
    cross_got = swap_x(after(cross, squares, back_got))
    (block,) = call(block_kernel, [((loc, D), bf16)], [idx], [new_unit, cross_got])
    sum_far = along_h(sum_unit, [(i, i ^ 2) for i in range(4)])
    block_sib, block_opp = swap_core(block), swap_y(block)
    block_diag = swap_core(after(block_opp, sum_far))

    def joined_with(unit, got):
        return call(join_kernel, [((loc, 2 * INNER + TAIL), bf16)], [idx], [unit, got])[0]

    def next_along_z(joined):
        return along_h(joined, [(i, i ^ 1) for i in range(4)])

    def spread(parts):
        span = 4
        while span < H:
            pairs = [(i, i + span) for i in range(span)]
            parts = [jnp.where((h >= span) & (h < 2 * span), along_h(v, pairs), v) for v in parts]
            span *= 2
        return parts

    def apply(keep, rate_long, rate_tap, parts, first, taps, last):
        return call(
            functools.partial(apply_kernel, keep, rate_long, rate_tap),
            [((loc, D), f32), ((KERNEL_TAPS, loc, INNER), f32), ((loc, D), f32)],
            [idx],
            [*parts, first, taps, last],
            limit=32,
        )

    joined = joined_with(sum_unit, sum_far)
    mine, theirs = call(
        ortho_kernel,
        [((loc, D), bf16), ((loc, INNER), bf16)],
        [idx],
        [after(block, joined, sums_one), block_sib, block_opp, block_diag],
        scratch=[
            ((INNER, D), f32),
            ((INNER, D), bf16),
            ((INNER, INNER), bf16),
            ((INNER, INNER), f32),
            ((INNER, INNER), bf16),
            ((INNER, INNER), bf16),
        ],
        limit=32,
        flops=14 * 10**9,
    )
    joined_x = swap_x(joined)
    other = next_along_z(joined)
    theirs_got = swap_core(theirs)
    (step_unit,) = call(step_kernel, [(size_taps, bf16)], [idx], [after(mine, joined_x, other), theirs_got])
    other_x = swap_x(after(other, step_unit))
    mom_parts = spread([joined, joined_x, other, other_x])

    vector = after(vector, step_unit)
    vector = vector + swap_core(vector)
    vector = vector + swap_y(vector)
    vector = vector + swap_x(vector)
    step_far = along_h(step_unit, [(i, i ^ 2) for i in range(4)])
    joined = joined_with(after(step_unit, vector, other_x), step_far)
    joined_x = swap_x(joined)
    other = after(next_along_z(joined), joined_x)

    grad_mine, grad_send = call(
        token_back_kernel,
        [((col, half), f32), ((col, half), f32)],
        [idx],
        [after(e_one, joined), hat_one, scale_one, part_one, swap_y(part_one)],
        scratch=[((half, HALF_D), f32), ((HALF_D, half), f32)],
    )
    grad_got, out_got = swap_core(grad_send), swap_core(out_send)
    other, vector, grad_got, out_got = lax.optimization_barrier((other, vector, grad_got, out_got))
    other_x = swap_x(other)
    bit = 2
    while bit < S:
        vector = vector + lax.ppermute(vector, "seq", [(i, i ^ bit) for i in range(S)])
        bit *= 2
    (block_output,) = call(place_kernel, [((col, T), f32)], [idx], [out_mine, out_got])
    (tokens_grad,) = call(place_add_kernel, [((col, T), f32)], [idx], [grad_mine, grad_got, cot])
    vector_first, vector_second, vector_values, root = call(
        adam_kernel,
        [(flat, f32)] * 3 + [((8, 128), f32)],
        [],
        [vector, flat_params, vector_moment.reshape(flat), vector_square.reshape(flat)],
        scratch=[((12, INNER), f32)],
    )
    vector_first, vector_second, vector_values = (
        v.reshape(VECTOR) for v in (vector_first, vector_second, vector_values)
    )
    root_means = root[:2, 0]
    new_first, new_taps, new_last = apply(
        muon_keep, 1.0, 1.0, [after(mom_parts[0], other), *mom_parts[1:]], m_first, m_taps, m_last
    )
    keep_weight = 1.0 - muon_rate * decay_rate
    rate = muon_rate * muon_scale
    out_first, out_taps, out_last = apply(
        keep_weight,
        -rate * math.sqrt(D),
        -rate * math.sqrt(INNER),
        spread([joined, joined_x, other, other_x]),
        w_first,
        w_taps,
        w_last,
    )
    return (
        block_output.T,
        tokens_grad.T,
        out_first.T,
        jnp.swapaxes(out_taps, 1, 2),
        out_last,
        new_first.T,
        jnp.swapaxes(new_taps, 1, 2),
        new_last,
        vector_first,
        vector_second,
        vector_values,
        root_means,
    )


def solution(mesh):
    placed = (
        P("seq", None),
        P("seq", "ch"),
        P(),
        P("seq"),
        P(None, "ch"),
        P(None, None, "ch"),
        P("ch", None),
        P(None, "ch"),
        P(None, None, "ch"),
        P("ch", None),
        P(),
        P(),
        P(),
    )
    return jax.shard_map(
        body,
        mesh=mesh,
        in_specs=placed,
        out_specs=(
            P("seq", "ch"),
            P("seq", "ch"),
            P(None, "ch"),
            P(None, None, "ch"),
            P("ch", None),
            P(None, "ch"),
            P(None, None, "ch"),
            P("ch", None),
            P(),
            P(),
            P(),
            P(),
        ),
        check_vma=False,
    )
```

```python
import functools
import math

import jax
import jax.numpy as jnp
from jax import lax
from jax.experimental import pallas as pl
from jax.experimental.pallas import tpu as pltpu
from jax.sharding import PartitionSpec as P

D = 1280
INNER = 640
KERNEL_TAPS = 5
DILATION_SPAN = 128
STEP = 10

norm_eps = 1e-05
coef_first = 3.4445
coef_second = -4.775
coef_third = 2.0315
adam_rate = 0.4
adam_first = 0.9
adam_second = 0.999
adam_eps = 1e-08
decay_rate = 0.01
muon_rate = 0.1
muon_keep = 0.95
muon_scale = 0.2
REACH = KERNEL_TAPS // 2 * DILATION_SPAN
VECTOR = 3 * D + 6 * INNER
HALF_D = D // 2
MIB = 1024 * 1024

f32 = jnp.float32
bf16 = jnp.bfloat16
NN = (((1,), (0,)), ((), ()))
NT = (((1,), (1,)), ((), ()))
TN = (((0,), (0,)), ((), ()))


def mul(a, b, dims):
    return lax.dot_general(a, b, dims, preferred_element_type=f32)


def erf_parts(v):
    a = jnp.abs(v) * math.sqrt(0.5)
    t = pl.reciprocal(1.0 + 0.3275911 * a)
    e = jnp.exp(-a * a)
    p = t * (0.254829592 + t * (-0.284496736 + t * (1.421413741 + t * (-1.453152027 + t * 1.061405429))))
    tail = 0.5 * p * e
    return jnp.where(v >= 0, 1.0 - tail, tail), e


def gelu_pair(v):
    cdf, e = erf_parts(v)
    return v * cdf, cdf + v * e * (1.0 / math.sqrt(2.0 * math.pi))


VMEM = pl.BlockSpec(memory_space=pltpu.VMEM)
SMEM = pl.BlockSpec(memory_space=pltpu.SMEM)


def call(kernel, outs, scalars, arrays, scratch=(), limit=16, flops=1000):
    shapes = [jax.ShapeDtypeStruct(shape, dtype) for shape, dtype in outs]
    return pl.pallas_call(
        kernel,
        out_shape=shapes,
        in_specs=[SMEM] * len(scalars) + [VMEM] * len(arrays),
        out_specs=[VMEM] * len(outs),
        scratch_shapes=[pltpu.VMEM(shape, dtype) for shape, dtype in scratch],
        compiler_params=pltpu.CompilerParams(vmem_limit_bytes=limit * MIB),
        cost_estimate=pl.CostEstimate(flops=flops, bytes_accessed=1000, transcendentals=0),
    )(*scalars, *arrays)


def chunks(count, step):
    return [pl.ds(i, step) for i in range(0, count, step)]


def at(index, count, step=32):
    return pl.ds(pl.multiple_of(index * count, step), count)


def prep_kernel(idx, w_ref, cot_ref, wo_ref, all_ref, other_ref, sums_ref):
    half = other_ref.shape[1]
    for r in chunks(cot_ref.shape[0], 32):
        v = cot_ref[r, :]
        all_ref[r, :] = v.astype(bf16)
        other_ref[r, :] = cot_ref[r, at(1 - idx[0], half, 128)].astype(bf16)
        sums_ref[r, :] = jnp.broadcast_to(jnp.sum(v, axis=1, keepdims=True), (32, 128))
    for r in chunks(w_ref.shape[0], 32):
        wo_ref[r, :] = w_ref[r, :].astype(bf16)


def rest_kernel(last_ref, taps_ref, o_ref):
    for r in chunks(last_ref.shape[0], 32):
        o_ref[r, :D] = last_ref[r, :].astype(bf16)
        for j in range(KERNEL_TAPS):
            o_ref[r, D + j * INNER : D + (j + 1) * INNER] = taps_ref[j, r, :].astype(bf16)


def input_kernel(idx, tok_ref, gs_ref, hid_ref, hat_ref, slope_ref, scale_ref):
    for r in chunks(tok_ref.shape[0], 16):
        v = tok_ref[r, :]
        center = jnp.sum(v, axis=1, keepdims=True) * (1.0 / D)
        square = jnp.sum(v * v, axis=1, keepdims=True) * (1.0 / D)
        scale = lax.rsqrt(square - center * center + norm_eps)
        hat = (v - center) * scale
        hid, slope = gelu_pair(hat * gs_ref[0:1, :] + gs_ref[1:2, :])
        hid_ref[r, :] = hid.astype(bf16)
        hat_ref[r, :] = hat.astype(bf16)
        slope_ref[r, :] = slope.astype(bf16)
        scale_ref[r, :] = jnp.broadcast_to(scale, (16, 128))


def put_stats(ref, parts):
    for i, part in enumerate(parts):
        ref[i : i + 1, :] = part


def first_kernel(idx, own_ref, got_ref, hid_ref, cols_ref, w_ref, inner_ref, st_ref):
    k = idx[0]
    loc = own_ref.shape[0]
    w_ref[at(k, loc), :] = own_ref[...]
    w_ref[at(1 - k, loc), :] = got_ref[...]
    v = mul(w_ref[...], hid_ref[...], NT) + cols_ref[:, 0:1]
    inner_ref[...] = v
    put_stats(st_ref, (jnp.sum(v, axis=0, keepdims=True), jnp.sum(v * v, axis=0, keepdims=True)))


def center_scale(st_ref, got_ref):
    center = (st_ref[0:1, :] + got_ref[0:1, :]) * (1.0 / INNER)
    square = (st_ref[1:2, :] + got_ref[1:2, :]) * (1.0 / INNER)
    return center, lax.rsqrt(square - center * center + norm_eps)


def second_kernel(
    idx, inner_ref, st_ref, got_ref, cols_ref, valid_ref, in_ref, out_ref, hat_ref, slope_ref, hid_ref
):
    center, scale = center_scale(st_ref, got_ref)
    valid = valid_ref[:, at(idx[0], hid_ref.shape[1], 128)].astype(f32)
    for r in chunks(inner_ref.shape[0], 32):
        hat = (inner_ref[r, :] - center) * scale
        hid, slope = gelu_pair(hat * cols_ref[r, 1:2] + cols_ref[r, 2:3])
        hid_ref[r, :] = (hid * valid).astype(bf16)
        hat_ref[r, :] = hat
        slope_ref[r, :] = slope * valid
    slabs_of(idx[0], hid_ref, slice(None), in_ref, out_ref)


def slabs_of(k, v_ref, row, in_ref, out_ref):
    half = v_ref.shape[1]
    rows = v_ref.shape[0]
    in_ref[row, :] = v_ref[:, at(1 - k, half - REACH, 128)]
    out_ref[row, :] = v_ref[:, at(k, half - REACH, 128)]


def fill_reach(k, ext_ref, in_ref, out_ref, half):
    @pl.when(k == 0)
    def _():
        ext_ref[:, :REACH] = out_ref[...]
        ext_ref[:, REACH + half :] = in_ref[...]

    @pl.when(k == 1)
    def _():
        ext_ref[:, :REACH] = in_ref[...]
        ext_ref[:, REACH + half :] = out_ref[...]


def conv_kernel(
    total, idx, lengths, own_in, own_out, opp_in, opp_out, sib_in, sib_opp_in, seq_out, seq_opp_out,
    wo_ref, wg_ref, cols_ref, ext_ref, inner_ref, st_ref, last_ref, taps_ref, mask_ref, stack,
):
    k, y = idx[0], idx[1]
    wide, reach = own_in.shape
    half = 2 * reach
    loc = wo_ref.shape[0]
    for q in range(2):
        @pl.when(k == q)
        def _():
            for place, (mine, other) in enumerate(
                ((seq_out, seq_opp_out), (own_out, opp_out), (own_in, opp_in), (sib_in, sib_opp_in))
            ):
                place = 3 - place if q else place
                lanes = slice(place * reach, (place + 1) * reach)
                ext_ref[at(y, wide), lanes] = mine[...]
                ext_ref[at(1 - y, wide), lanes] = other[...]

    last_ref[at(k, loc), :] = wo_ref[:, :D]
    last_ref[at(1 - k, loc), :] = wg_ref[:, :D]
    taps_ref[at(k, loc), :] = wo_ref[:, D:]
    taps_ref[at(1 - k, loc), :] = wg_ref[:, D:]
    positions = idx[5] - REACH + lax.broadcasted_iota(jnp.int32, (1, half + 2 * REACH), 1)
    segment = jnp.zeros_like(positions)
    bound = jnp.int32(0)
    for i in range(lengths.shape[0]):
        bound = bound + lengths[i]
        segment = segment + (positions >= bound).astype(jnp.int32)
    segment = jnp.where((positions >= 0) & (positions < total), segment, -1)
    centre = segment[:, REACH : REACH + half]
    for j in range(KERNEL_TAPS):
        lanes = slice(j * DILATION_SPAN, j * DILATION_SPAN + half)
        mask = (segment[:, lanes] == centre).astype(f32)
        mask_ref[j : j + 1, :] = mask
        low = mask.astype(bf16)
        for i in range(0, INNER, 160):
            stack[j * INNER + i : j * INNER + i + 160, :] = ext_ref[i : i + 160, lanes] * low
    v = mul(taps_ref[...], stack[...], NN) + cols_ref[:, 3:4]
    inner_ref[...] = v
    put_stats(st_ref, (jnp.sum(v, axis=0, keepdims=True), jnp.sum(v * v, axis=0, keepdims=True)))


def cotangent_kernel(idx, last_ref, all_ref, sib_ref, opp_ref, diag_ref, gw_ref, g_ref):
    k, y = idx[0], idx[1]
    col, half = sib_ref.shape
    mine = at(k, half, 128)
    gw_ref[at(2 * y + k, col), :] = all_ref[:, mine]
    gw_ref[at(2 * y + 1 - k, col), :] = sib_ref[...]
    gw_ref[at(2 * (1 - y) + k, col), :] = opp_ref[:, mine]
    gw_ref[at(2 * (1 - y) + 1 - k, col), :] = diag_ref[...]
    g_ref[...] = mul(last_ref[...], gw_ref[...], NN)


def other_half_kernel(idx, all_ref, o_ref):
    o_ref[...] = all_ref[:, at(1 - idx[0], o_ref.shape[1], 128)]


def third_kernel(inner_ref, st_ref, got_ref, cols_ref, g_ref, hid_ref, e_ref, hat_ref, part_ref):
    center, scale = center_scale(st_ref, got_ref)
    plain = jnp.zeros_like(center)
    cross = jnp.zeros_like(center)
    for r in chunks(inner_ref.shape[0], 32):
        hat = (inner_ref[r, :] - center) * scale
        gain = cols_ref[r, 4:5]
        hid, slope = gelu_pair(hat * gain + cols_ref[r, 5:6])
        hid_ref[r, :] = hid.astype(bf16)
        hat_ref[r, :] = hat
        e = slope * g_ref[r, :]
        e_ref[r, :] = e
        eg = e * gain
        plain = plain + jnp.sum(eg, axis=0, keepdims=True)
        cross = cross + jnp.sum(eg * hat, axis=0, keepdims=True)
    put_stats(part_ref, (plain, cross, scale))


def norm_back(r, e_ref, hat_ref, part_ref, got_ref, scale, gain, sums_ref):
    plain = (part_ref[0:1, :] + got_ref[0:1, :]) * (1.0 / INNER)
    cross = (part_ref[1:2, :] + got_ref[1:2, :]) * (1.0 / INNER)
    e, hat = e_ref[r, :], hat_ref[r, :]
    grad = scale * (e * gain - plain - hat * cross)
    sums_ref[r, 0:1] = jnp.sum(e * hat, axis=1, keepdims=True)
    sums_ref[r, 1:2] = jnp.sum(e, axis=1, keepdims=True)
    sums_ref[r, 2:3] = jnp.sum(grad, axis=1, keepdims=True)
    return grad


def third_back_kernel(idx, e_ref, hat_ref, part_ref, got_ref, cols_ref, dz_ref, in_ref, out_ref, sums_ref):
    for r in chunks(e_ref.shape[0], 32):
        grad = norm_back(r, e_ref, hat_ref, part_ref, got_ref, part_ref[2:3, :], cols_ref[r, 4:5], sums_ref)
        dz_ref[r, :] = grad.astype(bf16)
    slabs_of(idx[0], dz_ref, slice(None), in_ref, out_ref)


def split_rows(k, full, own_ref, send_ref, lanes):
    loc = own_ref.shape[0]
    own_ref[:, lanes] = full[at(k, loc), lanes]
    send_ref[:, lanes] = full[at(1 - k, loc), lanes].astype(bf16)


def grads_kernel(idx, dz_ref, ext_ref, mask_ref, hid_ref, gw_ref, own_ref, send_ref, full):
    k = idx[0]
    half = dz_ref.shape[1]
    full[:, :D] = mul(hid_ref[...], gw_ref[...], NT)
    split_rows(k, full, own_ref, send_ref, slice(0, D))
    for j in range(KERNEL_TAPS):
        masked = dz_ref[...] * mask_ref[j : j + 1, :].astype(bf16)
        moved = ext_ref[:, j * DILATION_SPAN : j * DILATION_SPAN + half]
        lanes = slice(D + j * INNER, D + (j + 1) * INNER)
        full[:, lanes] = mul(masked, moved, NT)
        split_rows(k, full, own_ref, send_ref, lanes)


def conv_back_kernel(idx, dz_ref, in_ref, out_ref, mask_ref, taps_ref, own_ref, send_ref, ext, full):
    k, y = idx[0], idx[1]
    wide, half = dz_ref.shape
    ext[:, REACH : REACH + half] = dz_ref[...]
    fill_reach(k, ext, in_ref, out_ref, half)
    total = None
    for j in range(KERNEL_TAPS):
        begin = REACH - (j - KERNEL_TAPS // 2) * DILATION_SPAN
        mask = mask_ref[KERNEL_TAPS - 1 - j : KERNEL_TAPS - j, :].astype(bf16)
        part = mul(taps_ref[:, j * INNER : (j + 1) * INNER], ext[:, begin : begin + half] * mask, TN)
        total = part if total is None else total + part
    full[...] = total
    own_ref[...] = full[at(y, wide), :]
    send_ref[...] = full[at(1 - y, wide), :].astype(bf16)


def second_back_kernel(own_ref, got_ref, slope_ref, hat_ref, cols_ref, e_ref, part_ref):
    plain = jnp.zeros((1, own_ref.shape[1]), f32)
    cross = jnp.zeros_like(plain)
    for r in chunks(own_ref.shape[0], 32):
        e = slope_ref[r, :] * (own_ref[r, :] + got_ref[r, :].astype(f32))
        e_ref[r, :] = e
        eg = e * cols_ref[r, 1:2]
        plain = plain + jnp.sum(eg, axis=0, keepdims=True)
        cross = cross + jnp.sum(eg * hat_ref[r, :], axis=0, keepdims=True)
    put_stats(part_ref, (plain, cross))


def first_back_kernel(
    idx, e_ref, hat_ref, part_ref, got_ref, st_ref, stg_ref, cols_ref, hid_ref,
    dz_ref, own_ref, send_ref, sums_ref, full,
):
    _, scale = center_scale(st_ref, stg_ref)
    for r in chunks(e_ref.shape[0], 32):
        grad = norm_back(r, e_ref, hat_ref, part_ref, got_ref, scale, cols_ref[r, 1:2], sums_ref)
        dz_ref[r, :] = grad.astype(bf16)
    full[...] = mul(dz_ref[...], hid_ref[...], NN)
    split_rows(idx[0], full, own_ref, send_ref, slice(0, D))


def halves_kernel(idx, z_ref, w_ref, own_ref, send_ref, full):
    y = idx[1]
    full[...] = mul(z_ref[...], w_ref[...], TN)
    for r in chunks(full.shape[0], 64):
        own_ref[r, :] = full[r, at(y, HALF_D, 128)]
        send_ref[r, :] = full[r, at(1 - y, HALF_D, 128)].astype(bf16)


def column_halves(k, flipped, mine_ref, send_ref, full):
    col = mine_ref.shape[0]
    full[...] = flipped
    mine_ref[...] = full[at(k, col), :]
    send_ref[...] = full[at(1 - k, col), :]


def output_kernel(idx, own_ref, got_ref, tok_ref, flat_ref, valid_ref, mine_ref, send_ref, sq_ref, full):
    k, y = idx[0], idx[1]
    half = own_ref.shape[0]
    per = HALF_D // 128
    first = (2 * D + 6 * INNER) // 128 + per * y
    bias = jnp.concatenate([flat_ref[pl.ds(first + q, 1), :] for q in range(per)], axis=1)
    branch = own_ref[...] + got_ref[...].astype(f32) + bias
    out = tok_ref[...] + branch
    valid = valid_ref[:, at(k, half, 128)].astype(f32)
    sq_ref[0:1, :] = jnp.sum(valid * mul_rows(out), axis=1, keepdims=True) * jnp.ones((1, 128), f32)
    sq_ref[1:2, :] = jnp.sum(valid * mul_rows(branch), axis=1, keepdims=True) * jnp.ones((1, 128), f32)
    sq_ref[2:3, :] = jnp.sum(valid, axis=1, keepdims=True) * jnp.full((1, 128), 0.5, f32)
    sq_ref[3:8, :] = jnp.zeros((5, 128), f32)
    column_halves(k, out.T, mine_ref, send_ref, full)


def mul_rows(v):
    rows = jnp.sum(v * v, axis=1, keepdims=True)
    return jnp.broadcast_to(rows, (v.shape[0], 128)).T[0:1, :]


def token_kernel(idx, own_ref, got_ref, slope_ref, hat_ref, gs_ref, e_ref, part_ref, sums_ref):
    y = idx[1]
    cols = at(y, HALF_D, 128)
    gain = gs_ref[0:1, cols]
    sum_cross = jnp.zeros((1, HALF_D), f32)
    sum_plain = jnp.zeros((1, HALF_D), f32)
    for r in chunks(own_ref.shape[0], 32):
        e = slope_ref[r, cols].astype(f32) * (own_ref[r, :] + got_ref[r, :].astype(f32))
        hat = hat_ref[r, cols].astype(f32)
        eg = e * gain
        e_ref[r, :] = eg
        part_ref[r, 0:1] = jnp.sum(eg, axis=1, keepdims=True)
        part_ref[r, 1:2] = jnp.sum(eg * hat, axis=1, keepdims=True)
        sum_cross = sum_cross + jnp.sum(e * hat, axis=0, keepdims=True)
        sum_plain = sum_plain + jnp.sum(e, axis=0, keepdims=True)
    put_stats(sums_ref, (sum_cross, sum_plain))


def flip_kernel(part_ref, o_ref):
    o_ref[...] = part_ref[...].T[0:8, :]


def token_back_kernel(idx, e_ref, hat_ref, scale_ref, part_ref, got_ref, mine_ref, send_ref, rows, full):
    cols = at(idx[1], HALF_D, 128)
    means = ((part_ref[...] + got_ref[...]) * (1.0 / D)).T
    for r in range(0, e_ref.shape[0], 64):
        s = slice(r, r + 64)
        hat = hat_ref[s, cols].astype(f32)
        rows[s, :] = scale_ref[s, 0:1] * (e_ref[s, :] - means[s, 0:1] - hat * means[s, 1:2])
    column_halves(idx[0], rows[...].T, mine_ref, send_ref, full)


def place_kernel(idx, mine_ref, got_ref, o_ref):
    half = mine_ref.shape[1]
    o_ref[:, at(idx[0], half, 128)] = mine_ref[...]
    o_ref[:, at(1 - idx[0], half, 128)] = got_ref[...]


def place_add_kernel(idx, mine_ref, got_ref, base_ref, o_ref):
    half = mine_ref.shape[1]
    mine, other = at(idx[0], half, 128), at(1 - idx[0], half, 128)
    o_ref[:, mine] = base_ref[:, mine] + mine_ref[...]
    o_ref[:, other] = base_ref[:, other] + got_ref[...]


TAIL = INNER // 2


def tap_columns(b):
    return ((D + b * INNER, INNER), (D + (2 + b) * INNER, INNER), (D + 4 * INNER + b * TAIL, TAIL))


def pair_columns(own_ref, got_ref, keep_ref, send_ref, mine, other):
    to = 0
    for (m, count), (o, _n) in zip(mine, other):
        for r in chunks(own_ref.shape[0], 32):
            keep_ref[r, to : to + count] = own_ref[r, m : m + count] + got_ref[r, m : m + count].astype(f32)
            send_ref[r, to : to + count] = (
                own_ref[r, o : o + count] + got_ref[r, o : o + count].astype(f32)
            ).astype(bf16)
        to += count


def early_kernel(idx, own_ref, got_ref, keep_last, send_last, keep_taps, send_taps):
    for b in range(2):

        @pl.when(idx[2] == b)
        def _():
            pair_columns(own_ref, got_ref, keep_last, send_last, [(b * INNER, INNER)], [((1 - b) * INNER, INNER)])
            pair_columns(own_ref, got_ref, keep_taps, send_taps, tap_columns(b), tap_columns(1 - b))


def pair_kernel(idx, own_ref, got_ref, keep_ref, send_ref):
    for b in range(2):

        @pl.when(idx[2] == b)
        def _():
            pair_columns(own_ref, got_ref, keep_ref, send_ref, [(b * INNER, INNER)], [((1 - b) * INNER, INNER)])


def taps_kernel(idx, keep_ref, got_ref, sum_ref, send_ref):
    for r in chunks(keep_ref.shape[0], 32):
        sum_ref[r, :] = keep_ref[r, :] + got_ref[r, :].astype(f32)

    @pl.when(idx[3] % 2 == 0)
    def _():
        send_ref[...] = sum_ref[:, INNER:].astype(bf16)

    @pl.when(idx[3] % 2 == 1)
    def _():
        send_ref[:, :INNER] = sum_ref[:, :INNER].astype(bf16)
        send_ref[:, INNER:] = jnp.zeros_like(send_ref[:, INNER:])


LINE = (
    ((0, 0), (1, 3), (2, 1), (3, 2)),
    ((0, 2), (1, 0), (2, 3), (3, 1)),
    ((0, 1), (1, 2), (2, 0), (3, 3)),
)
LINE_TAIL = ((0, 0), (1, 3), (2, 2), (3, 1))


def line_kernel(
    idx, keep_f, got_f, keep_l, got_l, taps_ref, taps_got,
    part_ref, tail_part, one_ref, two_ref, three_ref, tail_ref,
):
    h = idx[3]
    first = keep_f[...] + got_f[...].astype(f32)
    last = keep_l[...] + got_l[...].astype(f32)
    even = taps_ref[:, :INNER] + taps_got[:, :INNER].astype(f32)
    odd = taps_ref[:, INNER : 2 * INNER] + taps_got[:, :INNER].astype(f32)
    tail = taps_ref[:, 2 * INNER :] + taps_got[:, INNER:].astype(f32)
    low_first, low_last = first.astype(bf16), last.astype(bf16)
    tail_part[...] = tail
    tail_ref[...] = tail.astype(bf16)

    @pl.when(h == 0)
    def _():
        part_ref[...] = even
        one_ref[...] = low_first
        two_ref[...] = low_last
        three_ref[...] = low_first

    @pl.when(h == 1)
    def _():
        part_ref[...] = first
        one_ref[...] = odd.astype(bf16)
        two_ref[...] = low_last
        three_ref[...] = low_last

    @pl.when(h == 2)
    def _():
        part_ref[...] = last
        one_ref[...] = low_first
        two_ref[...] = low_first
        three_ref[...] = even.astype(bf16)

    @pl.when(h >= 3)
    def _():
        part_ref[...] = odd
        one_ref[...] = low_last
        two_ref[...] = low_first
        three_ref[...] = low_last


def own_kernel(idx, first_ref, taps_ref, last_ref, unit_ref):
    h, b = idx[3], idx[2]
    unit_ref[:, INNER:] = jnp.zeros_like(unit_ref[:, INNER:])
    for i in range(2):

        @pl.when((h == 0) & (b == i))
        def _():
            unit_ref[:, :INNER] = taps_ref[i]

        @pl.when((h == 1) & (b == i))
        def _():
            unit_ref[:, :INNER] = first_ref[:, i * INNER : (i + 1) * INNER]

        @pl.when((h == 2) & (b == i))
        def _():
            unit_ref[:, :INNER] = last_ref[:, i * INNER : (i + 1) * INNER]

        @pl.when((h == 3) & (b == i))
        def _():
            unit_ref[:, :INNER] = taps_ref[2 + i]
            unit_ref[:, INNER:] = taps_ref[4, :, i * TAIL : (i + 1) * TAIL]

    @pl.when(h > 3)
    def _():
        unit_ref[...] = jnp.zeros_like(unit_ref)


def finish_kernel(
    idx, old_ref, part_ref, tail_part, one_got, two_got, three_got, tail_got,
    sum_ref, tail_ref, new_ref, cross_ref,
):
    h = idx[3]

    def put(v):
        sum_ref[...] = v.astype(bf16)
        new_ref[:, :INNER] = (muon_keep * old_ref[:, :INNER] + v).astype(bf16)

    @pl.when(h == 0)
    def _():
        put(part_ref[...] + three_got[...].astype(f32))

    @pl.when((h == 1) | (h == 2))
    def _():
        put(part_ref[...] + one_got[...].astype(f32) + two_got[...].astype(f32) + three_got[...].astype(f32))

    @pl.when(h >= 3)
    def _():
        put(part_ref[...] + one_got[...].astype(f32))

    tail = tail_part[...] + tail_got[...].astype(f32)
    tail_ref[...] = tail.astype(bf16)
    new_ref[:, INNER:] = (muon_keep * old_ref[:, INNER:] + tail).astype(bf16)

    @pl.when(h == 3)
    def _():
        cross_ref[:, :TAIL] = new_ref[:, INNER:]
        cross_ref[:, TAIL:] = new_ref[:, INNER:]

    @pl.when(h != 3)
    def _():
        cross_ref[...] = new_ref[:, :INNER]


def block_kernel(idx, new_ref, got_ref, o_ref):
    h, b = idx[3], idx[2]
    long = (h == 1) | (h == 2)
    for i in range(2):

        @pl.when(long & (b == i))
        def _():
            o_ref[:, i * INNER : (i + 1) * INNER] = new_ref[:, :INNER]
            o_ref[:, (1 - i) * INNER : (2 - i) * INNER] = got_ref[...]

        @pl.when(jnp.logical_not(long) & (b == i))
        def _():
            o_ref[:, :INNER] = new_ref[:, :INNER]
            o_ref[:, INNER + i * TAIL : INNER + (i + 1) * TAIL] = new_ref[:, INNER:]
            o_ref[:, INNER + (1 - i) * TAIL : INNER + (2 - i) * TAIL] = got_ref[:, :TAIL]


def sweep(X, Xh, Xl, A, Bh, Rh, width, low, last, carry):
    scale, squares = carry
    n = X.shape[0]
    alpha = squares * scale * scale * (1.0 / n)
    outer = scale * scale
    tile = n // 2
    rest = (coef_second + 2.0 * coef_third * alpha) * 1.0
    keep = (coef_first + coef_second * alpha + coef_third * alpha * alpha) * scale
    if low:
        Bl = mul(Xh[:, :width], Xl[:, :width], NT)
        A[...] = Bl + Bl.T
    for i in range(0, n, tile):
        r = slice(i, i + tile)
        a = mul(Xh[r, :width], Xh[:, :width], NT)
        if low:
            a = a + A[r, :]
        row = lax.broadcasted_iota(jnp.int32, (tile, n), 0) + i
        col = lax.broadcasted_iota(jnp.int32, (tile, n), 1)
        a = a * outer - jnp.where(row == col, alpha, 0.0)
        A[r, :] = a
        Bh[r, :] = a.astype(bf16)
    for i in range(0, n, tile):
        r = slice(i, i + tile)
        Rh[r, :] = (rest * A[r, :] + coef_third * mul(Bh[r, :], Bh[...], NN)).astype(bf16)
    total = jnp.zeros((8, 128), f32)
    for i in range(0, width, 256):
        c = slice(i, min(i + 256, width))
        v = keep * X[:, c] + scale * mul(Rh[...], Xh[:, c], NN)
        X[:, c] = v
        Xh[:, c] = v.astype(bf16)
        if last is not None:
            Xl[:, c] = (v - Xh[:, c].astype(f32)).astype(bf16)
        for q in range(0, c.stop - c.start, 128):
            w = v[:, q : q + 128]
            total = total + jnp.sum((w * w).reshape(n // 8, 8, 128), axis=0)
    return jnp.float32(1.0), jnp.sum(total)


def ortho_kernel(idx, own_ref, sib_ref, opp_ref, diag_ref, mine_ref, theirs_ref, X, Xh, Xl, A, Bh, Rh):
    n, C = X.shape
    k, y, h = idx[0], idx[1], idx[3]
    loc = own_ref.shape[0]
    long = (h == 1) | (h == 2)
    fifth = (h == 3) & (k == 1)
    blocks = (
        (2 * y + k, own_ref),
        (2 * y + 1 - k, sib_ref),
        (2 * (1 - y) + k, opp_ref),
        (2 * (1 - y) + 1 - k, diag_ref),
    )

    def load(first, count):
        total = jnp.zeros((8, count), f32)
        for place, ref in blocks:
            base = pl.multiple_of(place * loc, 32)
            for i in range(0, loc, 32):
                low = ref[i : i + 32, first : first + count]
                v = low.astype(f32)
                Xh[pl.ds(base + i, 32), :count] = low
                X[pl.ds(base + i, 32), :count] = v
                total = total + jnp.sum((v * v).reshape(4, 8, count), axis=0)
        squares = jnp.sum(total)
        return 1.0 / (jnp.sqrt(squares) + 1e-07), squares

    @pl.when(long)
    def _():
        carry = load(0, C)
        lax.fori_loop(0, 5, lambda i, c: sweep(X, Xh, Xl, A, Bh, Rh, C, False, None, c), carry)

    def taps(first):
        carry = load(first, INNER)
        carry = lax.fori_loop(0, 2, lambda i, c: sweep(X, Xh, Xl, A, Bh, Rh, INNER, False, True, c), carry)
        lax.fori_loop(0, 3, lambda i, c: sweep(X, Xh, Xl, A, Bh, Rh, INNER, True, True, c), carry)

    @pl.when(jnp.logical_not(long) & jnp.logical_not(fifth))
    def _():
        taps(0)

    @pl.when(fifth)
    def _():
        taps(INNER)

    mine_ref[...] = X[at(2 * y + k, loc), :].astype(bf16)
    theirs_ref[...] = X[at(2 * y + 1 - k, loc), :INNER].astype(bf16)


def step_kernel(idx, mine_ref, got_ref, o_ref, tail_ref):
    h, b, k = idx[3], idx[2], idx[0]

    @pl.when((h == 0) | ((h == 3) & (k == 0)) | (h > 3))
    def _():
        o_ref[...] = mine_ref[:, :INNER]

    @pl.when((h == 3) & (k == 1))
    def _():
        o_ref[...] = got_ref[...]

    for i in range(2):

        @pl.when(((h == 1) | (h == 2)) & (b == i))
        def _():
            o_ref[...] = mine_ref[:, i * INNER : (i + 1) * INNER]

        @pl.when((h == 3) & (k == 0) & (b == i))
        def _():
            tail_ref[...] = got_ref[:, i * TAIL : (i + 1) * TAIL]

        @pl.when((h == 3) & (k == 1) & (b == i))
        def _():
            tail_ref[...] = mine_ref[:, i * TAIL : (i + 1) * TAIL]

    @pl.when(h != 3)
    def _():
        tail_ref[...] = jnp.zeros_like(tail_ref)


def join_kernel(idx, own_ref, got_ref, tail_ref, tail_got, o_ref):
    h = idx[3]
    for q in range(2):

        @pl.when(h // 2 % 2 == q)
        def _():
            o_ref[:, q * INNER : (q + 1) * INNER] = own_ref[...]
            o_ref[:, (1 - q) * INNER : (2 - q) * INNER] = got_ref[...]
            o_ref[:, 2 * INNER :] = (tail_ref if q else tail_got)[...]


def apply_kernel(
    keep, rate_long, rate_tap, idx, own_ref, x_ref, z_ref, zx_ref, first_ref, taps_ref, last_ref,
    of_ref, ot_ref, ol_ref,
):
    h, b = idx[3], idx[2]
    for odd in range(2):
        for i in range(2):

            @pl.when((h % 2 == odd) & (b == i))
            def _():
                even = (own_ref, x_ref) if odd == 0 else (z_ref, zx_ref)
                odds = (z_ref, zx_ref) if odd == 0 else (own_ref, x_ref)
                for r in chunks(first_ref.shape[0], 32):
                    for q in range(2):
                        e = even[q ^ i]
                        o = odds[q ^ i]
                        lanes = slice(q * INNER, (q + 1) * INNER)
                        tail = slice(q * TAIL, (q + 1) * TAIL)
                        of_ref[r, lanes] = keep * first_ref[r, lanes] + rate_long * o[r, :INNER].astype(f32)
                        ol_ref[r, lanes] = keep * last_ref[r, lanes] + rate_long * e[r, INNER : 2 * INNER].astype(f32)
                        ot_ref[q, r, :] = keep * taps_ref[q, r, :] + rate_tap * e[r, :INNER].astype(f32)
                        ot_ref[2 + q, r, :] = keep * taps_ref[2 + q, r, :] + rate_tap * o[
                            r, INNER : 2 * INNER
                        ].astype(f32)
                        ot_ref[4, r, tail] = keep * taps_ref[4, r, tail] + rate_tap * o[r, 2 * INNER :].astype(f32)


ROWS = 24


def vector_kernel(idx, two_ref, three_ref, one_ref, cot_ref, sq_ref, o_ref):
    y, c = idx[1], 2 * idx[1] + idx[0]
    o_ref[...] = jnp.zeros_like(o_ref)
    o_ref[pl.ds(y, 1), :] = one_ref[0:1, :]
    o_ref[pl.ds(2 + y, 1), :] = one_ref[1:2, :]
    two = two_ref[...].T
    three = three_ref[...].T
    wide = two_ref.shape[0]
    pieces = (two[2:3], two[0:1], two[1:2], three[2:3], three[0:1], three[1:2])
    for i, piece in enumerate(pieces):
        o_ref[pl.ds(4 + 6 * y + i, 1), :wide] = piece
    cot = cot_ref[...].T
    o_ref[pl.ds(16 + c, 1), : cot_ref.shape[0]] = cot[0:1]
    for i in range(3):
        o_ref[20 + i : 21 + i, :128] = sq_ref[i : i + 1, :]


def adam_kernel(v_ref, par_ref, mom_ref, sqr_ref, first_ref, second_ref, value_ref, root_ref, g):
    wide = INNER // 2
    g[0:4, :] = v_ref[0:4, :]
    for i in range(6):
        g[4 + i : 5 + i, :wide] = v_ref[4 + i : 5 + i, :wide]
        g[4 + i : 5 + i, wide:] = v_ref[10 + i : 11 + i, :wide]
    for i in range(2):
        g[10 + i : 11 + i, :wide] = v_ref[16 + 2 * i : 17 + 2 * i, :wide]
        g[10 + i : 11 + i, wide:] = v_ref[17 + 2 * i : 18 + 2 * i, :wide]
    per = INNER // 128
    for r in range(12):
        for q in range(per):
            at_row = slice(r * per + q, r * per + q + 1)
            grad = g[r : r + 1, q * 128 : (q + 1) * 128]
            par = par_ref[at_row, :]
            first = adam_first * mom_ref[at_row, :] + (1.0 - adam_first) * grad
            second = adam_second * sqr_ref[at_row, :] + (1.0 - adam_second) * grad * grad
            first_ref[at_row, :] = first
            second_ref[at_row, :] = second
            value_ref[at_row, :] = par - adam_rate * (
                (first / (1.0 - adam_first**STEP)) / (jnp.sqrt(second / (1.0 - adam_second**STEP)) + adam_eps)
                + decay_rate * par
            )
    count = v_ref[22:23, :128] * D
    root_ref[...] = jnp.zeros_like(root_ref)
    for i in range(2):
        root_ref[i : i + 1, :] = jnp.sqrt(v_ref[20 + i : 21 + i, :128] / count)


def after(value, *others):
    return lax.optimization_barrier((value, *others))[0]


def body(
    tokens,
    cotangent,
    lengths,
    valid_mask,
    weight_first,
    weight_dilated,
    weight_last,
    momentum_first,
    momentum_dilated,
    momentum_last,
    vector_params,
    vector_moment,
    vector_square,
):
    C = lax.axis_size("ch")
    S = lax.axis_size("seq")
    c = lax.axis_index("ch")
    s = lax.axis_index("seq")
    k = c % 2
    y = c // 2
    T = tokens.shape[0]
    half = T // 2
    loc = weight_first.shape[1]
    wide = 2 * loc
    col = D // C
    H = S // 2
    b = s % 2
    h = s // 2
    idx = jnp.stack([k, y, b, h, s, s * T + k * half]).astype(jnp.int32)

    sib = [(i, i ^ 1) for i in range(C)]
    opp = [(i, i ^ 2) for i in range(C)]
    xsw = [(i, i ^ 1) for i in range(S)]

    def swap_core(v):
        return lax.ppermute(v, "ch", sib)

    def swap_y(v):
        return lax.ppermute(v, "ch", opp)

    def swap_x(v):
        return lax.ppermute(v, "seq", xsw)

    def along_h(v, pairs):
        return lax.ppermute(v, "seq", [(2 * i + q, 2 * j + q) for i, j in pairs for q in range(2)])

    outer_pairs = []
    for i in range(S):
        for j in range(C):
            if j % 2 == 0 and i >= 1:
                outer_pairs.append((i * C + j, (i - 1) * C + (j ^ 1)))
            if j % 2 == 1 and i + 1 < S:
                outer_pairs.append((i * C + j, (i + 1) * C + (j ^ 1)))

    def swap_outer(v):
        return lax.ppermute(v, ("seq", "ch"), outer_pairs)

    w_first, w_taps, w_last = weight_first.T, jnp.swapaxes(weight_dilated, 1, 2), weight_last
    m_first, m_taps, m_last = momentum_first.T, jnp.swapaxes(momentum_dilated, 1, 2), momentum_last
    cot = cotangent.T
    valid = valid_mask.reshape(1, T)
    gain_shift = vector_params[: 2 * D].reshape(2, D)
    inner_rows = vector_params[2 * D : 2 * D + 6 * INNER].reshape(6, INNER)
    cols = lax.dynamic_slice_in_dim(inner_rows, y * wide, wide, 1).T
    flat = (VECTOR // 128, 128)
    flat_params = vector_params.reshape(flat)

    low_first, cot_all, cot_other, cot_sums = call(
        prep_kernel,
        [((loc, D), bf16), ((col, T), bf16), ((col, half), bf16), ((col, 128), f32)],
        [idx],
        [w_first, cot],
    )
    got_first = swap_core(low_first)
    cot_opp = swap_y(cot_all)
    cot_sib = swap_core(cot_other)

    rows = 128
    steps = half // rows
    hid_one, hat_one, slope_one, scale_one = pl.pallas_call(
        input_kernel,
        out_shape=[
            jax.ShapeDtypeStruct((half, D), bf16),
            jax.ShapeDtypeStruct((half, D), bf16),
            jax.ShapeDtypeStruct((half, D), bf16),
            jax.ShapeDtypeStruct((half, 128), f32),
        ],
        grid_spec=pltpu.PrefetchScalarGridSpec(
            num_scalar_prefetch=1,
            grid=(steps,),
            in_specs=[
                pl.BlockSpec((rows, D), lambda i, idx: (idx[0] * steps + i, 0)),
                pl.BlockSpec((2, D), lambda i, idx: (0, 0)),
            ],
            out_specs=[
                pl.BlockSpec((rows, D), lambda i, idx: (i, 0)),
                pl.BlockSpec((rows, D), lambda i, idx: (i, 0)),
                pl.BlockSpec((rows, D), lambda i, idx: (i, 0)),
                pl.BlockSpec((rows, 128), lambda i, idx: (i, 0)),
            ],
        ),
        compiler_params=pltpu.CompilerParams(vmem_limit_bytes=16 * MIB),
        cost_estimate=pl.CostEstimate(flops=5000000000, bytes_accessed=1000, transcendentals=0),
    )(after(idx, cot_all, low_first), tokens, gain_shift)

    (low_rest,) = call(
        rest_kernel, [((loc, D + KERNEL_TAPS * INNER), bf16)], [], [w_last, w_taps]
    )
    got_rest = swap_core(low_rest)

    full_first, inner_one, st_two = call(
        first_kernel,
        [((wide, D), bf16), ((wide, half), f32), ((8, half), f32)],
        [idx],
        [low_first, got_first, hid_one, cols],
    )
    st_two_got = after(swap_y(st_two), cot_sib, cot_opp)
    (cot_diag,) = call(other_half_kernel, [((col, half), bf16)], [idx], [cot_opp])
    cot_diag = swap_core(cot_diag)
    slab = ((wide, REACH), bf16)
    own_in, own_out, hat_two, slope_two = call(
        second_kernel,
        [slab, slab, ((wide, half), f32), ((wide, half), f32)],
        [idx],
        [inner_one, st_two, st_two_got, cols, valid],
        scratch=[((wide, half), bf16)],
    )
    opp_in, opp_out = swap_y(own_in), swap_y(own_out)
    sib_in, seq_out = swap_core(own_in), swap_outer(own_out)
    sib_opp_in, seq_opp_out = swap_core(opp_in), swap_y(seq_out)
    ext, inner_two, st_three, full_last, full_taps, masks = call(
        functools.partial(conv_kernel, S * T),
        [
            ((INNER, half + 2 * REACH), bf16),
            ((wide, half), f32),
            ((8, half), f32),
            ((wide, D), bf16),
            ((wide, KERNEL_TAPS * INNER), bf16),
            ((8, half), f32),
        ],
        [idx, lengths],
        [
            own_in, own_out, opp_in, opp_out, sib_in, sib_opp_in, seq_out, seq_opp_out,
            low_rest, got_rest, cols,
        ],
        scratch=[((KERNEL_TAPS * INNER, half), bf16)],
    )
    st_three_got = swap_y(st_three)
    gw, g_three = call(
        cotangent_kernel,
        [((D, half), bf16), ((wide, half), f32)],
        [idx],
        [full_last, cot_all, cot_sib, cot_opp, cot_diag],
    )
    hid_three, e_three, hat_three, part_three = call(
        third_kernel,
        [((wide, half), bf16), ((wide, half), f32), ((wide, half), f32), ((8, half), f32)],
        [],
        [inner_two, st_three, st_three_got, cols, g_three],
    )
    part_three_got = swap_y(part_three)
    dz_two, slab_in, slab_out, sums_three = call(
        third_back_kernel,
        [((wide, half), bf16), ((wide, REACH), bf16), ((wide, REACH), bf16), ((wide, 128), f32)],
        [idx],
        [e_three, hat_three, part_three, part_three_got, cols],
    )
    got_in, got_out = swap_core(slab_in), swap_outer(slab_out)
    back_own, back_send = call(
        conv_back_kernel,
        [((wide, half), f32), ((wide, half), bf16)],
        [idx],
        [dz_two, got_in, got_out, masks, full_taps],
        scratch=[((wide, half + 2 * REACH), bf16), ((INNER, half), f32)],
    )
    back_got = swap_y(back_send)
    early_size = D + KERNEL_TAPS * INNER
    early_own, early_send = call(
        grads_kernel,
        [((loc, early_size), f32), ((loc, early_size), bf16)],
        [idx],
        [after(dz_two, back_send), ext, masks, hid_three, gw],
        scratch=[((wide, early_size), f32)],
        limit=32,
    )
    early_got = swap_core(early_send)
    unit, unit_low = ((loc, INNER), f32), ((loc, INNER), bf16)
    last_keep, last_send, taps_keep, taps_send = call(
        early_kernel,
        [unit, unit_low, ((loc, 2 * INNER + TAIL), f32), ((loc, 2 * INNER + TAIL), bf16)],
        [idx],
        [early_own, early_got],
    )
    last_got, taps_got = swap_x(last_send), swap_x(taps_send)
    e_two, part_two = call(
        second_back_kernel,
        [((wide, half), f32), ((8, half), f32)],
        [],
        [after(back_own, taps_send), back_got, slope_two, hat_two, cols],
    )
    half_out = [((half, HALF_D), f32), ((half, HALF_D), bf16)]
    branch_own, branch_send = call(
        halves_kernel, half_out, [idx], [after(hid_three, back_send), full_last], scratch=[((half, D), f32)]
    )
    part_two_got = after(swap_y(part_two), branch_send)
    branch_got = swap_y(after(branch_send, part_two_got))
    dz_one, first_own, first_send, sums_two = call(
        first_back_kernel,
        [((wide, half), bf16), ((loc, D), f32), ((loc, D), bf16), ((wide, 128), f32)],
        [idx],
        [e_two, hat_two, part_two, part_two_got, st_two, st_two_got, cols, hid_one],
        scratch=[((wide, D), f32)],
    )
    first_got = swap_core(first_send)
    first_keep, first_low = call(pair_kernel, [unit, unit_low], [idx], [first_own, first_got])
    first_low = after(first_low, taps_got)
    first_got = swap_x(first_low)

    span = H
    while span > 4:
        span //= 2
        fold = [(i + span, i) for i in range(span)]

        def folded(keep, got):
            total = keep + got.astype(f32)
            return total + along_h(total.astype(bf16), fold).astype(f32), jnp.zeros_like(got)

        first_keep, first_got = folded(first_keep, first_got)
        last_keep, last_got = folded(last_keep, last_got)
        taps_keep, taps_got = folded(taps_keep, taps_got)
    line = 4

    size_taps = (loc, INNER + TAIL)
    sum_taps, send_taps = call(
        taps_kernel, [((loc, 2 * INNER + TAIL), f32), (size_taps, bf16)], [idx], [taps_keep, taps_got]
    )
    got_taps = along_h(send_taps, [(i, i ^ 1) for i in range(line)])
    tail_low = ((loc, TAIL), bf16)
    part_unit, part_tail, *sends, tail_send = call(
        line_kernel,
        [unit, ((loc, TAIL), f32), unit_low, unit_low, unit_low, tail_low],
        [idx],
        [first_keep, first_got, last_keep, last_got, sum_taps, got_taps],
    )
    got_units = [along_h(v, pairs) for v, pairs in zip(sends, LINE)]
    got_tail = along_h(tail_send, LINE_TAIL)
    back_own, back_send = call(
        halves_kernel, half_out, [idx], [after(dz_one, part_unit), full_first], scratch=[((half, D), f32)]
    )
    back_got = swap_y(back_send)
    def whole_block(shape):
        return pl.BlockSpec(shape, lambda i, idx: (0, 0))

    out_mine, out_send, squares = pl.pallas_call(
        output_kernel,
        out_shape=[
            jax.ShapeDtypeStruct((col, half), f32),
            jax.ShapeDtypeStruct((col, half), f32),
            jax.ShapeDtypeStruct((8, 128), f32),
        ],
        grid_spec=pltpu.PrefetchScalarGridSpec(
            num_scalar_prefetch=1,
            grid=(1,),
            in_specs=[
                whole_block((half, HALF_D)),
                whole_block((half, HALF_D)),
                pl.BlockSpec((half, HALF_D), lambda i, idx: (idx[0], idx[1])),
                whole_block((VECTOR // 128, 128)),
                whole_block((1, T)),
            ],
            out_specs=[whole_block((col, half)), whole_block((col, half)), whole_block((8, 128))],
            scratch_shapes=[pltpu.VMEM((HALF_D, half), f32)],
        ),
        compiler_params=pltpu.CompilerParams(vmem_limit_bytes=24 * MIB),
        cost_estimate=pl.CostEstimate(flops=1000, bytes_accessed=1000, transcendentals=0),
    )(idx, branch_own, branch_got, tokens, flat_params, valid)
    e_one, part_one, sums_one = call(
        token_kernel,
        [((half, HALF_D), f32), ((half, 128), f32), ((8, HALF_D), f32)],
        [idx],
        [back_own, back_got, slope_one, hat_one, gain_shift],
    )
    (part_one,) = call(flip_kernel, [((8, half), f32)], [], [part_one])
    (vector,) = call(
        vector_kernel, [((ROWS, INNER), f32)], [idx], [sums_two, sums_three, sums_one, cot_sums, squares]
    )
    (old_unit,) = call(own_kernel, [(size_taps, f32)], [idx], [m_first, m_taps, m_last])
    sum_unit, sum_tail, new_unit, cross = call(
        finish_kernel,
        [unit_low, tail_low, (size_taps, bf16), unit_low],
        [idx],
        [old_unit, part_unit, part_tail, *got_units, got_tail],
    )
    cross_got = swap_x(after(cross, squares, back_got))
    (block,) = call(block_kernel, [((loc, D), bf16)], [idx], [new_unit, cross_got])

    def far_along_z(unit, tail):
        return along_h(unit, [(i, i ^ 2) for i in range(4)]), along_h(tail, LINE_TAIL)

    sum_far, tail_far = far_along_z(sum_unit, sum_tail)
    block_sib, block_opp = swap_core(block), swap_y(block)
    block_diag = swap_core(after(block_opp, sum_far, tail_far, vector))

    def joined_with(unit, got, tail, tail_got):
        return call(
            join_kernel, [((loc, 2 * INNER + TAIL), bf16)], [idx], [unit, got, tail, tail_got]
        )[0]

    def next_along_z(joined):
        return along_h(joined, [(i, i ^ 1) for i in range(4)])

    def spread(parts):
        span = 4
        while span < H:
            pairs = [(i, i + span) for i in range(span)]
            parts = [jnp.where((h >= span) & (h < 2 * span), along_h(v, pairs), v) for v in parts]
            span *= 2
        return parts

    def apply(keep, rate_long, rate_tap, parts, first, taps, last):
        return call(
            functools.partial(apply_kernel, keep, rate_long, rate_tap),
            [((loc, D), f32), ((KERNEL_TAPS, loc, INNER), f32), ((loc, D), f32)],
            [idx],
            [*parts, first, taps, last],
            limit=32,
        )

    joined = joined_with(sum_unit, sum_far, sum_tail, tail_far)
    vector_x = swap_x(vector)
    mine, theirs = call(
        ortho_kernel,
        [((loc, D), bf16), ((loc, INNER), bf16)],
        [idx],
        [after(block, joined, vector_x), block_sib, block_opp, block_diag],
        scratch=[
            ((INNER, D), f32),
            ((INNER, D), bf16),
            ((INNER, INNER), bf16),
            ((INNER, INNER), f32),
            ((INNER, INNER), bf16),
            ((INNER, INNER), bf16),
        ],
        limit=32,
        flops=14 * 10**9,
    )
    joined_x = swap_x(joined)
    other = next_along_z(joined)
    part_got = swap_y(part_one)
    vector = vector + vector_x
    vector_core = swap_core(vector)
    theirs_got = swap_core(theirs)
    step_unit, step_tail = call(
        step_kernel, [unit_low, ((loc, TAIL), bf16)], [idx], [after(mine, joined_x, other, vector_core, part_got), theirs_got]
    )
    other_x = swap_x(after(other, step_unit))
    mom_parts = spread([joined, joined_x, other, other_x])

    vector = vector + vector_core
    vector = vector + swap_y(vector)
    step_far, tail_far = far_along_z(step_unit, step_tail)
    grad_mine, grad_send = call(
        token_back_kernel,
        [((col, half), f32), ((col, half), f32)],
        [idx],
        [after(e_one, step_unit), hat_one, scale_one, part_one, part_got],
        scratch=[((half, HALF_D), f32), ((HALF_D, half), f32)],
    )
    joined = joined_with(after(step_unit, vector, other_x, grad_send), step_far, step_tail, tail_far)
    joined_x = swap_x(joined)
    other = after(next_along_z(joined), joined_x)

    grad_got, out_got = swap_core(grad_send), swap_core(out_send)
    vector = vector + lax.ppermute(vector, "seq", [(i, i ^ 2) for i in range(S)])
    other, vector, grad_got, out_got = lax.optimization_barrier((other, vector, grad_got, out_got))
    other_x = swap_x(other)
    bit = 4
    while bit < S:
        vector = vector + lax.ppermute(vector, "seq", [(i, i ^ bit) for i in range(S)])
        bit *= 2
    (block_output,) = call(place_kernel, [((col, T), f32)], [idx], [out_mine, out_got])
    (tokens_grad,) = call(place_add_kernel, [((col, T), f32)], [idx], [grad_mine, grad_got, cot])
    vector_first, vector_second, vector_values, root = call(
        adam_kernel,
        [(flat, f32)] * 3 + [((8, 128), f32)],
        [],
        [vector, flat_params, vector_moment.reshape(flat), vector_square.reshape(flat)],
        scratch=[((12, INNER), f32)],
    )
    vector_first, vector_second, vector_values = (
        v.reshape(VECTOR) for v in (vector_first, vector_second, vector_values)
    )
    root_means = root[:2, 0]
    new_first, new_taps, new_last = apply(
        muon_keep, 1.0, 1.0, [after(mom_parts[0], other), *mom_parts[1:]], m_first, m_taps, m_last
    )
    keep_weight = 1.0 - muon_rate * decay_rate
    rate = muon_rate * muon_scale
    out_first, out_taps, out_last = apply(
        keep_weight,
        -rate * math.sqrt(D),
        -rate * math.sqrt(INNER),
        spread([joined, joined_x, other, other_x]),
        w_first,
        w_taps,
        w_last,
    )
    return (
        block_output.T,
        tokens_grad.T,
        out_first.T,
        jnp.swapaxes(out_taps, 1, 2),
        out_last,
        new_first.T,
        jnp.swapaxes(new_taps, 1, 2),
        new_last,
        vector_first,
        vector_second,
        vector_values,
        root_means,
    )


def solution(mesh):
    placed = (
        P("seq", None),
        P("seq", "ch"),
        P(),
        P("seq"),
        P(None, "ch"),
        P(None, None, "ch"),
        P("ch", None),
        P(None, "ch"),
        P(None, None, "ch"),
        P("ch", None),
        P(),
        P(),
        P(),
    )
    return jax.shard_map(
        body,
        mesh=mesh,
        in_specs=placed,
        out_specs=(
            P("seq", "ch"),
            P("seq", "ch"),
            P(None, "ch"),
            P(None, None, "ch"),
            P("ch", None),
            P(None, "ch"),
            P(None, None, "ch"),
            P("ch", None),
            P(),
            P(),
            P(),
            P(),
        ),
        check_vma=False,
    )
```

```python
import functools
import math

import jax
import jax.numpy as jnp
from jax import lax
from jax.experimental import pallas as pl
from jax.experimental.pallas import tpu as pltpu
from jax.sharding import PartitionSpec as P

D = 1280
INNER = 640
KERNEL_TAPS = 5
DILATION_SPAN = 128
STEP = 10

norm_eps = 1e-05
coef_first = 3.4445
coef_second = -4.775
coef_third = 2.0315
adam_rate = 0.4
adam_first = 0.9
adam_second = 0.999
adam_eps = 1e-08
decay_rate = 0.01
muon_rate = 0.1
muon_keep = 0.95
muon_scale = 0.2
REACH = KERNEL_TAPS // 2 * DILATION_SPAN
VECTOR = 3 * D + 6 * INNER
HALF_D = D // 2
MIB = 1024 * 1024

f32 = jnp.float32
bf16 = jnp.bfloat16
NN = (((1,), (0,)), ((), ()))
NT = (((1,), (1,)), ((), ()))
TN = (((0,), (0,)), ((), ()))


def mul(a, b, dims):
    return lax.dot_general(a, b, dims, preferred_element_type=f32)


def erf_parts(v):
    a = jnp.abs(v) * math.sqrt(0.5)
    t = pl.reciprocal(1.0 + 0.3275911 * a)
    e = jnp.exp(-a * a)
    p = t * (0.254829592 + t * (-0.284496736 + t * (1.421413741 + t * (-1.453152027 + t * 1.061405429))))
    tail = 0.5 * p * e
    return jnp.where(v >= 0, 1.0 - tail, tail), e


def gelu_pair(v):
    cdf, e = erf_parts(v)
    return v * cdf, cdf + v * e * (1.0 / math.sqrt(2.0 * math.pi))


VMEM = pl.BlockSpec(memory_space=pltpu.VMEM)
SMEM = pl.BlockSpec(memory_space=pltpu.SMEM)


def call(kernel, outs, scalars, arrays, scratch=(), limit=16, flops=1000):
    shapes = [jax.ShapeDtypeStruct(shape, dtype) for shape, dtype in outs]
    return pl.pallas_call(
        kernel,
        out_shape=shapes,
        in_specs=[SMEM] * len(scalars) + [VMEM] * len(arrays),
        out_specs=[VMEM] * len(outs),
        scratch_shapes=[pltpu.VMEM(shape, dtype) for shape, dtype in scratch],
        compiler_params=pltpu.CompilerParams(vmem_limit_bytes=limit * MIB),
        cost_estimate=pl.CostEstimate(flops=flops, bytes_accessed=1000, transcendentals=0),
    )(*scalars, *arrays)


def chunks(count, step):
    return [pl.ds(i, step) for i in range(0, count, step)]


def at(index, count, step=32):
    return pl.ds(pl.multiple_of(index * count, step), count)


def prep_kernel(idx, w_ref, cot_ref, wo_ref, all_ref, other_ref, sums_ref):
    half = other_ref.shape[1]
    for r in chunks(cot_ref.shape[0], 32):
        v = cot_ref[r, :]
        all_ref[r, :] = v.astype(bf16)
        other_ref[r, :] = cot_ref[r, at(1 - idx[0], half, 128)].astype(bf16)
        sums_ref[r, :] = jnp.broadcast_to(jnp.sum(v, axis=1, keepdims=True), (32, 128))
    for r in chunks(w_ref.shape[0], 32):
        wo_ref[r, :] = w_ref[r, :].astype(bf16)


def rest_kernel(last_ref, taps_ref, o_ref):
    for r in chunks(last_ref.shape[0], 32):
        o_ref[r, :D] = last_ref[r, :].astype(bf16)
        for j in range(KERNEL_TAPS):
            o_ref[r, D + j * INNER : D + (j + 1) * INNER] = taps_ref[j, r, :].astype(bf16)


def input_kernel(idx, tok_ref, gs_ref, hid_ref, hat_ref, slope_ref, scale_ref):
    for r in chunks(tok_ref.shape[0], 16):
        v = tok_ref[r, :]
        center = jnp.sum(v, axis=1, keepdims=True) * (1.0 / D)
        square = jnp.sum(v * v, axis=1, keepdims=True) * (1.0 / D)
        scale = lax.rsqrt(square - center * center + norm_eps)
        hat = (v - center) * scale
        hid, slope = gelu_pair(hat * gs_ref[0:1, :] + gs_ref[1:2, :])
        hid_ref[r, :] = hid.astype(bf16)
        hat_ref[r, :] = hat.astype(bf16)
        slope_ref[r, :] = slope.astype(bf16)
        scale_ref[r, :] = jnp.broadcast_to(scale, (16, 128))


def put_stats(ref, parts):
    for i, part in enumerate(parts):
        ref[i : i + 1, :] = part


def first_kernel(idx, own_ref, got_ref, hid_ref, cols_ref, w_ref, inner_ref, st_ref):
    k = idx[0]
    loc = own_ref.shape[0]
    w_ref[at(k, loc), :] = own_ref[...]
    w_ref[at(1 - k, loc), :] = got_ref[...]
    v = mul(w_ref[...], hid_ref[...], NT) + cols_ref[:, 0:1]
    inner_ref[...] = v
    put_stats(st_ref, (jnp.sum(v, axis=0, keepdims=True), jnp.sum(v * v, axis=0, keepdims=True)))


def center_scale(st_ref, got_ref):
    center = (st_ref[0:1, :] + got_ref[0:1, :]) * (1.0 / INNER)
    square = (st_ref[1:2, :] + got_ref[1:2, :]) * (1.0 / INNER)
    return center, lax.rsqrt(square - center * center + norm_eps)


def second_kernel(
    idx, inner_ref, st_ref, got_ref, cols_ref, valid_ref, in_ref, out_ref, hat_ref, slope_ref, hid_ref
):
    center, scale = center_scale(st_ref, got_ref)
    valid = valid_ref[:, at(idx[0], hid_ref.shape[1], 128)].astype(f32)
    for r in chunks(inner_ref.shape[0], 32):
        hat = (inner_ref[r, :] - center) * scale
        hid, slope = gelu_pair(hat * cols_ref[r, 1:2] + cols_ref[r, 2:3])
        hid_ref[r, :] = (hid * valid).astype(bf16)
        hat_ref[r, :] = hat
        slope_ref[r, :] = slope * valid
    slabs_of(idx[0], hid_ref, slice(None), in_ref, out_ref)


def slabs_of(k, v_ref, row, in_ref, out_ref):
    half = v_ref.shape[1]
    rows = v_ref.shape[0]
    in_ref[row, :] = v_ref[:, at(1 - k, half - REACH, 128)]
    out_ref[row, :] = v_ref[:, at(k, half - REACH, 128)]


def fill_reach(k, ext_ref, in_ref, out_ref, half):
    @pl.when(k == 0)
    def _():
        ext_ref[:, :REACH] = out_ref[...]
        ext_ref[:, REACH + half :] = in_ref[...]

    @pl.when(k == 1)
    def _():
        ext_ref[:, :REACH] = in_ref[...]
        ext_ref[:, REACH + half :] = out_ref[...]


def conv_kernel(
    total, idx, lengths, own_in, own_out, opp_in, opp_out, sib_in, sib_opp_in, seq_out, seq_opp_out,
    wo_ref, wg_ref, cols_ref, ext_ref, inner_ref, st_ref, last_ref, taps_ref, mask_ref, stack,
):
    k, y = idx[0], idx[1]
    wide, reach = own_in.shape
    half = 2 * reach
    loc = wo_ref.shape[0]
    for q in range(2):
        @pl.when(k == q)
        def _():
            for place, (mine, other) in enumerate(
                ((seq_out, seq_opp_out), (own_out, opp_out), (own_in, opp_in), (sib_in, sib_opp_in))
            ):
                place = 3 - place if q else place
                lanes = slice(place * reach, (place + 1) * reach)
                ext_ref[at(y, wide), lanes] = mine[...]
                ext_ref[at(1 - y, wide), lanes] = other[...]

    last_ref[at(k, loc), :] = wo_ref[:, :D]
    last_ref[at(1 - k, loc), :] = wg_ref[:, :D]
    taps_ref[at(k, loc), :] = wo_ref[:, D:]
    taps_ref[at(1 - k, loc), :] = wg_ref[:, D:]
    positions = idx[5] - REACH + lax.broadcasted_iota(jnp.int32, (1, half + 2 * REACH), 1)
    segment = jnp.zeros_like(positions)
    bound = jnp.int32(0)
    for i in range(lengths.shape[0]):
        bound = bound + lengths[i]
        segment = segment + (positions >= bound).astype(jnp.int32)
    segment = jnp.where((positions >= 0) & (positions < total), segment, -1)
    centre = segment[:, REACH : REACH + half]
    for j in range(KERNEL_TAPS):
        lanes = slice(j * DILATION_SPAN, j * DILATION_SPAN + half)
        mask = (segment[:, lanes] == centre).astype(f32)
        mask_ref[j : j + 1, :] = mask
        low = mask.astype(bf16)
        for i in range(0, INNER, 160):
            stack[j * INNER + i : j * INNER + i + 160, :] = ext_ref[i : i + 160, lanes] * low
    v = mul(taps_ref[...], stack[...], NN) + cols_ref[:, 3:4]
    inner_ref[...] = v
    put_stats(st_ref, (jnp.sum(v, axis=0, keepdims=True), jnp.sum(v * v, axis=0, keepdims=True)))


def cotangent_kernel(idx, last_ref, all_ref, sib_ref, opp_ref, diag_ref, gw_ref, g_ref):
    k, y = idx[0], idx[1]
    col, half = sib_ref.shape
    mine = at(k, half, 128)
    gw_ref[at(2 * y + k, col), :] = all_ref[:, mine]
    gw_ref[at(2 * y + 1 - k, col), :] = sib_ref[...]
    gw_ref[at(2 * (1 - y) + k, col), :] = opp_ref[:, mine]
    gw_ref[at(2 * (1 - y) + 1 - k, col), :] = diag_ref[...]
    g_ref[...] = mul(last_ref[...], gw_ref[...], NN)


def other_half_kernel(idx, all_ref, o_ref):
    o_ref[...] = all_ref[:, at(1 - idx[0], o_ref.shape[1], 128)]


def third_kernel(inner_ref, st_ref, got_ref, cols_ref, g_ref, hid_ref, e_ref, hat_ref, part_ref):
    center, scale = center_scale(st_ref, got_ref)
    plain = jnp.zeros_like(center)
    cross = jnp.zeros_like(center)
    for r in chunks(inner_ref.shape[0], 32):
        hat = (inner_ref[r, :] - center) * scale
        gain = cols_ref[r, 4:5]
        hid, slope = gelu_pair(hat * gain + cols_ref[r, 5:6])
        hid_ref[r, :] = hid.astype(bf16)
        hat_ref[r, :] = hat
        e = slope * g_ref[r, :]
        e_ref[r, :] = e
        eg = e * gain
        plain = plain + jnp.sum(eg, axis=0, keepdims=True)
        cross = cross + jnp.sum(eg * hat, axis=0, keepdims=True)
    put_stats(part_ref, (plain, cross, scale))


def norm_back(r, e_ref, hat_ref, part_ref, got_ref, scale, gain, sums_ref):
    plain = (part_ref[0:1, :] + got_ref[0:1, :]) * (1.0 / INNER)
    cross = (part_ref[1:2, :] + got_ref[1:2, :]) * (1.0 / INNER)
    e, hat = e_ref[r, :], hat_ref[r, :]
    grad = scale * (e * gain - plain - hat * cross)
    sums_ref[r, 0:1] = jnp.sum(e * hat, axis=1, keepdims=True)
    sums_ref[r, 1:2] = jnp.sum(e, axis=1, keepdims=True)
    sums_ref[r, 2:3] = jnp.sum(grad, axis=1, keepdims=True)
    return grad


def third_back_kernel(idx, e_ref, hat_ref, part_ref, got_ref, cols_ref, dz_ref, in_ref, out_ref, sums_ref):
    for r in chunks(e_ref.shape[0], 32):
        grad = norm_back(r, e_ref, hat_ref, part_ref, got_ref, part_ref[2:3, :], cols_ref[r, 4:5], sums_ref)
        dz_ref[r, :] = grad.astype(bf16)
    slabs_of(idx[0], dz_ref, slice(None), in_ref, out_ref)


def split_rows(k, full, own_ref, send_ref, lanes):
    loc = own_ref.shape[0]
    own_ref[:, lanes] = full[at(k, loc), lanes]
    send_ref[:, lanes] = full[at(1 - k, loc), lanes].astype(bf16)


def grads_kernel(idx, dz_ref, ext_ref, mask_ref, hid_ref, gw_ref, own_ref, send_ref, full):
    k = idx[0]
    half = dz_ref.shape[1]
    full[:, :D] = mul(hid_ref[...], gw_ref[...], NT)
    split_rows(k, full, own_ref, send_ref, slice(0, D))
    for j in range(KERNEL_TAPS):
        masked = dz_ref[...] * mask_ref[j : j + 1, :].astype(bf16)
        moved = ext_ref[:, j * DILATION_SPAN : j * DILATION_SPAN + half]
        lanes = slice(D + j * INNER, D + (j + 1) * INNER)
        full[:, lanes] = mul(masked, moved, NT)
        split_rows(k, full, own_ref, send_ref, lanes)


def conv_back_kernel(idx, dz_ref, in_ref, out_ref, mask_ref, taps_ref, own_ref, send_ref, ext, full):
    k, y = idx[0], idx[1]
    wide, half = dz_ref.shape
    ext[:, REACH : REACH + half] = dz_ref[...]
    fill_reach(k, ext, in_ref, out_ref, half)
    total = None
    for j in range(KERNEL_TAPS):
        begin = REACH - (j - KERNEL_TAPS // 2) * DILATION_SPAN
        mask = mask_ref[KERNEL_TAPS - 1 - j : KERNEL_TAPS - j, :].astype(bf16)
        part = mul(taps_ref[:, j * INNER : (j + 1) * INNER], ext[:, begin : begin + half] * mask, TN)
        total = part if total is None else total + part
    full[...] = total
    own_ref[...] = full[at(y, wide), :]
    send_ref[...] = full[at(1 - y, wide), :].astype(bf16)


def second_back_kernel(own_ref, got_ref, slope_ref, hat_ref, cols_ref, e_ref, part_ref):
    plain = jnp.zeros((1, own_ref.shape[1]), f32)
    cross = jnp.zeros_like(plain)
    for r in chunks(own_ref.shape[0], 32):
        e = slope_ref[r, :] * (own_ref[r, :] + got_ref[r, :].astype(f32))
        e_ref[r, :] = e
        eg = e * cols_ref[r, 1:2]
        plain = plain + jnp.sum(eg, axis=0, keepdims=True)
        cross = cross + jnp.sum(eg * hat_ref[r, :], axis=0, keepdims=True)
    put_stats(part_ref, (plain, cross))


def first_back_kernel(
    idx, e_ref, hat_ref, part_ref, got_ref, st_ref, stg_ref, cols_ref, hid_ref,
    dz_ref, own_ref, send_ref, sums_ref, full,
):
    _, scale = center_scale(st_ref, stg_ref)
    for r in chunks(e_ref.shape[0], 32):
        grad = norm_back(r, e_ref, hat_ref, part_ref, got_ref, scale, cols_ref[r, 1:2], sums_ref)
        dz_ref[r, :] = grad.astype(bf16)
    full[...] = mul(dz_ref[...], hid_ref[...], NN)
    split_rows(idx[0], full, own_ref, send_ref, slice(0, D))


def halves_kernel(idx, z_ref, w_ref, own_ref, send_ref, full):
    y = idx[1]
    full[...] = mul(z_ref[...], w_ref[...], TN)
    for r in chunks(full.shape[0], 64):
        own_ref[r, :] = full[r, at(y, HALF_D, 128)]
        send_ref[r, :] = full[r, at(1 - y, HALF_D, 128)].astype(bf16)


def column_halves(k, flipped, mine_ref, send_ref, full):
    col = mine_ref.shape[0]
    full[...] = flipped
    mine_ref[...] = full[at(k, col), :]
    send_ref[...] = full[at(1 - k, col), :]


def output_kernel(idx, own_ref, got_ref, tok_ref, flat_ref, valid_ref, mine_ref, send_ref, sq_ref, full):
    k, y = idx[0], idx[1]
    half = own_ref.shape[0]
    per = HALF_D // 128
    first = (2 * D + 6 * INNER) // 128 + per * y
    bias = jnp.concatenate([flat_ref[pl.ds(first + q, 1), :] for q in range(per)], axis=1)
    branch = own_ref[...] + got_ref[...].astype(f32) + bias
    out = tok_ref[...] + branch
    valid = valid_ref[:, at(k, half, 128)].astype(f32)
    sq_ref[0:1, :] = jnp.sum(valid * mul_rows(out), axis=1, keepdims=True) * jnp.ones((1, 128), f32)
    sq_ref[1:2, :] = jnp.sum(valid * mul_rows(branch), axis=1, keepdims=True) * jnp.ones((1, 128), f32)
    sq_ref[2:3, :] = jnp.sum(valid, axis=1, keepdims=True) * jnp.full((1, 128), 0.5, f32)
    sq_ref[3:8, :] = jnp.zeros((5, 128), f32)
    column_halves(k, out.T, mine_ref, send_ref, full)


def mul_rows(v):
    rows = jnp.sum(v * v, axis=1, keepdims=True)
    return jnp.broadcast_to(rows, (v.shape[0], 128)).T[0:1, :]


def token_kernel(idx, own_ref, got_ref, slope_ref, hat_ref, gs_ref, e_ref, part_ref, sums_ref):
    y = idx[1]
    cols = at(y, HALF_D, 128)
    gain = gs_ref[0:1, cols]
    sum_cross = jnp.zeros((1, HALF_D), f32)
    sum_plain = jnp.zeros((1, HALF_D), f32)
    for r in chunks(own_ref.shape[0], 32):
        e = slope_ref[r, cols].astype(f32) * (own_ref[r, :] + got_ref[r, :].astype(f32))
        hat = hat_ref[r, cols].astype(f32)
        eg = e * gain
        e_ref[r, :] = eg
        part_ref[r, 0:1] = jnp.sum(eg, axis=1, keepdims=True)
        part_ref[r, 1:2] = jnp.sum(eg * hat, axis=1, keepdims=True)
        sum_cross = sum_cross + jnp.sum(e * hat, axis=0, keepdims=True)
        sum_plain = sum_plain + jnp.sum(e, axis=0, keepdims=True)
    put_stats(sums_ref, (sum_cross, sum_plain))


def flip_kernel(part_ref, o_ref):
    o_ref[...] = part_ref[...].T[0:8, :]


def token_back_kernel(idx, e_ref, hat_ref, scale_ref, part_ref, got_ref, mine_ref, send_ref, rows, full):
    cols = at(idx[1], HALF_D, 128)
    means = ((part_ref[...] + got_ref[...]) * (1.0 / D)).T
    for r in range(0, e_ref.shape[0], 64):
        s = slice(r, r + 64)
        hat = hat_ref[s, cols].astype(f32)
        rows[s, :] = scale_ref[s, 0:1] * (e_ref[s, :] - means[s, 0:1] - hat * means[s, 1:2])
    column_halves(idx[0], rows[...].T, mine_ref, send_ref, full)


def place_kernel(idx, mine_ref, got_ref, o_ref):
    half = mine_ref.shape[1]
    o_ref[:, at(idx[0], half, 128)] = mine_ref[...]
    o_ref[:, at(1 - idx[0], half, 128)] = got_ref[...]


def place_add_kernel(idx, mine_ref, got_ref, base_ref, o_ref):
    half = mine_ref.shape[1]
    mine, other = at(idx[0], half, 128), at(1 - idx[0], half, 128)
    o_ref[:, mine] = base_ref[:, mine] + mine_ref[...]
    o_ref[:, other] = base_ref[:, other] + got_ref[...]


TAIL = INNER // 2


def tap_columns(b):
    return ((D + b * INNER, INNER), (D + (2 + b) * INNER, INNER), (D + 4 * INNER + b * TAIL, TAIL))


def pair_columns(own_ref, got_ref, keep_ref, send_ref, mine, other):
    to = 0
    for (m, count), (o, _n) in zip(mine, other):
        for r in chunks(own_ref.shape[0], 32):
            keep_ref[r, to : to + count] = own_ref[r, m : m + count] + got_ref[r, m : m + count].astype(f32)
            send_ref[r, to : to + count] = (
                own_ref[r, o : o + count] + got_ref[r, o : o + count].astype(f32)
            ).astype(bf16)
        to += count


def early_kernel(idx, own_ref, got_ref, keep_last, send_last, keep_taps, send_taps):
    for b in range(2):

        @pl.when(idx[2] == b)
        def _():
            pair_columns(own_ref, got_ref, keep_last, send_last, [(b * INNER, INNER)], [((1 - b) * INNER, INNER)])
            pair_columns(own_ref, got_ref, keep_taps, send_taps, tap_columns(b), tap_columns(1 - b))


def pair_kernel(idx, own_ref, got_ref, keep_ref, send_ref):
    for b in range(2):

        @pl.when(idx[2] == b)
        def _():
            pair_columns(own_ref, got_ref, keep_ref, send_ref, [(b * INNER, INNER)], [((1 - b) * INNER, INNER)])


def taps_kernel(idx, keep_ref, got_ref, sum_ref, send_ref):
    for r in chunks(keep_ref.shape[0], 32):
        sum_ref[r, :] = keep_ref[r, :] + got_ref[r, :].astype(f32)

    @pl.when(idx[3] % 2 == 0)
    def _():
        send_ref[...] = sum_ref[:, INNER:].astype(bf16)

    @pl.when(idx[3] % 2 == 1)
    def _():
        send_ref[:, :INNER] = sum_ref[:, :INNER].astype(bf16)
        send_ref[:, INNER:] = jnp.zeros_like(send_ref[:, INNER:])


LINE = (
    ((0, 0), (1, 3), (2, 1), (3, 2)),
    ((0, 2), (1, 0), (2, 3), (3, 1)),
    ((0, 1), (1, 2), (2, 0), (3, 3)),
)
LINE_TAIL = ((0, 0), (1, 3), (2, 2), (3, 1))


def line_kernel(
    idx, keep_f, got_f, keep_l, got_l, taps_ref, taps_got,
    part_ref, tail_part, one_ref, two_ref, three_ref, tail_ref,
):
    h = idx[3]
    first = keep_f[...] + got_f[...].astype(f32)
    last = keep_l[...] + got_l[...].astype(f32)
    even = taps_ref[:, :INNER] + taps_got[:, :INNER].astype(f32)
    odd = taps_ref[:, INNER : 2 * INNER] + taps_got[:, :INNER].astype(f32)
    tail = taps_ref[:, 2 * INNER :] + taps_got[:, INNER:].astype(f32)
    low_first, low_last = first.astype(bf16), last.astype(bf16)
    tail_part[...] = tail
    tail_ref[...] = tail.astype(bf16)

    @pl.when(h == 0)
    def _():
        part_ref[...] = even
        one_ref[...] = low_first
        two_ref[...] = low_last
        three_ref[...] = low_first

    @pl.when(h == 1)
    def _():
        part_ref[...] = first
        one_ref[...] = odd.astype(bf16)
        two_ref[...] = low_last
        three_ref[...] = low_last

    @pl.when(h == 2)
    def _():
        part_ref[...] = last
        one_ref[...] = low_first
        two_ref[...] = low_first
        three_ref[...] = even.astype(bf16)

    @pl.when(h >= 3)
    def _():
        part_ref[...] = odd
        one_ref[...] = low_last
        two_ref[...] = low_first
        three_ref[...] = low_last


def own_kernel(idx, first_ref, taps_ref, last_ref, unit_ref):
    h, b = idx[3], idx[2]
    unit_ref[:, INNER:] = jnp.zeros_like(unit_ref[:, INNER:])
    for i in range(2):

        @pl.when((h == 0) & (b == i))
        def _():
            unit_ref[:, :INNER] = taps_ref[i]

        @pl.when((h == 1) & (b == i))
        def _():
            unit_ref[:, :INNER] = first_ref[:, i * INNER : (i + 1) * INNER]

        @pl.when((h == 2) & (b == i))
        def _():
            unit_ref[:, :INNER] = last_ref[:, i * INNER : (i + 1) * INNER]

        @pl.when((h == 3) & (b == i))
        def _():
            unit_ref[:, :INNER] = taps_ref[2 + i]
            unit_ref[:, INNER:] = taps_ref[4, :, i * TAIL : (i + 1) * TAIL]

    @pl.when(h > 3)
    def _():
        unit_ref[...] = jnp.zeros_like(unit_ref)


def finish_kernel(
    idx, old_ref, part_ref, tail_part, one_got, two_got, three_got, tail_got,
    sum_ref, tail_ref, new_ref, cross_ref,
):
    h = idx[3]

    def put(v):
        sum_ref[...] = v.astype(bf16)
        new_ref[:, :INNER] = (muon_keep * old_ref[:, :INNER] + v).astype(bf16)

    @pl.when(h == 0)
    def _():
        put(part_ref[...] + three_got[...].astype(f32))

    @pl.when((h == 1) | (h == 2))
    def _():
        put(part_ref[...] + one_got[...].astype(f32) + two_got[...].astype(f32) + three_got[...].astype(f32))

    @pl.when(h >= 3)
    def _():
        put(part_ref[...] + one_got[...].astype(f32))

    tail = tail_part[...] + tail_got[...].astype(f32)
    tail_ref[...] = tail.astype(bf16)
    new_ref[:, INNER:] = (muon_keep * old_ref[:, INNER:] + tail).astype(bf16)

    @pl.when(h == 3)
    def _():
        cross_ref[:, :TAIL] = new_ref[:, INNER:]
        cross_ref[:, TAIL:] = new_ref[:, INNER:]

    @pl.when(h != 3)
    def _():
        cross_ref[...] = new_ref[:, :INNER]


def block_kernel(idx, new_ref, got_ref, o_ref):
    h, b = idx[3], idx[2]
    long = (h == 1) | (h == 2)
    for i in range(2):

        @pl.when(long & (b == i))
        def _():
            o_ref[:, i * INNER : (i + 1) * INNER] = new_ref[:, :INNER]
            o_ref[:, (1 - i) * INNER : (2 - i) * INNER] = got_ref[...]

        @pl.when(jnp.logical_not(long) & (b == i))
        def _():
            o_ref[:, :INNER] = new_ref[:, :INNER]
            o_ref[:, INNER + i * TAIL : INNER + (i + 1) * TAIL] = new_ref[:, INNER:]
            o_ref[:, INNER + (1 - i) * TAIL : INNER + (2 - i) * TAIL] = got_ref[:, :TAIL]


def sweep(X, Xh, Xl, A, Bh, Rh, width, low, last, carry):
    scale, squares = carry
    n = X.shape[0]
    alpha = squares * scale * scale * (1.0 / n)
    outer = scale * scale
    rest = coef_second + 2.0 * coef_third * alpha
    keep = (coef_first + coef_second * alpha + coef_third * alpha * alpha) * scale
    if low:
        Bl = mul(Xh[:, :width], Xl[:, :width], NT)
        A[...] = Bl + Bl.T
    blocks = [(i, min(i + 256, n)) for i in range(0, n, 256)]
    for i, e in blocks:
        a = mul(Xh[i:e, :width], Xh[i:, :width], NT)
        if low:
            a = a + A[i:e, i:]
        row = lax.broadcasted_iota(jnp.int32, a.shape, 0)
        col = lax.broadcasted_iota(jnp.int32, a.shape, 1)
        a = a * outer - jnp.where(row == col, alpha, 0.0)
        A[i:e, i:] = a
        Bh[i:e, i:] = a.astype(bf16)
        if e < n:
            Bh[e:, i:e] = a[:, e - i :].T.astype(bf16)
    for i, e in blocks:
        p = rest * A[i:e, i:] + coef_third * mul(Bh[i:e, :], Bh[:, i:], NN)
        Rh[i:e, i:] = p.astype(bf16)
        if e < n:
            Rh[e:, i:e] = p[:, e - i :].T.astype(bf16)
    total = jnp.zeros((8, 128), f32)
    for i in range(0, width, 256):
        c = slice(i, min(i + 256, width))
        v = keep * X[:, c] + scale * mul(Rh[...], Xh[:, c], NN)
        X[:, c] = v
        Xh[:, c] = v.astype(bf16)
        if last is not None:
            Xl[:, c] = (v - Xh[:, c].astype(f32)).astype(bf16)
        for q in range(0, c.stop - c.start, 128):
            w = v[:, q : q + 128]
            total = total + jnp.sum((w * w).reshape(n // 8, 8, 128), axis=0)
    return jnp.float32(1.0), jnp.sum(total)


def ortho_kernel(idx, own_ref, sib_ref, opp_ref, diag_ref, mine_ref, theirs_ref, X, Xh, Xl, A, Bh, Rh):
    n, C = X.shape
    k, y, h = idx[0], idx[1], idx[3]
    loc = own_ref.shape[0]
    long = (h == 1) | (h == 2)
    fifth = (h == 3) & (k == 1)
    blocks = (
        (2 * y + k, own_ref),
        (2 * y + 1 - k, sib_ref),
        (2 * (1 - y) + k, opp_ref),
        (2 * (1 - y) + 1 - k, diag_ref),
    )

    def load(first, count):
        total = jnp.zeros((8, count), f32)
        for place, ref in blocks:
            base = pl.multiple_of(place * loc, 32)
            for i in range(0, loc, 32):
                low = ref[i : i + 32, first : first + count]
                v = low.astype(f32)
                Xh[pl.ds(base + i, 32), :count] = low
                X[pl.ds(base + i, 32), :count] = v
                total = total + jnp.sum((v * v).reshape(4, 8, count), axis=0)
        squares = jnp.sum(total)
        return 1.0 / (jnp.sqrt(squares) + 1e-07), squares

    @pl.when(long)
    def _():
        carry = load(0, C)
        lax.fori_loop(0, 5, lambda i, c: sweep(X, Xh, Xl, A, Bh, Rh, C, False, None, c), carry)

    def taps(first):
        carry = load(first, INNER)
        carry = lax.fori_loop(0, 2, lambda i, c: sweep(X, Xh, Xl, A, Bh, Rh, INNER, False, True, c), carry)
        lax.fori_loop(0, 3, lambda i, c: sweep(X, Xh, Xl, A, Bh, Rh, INNER, True, True, c), carry)

    @pl.when(jnp.logical_not(long) & jnp.logical_not(fifth))
    def _():
        taps(0)

    @pl.when(fifth)
    def _():
        taps(INNER)

    mine_ref[...] = X[at(2 * y + k, loc), :].astype(bf16)
    theirs_ref[...] = X[at(2 * y + 1 - k, loc), :INNER].astype(bf16)


def step_kernel(idx, mine_ref, got_ref, o_ref, tail_ref):
    h, b, k = idx[3], idx[2], idx[0]

    @pl.when((h == 0) | ((h == 3) & (k == 0)) | (h > 3))
    def _():
        o_ref[...] = mine_ref[:, :INNER]

    @pl.when((h == 3) & (k == 1))
    def _():
        o_ref[...] = got_ref[...]

    for i in range(2):

        @pl.when(((h == 1) | (h == 2)) & (b == i))
        def _():
            o_ref[...] = mine_ref[:, i * INNER : (i + 1) * INNER]

        @pl.when((h == 3) & (k == 0) & (b == i))
        def _():
            tail_ref[...] = got_ref[:, i * TAIL : (i + 1) * TAIL]

        @pl.when((h == 3) & (k == 1) & (b == i))
        def _():
            tail_ref[...] = mine_ref[:, i * TAIL : (i + 1) * TAIL]

    @pl.when(h != 3)
    def _():
        tail_ref[...] = jnp.zeros_like(tail_ref)


def join_kernel(idx, own_ref, got_ref, tail_ref, tail_got, o_ref):
    h = idx[3]
    for q in range(2):

        @pl.when(h // 2 % 2 == q)
        def _():
            o_ref[:, q * INNER : (q + 1) * INNER] = own_ref[...]
            o_ref[:, (1 - q) * INNER : (2 - q) * INNER] = got_ref[...]
            o_ref[:, 2 * INNER :] = (tail_ref if q else tail_got)[...]


def apply_kernel(
    keep, rate_long, rate_tap, idx, own_ref, x_ref, z_ref, zx_ref, first_ref, taps_ref, last_ref,
    of_ref, ot_ref, ol_ref,
):
    h, b = idx[3], idx[2]
    for odd in range(2):
        for i in range(2):

            @pl.when((h % 2 == odd) & (b == i))
            def _():
                even = (own_ref, x_ref) if odd == 0 else (z_ref, zx_ref)
                odds = (z_ref, zx_ref) if odd == 0 else (own_ref, x_ref)
                for r in chunks(first_ref.shape[0], 32):
                    for q in range(2):
                        e = even[q ^ i]
                        o = odds[q ^ i]
                        lanes = slice(q * INNER, (q + 1) * INNER)
                        tail = slice(q * TAIL, (q + 1) * TAIL)
                        of_ref[r, lanes] = keep * first_ref[r, lanes] + rate_long * o[r, :INNER].astype(f32)
                        ol_ref[r, lanes] = keep * last_ref[r, lanes] + rate_long * e[r, INNER : 2 * INNER].astype(f32)
                        ot_ref[q, r, :] = keep * taps_ref[q, r, :] + rate_tap * e[r, :INNER].astype(f32)
                        ot_ref[2 + q, r, :] = keep * taps_ref[2 + q, r, :] + rate_tap * o[
                            r, INNER : 2 * INNER
                        ].astype(f32)
                        ot_ref[4, r, tail] = keep * taps_ref[4, r, tail] + rate_tap * o[r, 2 * INNER :].astype(f32)


ROWS = 24


def vector_kernel(idx, two_ref, three_ref, one_ref, cot_ref, sq_ref, o_ref):
    y, c = idx[1], 2 * idx[1] + idx[0]
    o_ref[...] = jnp.zeros_like(o_ref)
    o_ref[pl.ds(y, 1), :] = one_ref[0:1, :]
    o_ref[pl.ds(2 + y, 1), :] = one_ref[1:2, :]
    two = two_ref[...].T
    three = three_ref[...].T
    wide = two_ref.shape[0]
    pieces = (two[2:3], two[0:1], two[1:2], three[2:3], three[0:1], three[1:2])
    for i, piece in enumerate(pieces):
        o_ref[pl.ds(4 + 6 * y + i, 1), :wide] = piece
    cot = cot_ref[...].T
    o_ref[pl.ds(16 + c, 1), : cot_ref.shape[0]] = cot[0:1]
    for i in range(3):
        o_ref[20 + i : 21 + i, :128] = sq_ref[i : i + 1, :]


def adam_kernel(v_ref, par_ref, mom_ref, sqr_ref, first_ref, second_ref, value_ref, root_ref, g):
    wide = INNER // 2
    g[0:4, :] = v_ref[0:4, :]
    for i in range(6):
        g[4 + i : 5 + i, :wide] = v_ref[4 + i : 5 + i, :wide]
        g[4 + i : 5 + i, wide:] = v_ref[10 + i : 11 + i, :wide]
    for i in range(2):
        g[10 + i : 11 + i, :wide] = v_ref[16 + 2 * i : 17 + 2 * i, :wide]
        g[10 + i : 11 + i, wide:] = v_ref[17 + 2 * i : 18 + 2 * i, :wide]
    per = INNER // 128
    for r in range(12):
        for q in range(per):
            at_row = slice(r * per + q, r * per + q + 1)
            grad = g[r : r + 1, q * 128 : (q + 1) * 128]
            par = par_ref[at_row, :]
            first = adam_first * mom_ref[at_row, :] + (1.0 - adam_first) * grad
            second = adam_second * sqr_ref[at_row, :] + (1.0 - adam_second) * grad * grad
            first_ref[at_row, :] = first
            second_ref[at_row, :] = second
            value_ref[at_row, :] = par - adam_rate * (
                (first / (1.0 - adam_first**STEP)) / (jnp.sqrt(second / (1.0 - adam_second**STEP)) + adam_eps)
                + decay_rate * par
            )
    count = v_ref[22:23, :128] * D
    root_ref[...] = jnp.zeros_like(root_ref)
    for i in range(2):
        root_ref[i : i + 1, :] = jnp.sqrt(v_ref[20 + i : 21 + i, :128] / count)


def after(value, *others):
    return lax.optimization_barrier((value, *others))[0]


def body(
    tokens,
    cotangent,
    lengths,
    valid_mask,
    weight_first,
    weight_dilated,
    weight_last,
    momentum_first,
    momentum_dilated,
    momentum_last,
    vector_params,
    vector_moment,
    vector_square,
):
    C = lax.axis_size("ch")
    S = lax.axis_size("seq")
    c = lax.axis_index("ch")
    s = lax.axis_index("seq")
    k = c % 2
    y = c // 2
    T = tokens.shape[0]
    half = T // 2
    loc = weight_first.shape[1]
    wide = 2 * loc
    col = D // C
    H = S // 2
    b = s % 2
    h = s // 2
    idx = jnp.stack([k, y, b, h, s, s * T + k * half]).astype(jnp.int32)

    sib = [(i, i ^ 1) for i in range(C)]
    opp = [(i, i ^ 2) for i in range(C)]
    xsw = [(i, i ^ 1) for i in range(S)]

    def swap_core(v):
        return lax.ppermute(v, "ch", sib)

    def swap_y(v):
        return lax.ppermute(v, "ch", opp)

    def swap_x(v):
        return lax.ppermute(v, "seq", xsw)

    def along_h(v, pairs):
        return lax.ppermute(v, "seq", [(2 * i + q, 2 * j + q) for i, j in pairs for q in range(2)])

    outer_pairs = []
    for i in range(S):
        for j in range(C):
            if j % 2 == 0 and i >= 1:
                outer_pairs.append((i * C + j, (i - 1) * C + (j ^ 1)))
            if j % 2 == 1 and i + 1 < S:
                outer_pairs.append((i * C + j, (i + 1) * C + (j ^ 1)))

    def swap_outer(v):
        return lax.ppermute(v, ("seq", "ch"), outer_pairs)

    w_first, w_taps, w_last = weight_first.T, jnp.swapaxes(weight_dilated, 1, 2), weight_last
    m_first, m_taps, m_last = momentum_first.T, jnp.swapaxes(momentum_dilated, 1, 2), momentum_last
    cot = cotangent.T
    valid = valid_mask.reshape(1, T)
    gain_shift = vector_params[: 2 * D].reshape(2, D)
    inner_rows = vector_params[2 * D : 2 * D + 6 * INNER].reshape(6, INNER)
    cols = lax.dynamic_slice_in_dim(inner_rows, y * wide, wide, 1).T
    flat = (VECTOR // 128, 128)
    flat_params = vector_params.reshape(flat)

    low_first, cot_all, cot_other, cot_sums = call(
        prep_kernel,
        [((loc, D), bf16), ((col, T), bf16), ((col, half), bf16), ((col, 128), f32)],
        [idx],
        [w_first, cot],
    )
    got_first = swap_core(low_first)
    cot_opp = swap_y(cot_all)
    cot_sib = swap_core(cot_other)

    rows = 128
    steps = half // rows
    hid_one, hat_one, slope_one, scale_one = pl.pallas_call(
        input_kernel,
        out_shape=[
            jax.ShapeDtypeStruct((half, D), bf16),
            jax.ShapeDtypeStruct((half, D), bf16),
            jax.ShapeDtypeStruct((half, D), bf16),
            jax.ShapeDtypeStruct((half, 128), f32),
        ],
        grid_spec=pltpu.PrefetchScalarGridSpec(
            num_scalar_prefetch=1,
            grid=(steps,),
            in_specs=[
                pl.BlockSpec((rows, D), lambda i, idx: (idx[0] * steps + i, 0)),
                pl.BlockSpec((2, D), lambda i, idx: (0, 0)),
            ],
            out_specs=[
                pl.BlockSpec((rows, D), lambda i, idx: (i, 0)),
                pl.BlockSpec((rows, D), lambda i, idx: (i, 0)),
                pl.BlockSpec((rows, D), lambda i, idx: (i, 0)),
                pl.BlockSpec((rows, 128), lambda i, idx: (i, 0)),
            ],
        ),
        compiler_params=pltpu.CompilerParams(vmem_limit_bytes=16 * MIB),
        cost_estimate=pl.CostEstimate(flops=5000000000, bytes_accessed=1000, transcendentals=0),
    )(after(idx, cot_all, low_first), tokens, gain_shift)

    (low_rest,) = call(
        rest_kernel, [((loc, D + KERNEL_TAPS * INNER), bf16)], [], [w_last, w_taps]
    )
    got_rest = swap_core(low_rest)

    full_first, inner_one, st_two = call(
        first_kernel,
        [((wide, D), bf16), ((wide, half), f32), ((8, half), f32)],
        [idx],
        [low_first, got_first, hid_one, cols],
    )
    st_two_got = after(swap_y(st_two), cot_sib, cot_opp)
    (cot_diag,) = call(other_half_kernel, [((col, half), bf16)], [idx], [cot_opp])
    cot_diag = swap_core(cot_diag)
    slab = ((wide, REACH), bf16)
    own_in, own_out, hat_two, slope_two = call(
        second_kernel,
        [slab, slab, ((wide, half), f32), ((wide, half), f32)],
        [idx],
        [inner_one, st_two, st_two_got, cols, valid],
        scratch=[((wide, half), bf16)],
    )
    opp_in, opp_out = swap_y(own_in), swap_y(own_out)
    sib_in, seq_out = swap_core(own_in), swap_outer(own_out)
    sib_opp_in, seq_opp_out = swap_core(opp_in), swap_y(seq_out)
    ext, inner_two, st_three, full_last, full_taps, masks = call(
        functools.partial(conv_kernel, S * T),
        [
            ((INNER, half + 2 * REACH), bf16),
            ((wide, half), f32),
            ((8, half), f32),
            ((wide, D), bf16),
            ((wide, KERNEL_TAPS * INNER), bf16),
            ((8, half), f32),
        ],
        [idx, lengths],
        [
            own_in, own_out, opp_in, opp_out, sib_in, sib_opp_in, seq_out, seq_opp_out,
            low_rest, got_rest, cols,
        ],
        scratch=[((KERNEL_TAPS * INNER, half), bf16)],
    )
    st_three_got = swap_y(st_three)
    gw, g_three = call(
        cotangent_kernel,
        [((D, half), bf16), ((wide, half), f32)],
        [idx],
        [full_last, cot_all, cot_sib, cot_opp, cot_diag],
    )
    hid_three, e_three, hat_three, part_three = call(
        third_kernel,
        [((wide, half), bf16), ((wide, half), f32), ((wide, half), f32), ((8, half), f32)],
        [],
        [inner_two, st_three, st_three_got, cols, g_three],
    )
    part_three_got = swap_y(part_three)
    dz_two, slab_in, slab_out, sums_three = call(
        third_back_kernel,
        [((wide, half), bf16), ((wide, REACH), bf16), ((wide, REACH), bf16), ((wide, 128), f32)],
        [idx],
        [e_three, hat_three, part_three, part_three_got, cols],
    )
    got_in, got_out = swap_core(slab_in), swap_outer(slab_out)
    back_own, back_send = call(
        conv_back_kernel,
        [((wide, half), f32), ((wide, half), bf16)],
        [idx],
        [dz_two, got_in, got_out, masks, full_taps],
        scratch=[((wide, half + 2 * REACH), bf16), ((INNER, half), f32)],
    )
    back_got = swap_y(back_send)
    early_size = D + KERNEL_TAPS * INNER
    early_own, early_send = call(
        grads_kernel,
        [((loc, early_size), f32), ((loc, early_size), bf16)],
        [idx],
        [after(dz_two, back_send), ext, masks, hid_three, gw],
        scratch=[((wide, early_size), f32)],
        limit=32,
    )
    early_got = swap_core(early_send)
    unit, unit_low = ((loc, INNER), f32), ((loc, INNER), bf16)
    last_keep, last_send, taps_keep, taps_send = call(
        early_kernel,
        [unit, unit_low, ((loc, 2 * INNER + TAIL), f32), ((loc, 2 * INNER + TAIL), bf16)],
        [idx],
        [early_own, early_got],
    )
    last_got, taps_got = swap_x(last_send), swap_x(taps_send)
    e_two, part_two = call(
        second_back_kernel,
        [((wide, half), f32), ((8, half), f32)],
        [],
        [after(back_own, taps_send), back_got, slope_two, hat_two, cols],
    )
    half_out = [((half, HALF_D), f32), ((half, HALF_D), bf16)]
    branch_own, branch_send = call(
        halves_kernel, half_out, [idx], [after(hid_three, back_send), full_last], scratch=[((half, D), f32)]
    )
    part_two_got = after(swap_y(part_two), branch_send)
    branch_got = swap_y(after(branch_send, part_two_got))
    dz_one, first_own, first_send, sums_two = call(
        first_back_kernel,
        [((wide, half), bf16), ((loc, D), f32), ((loc, D), bf16), ((wide, 128), f32)],
        [idx],
        [e_two, hat_two, part_two, part_two_got, st_two, st_two_got, cols, hid_one],
        scratch=[((wide, D), f32)],
    )
    first_got = swap_core(first_send)
    back_own, back_send = call(
        halves_kernel, half_out, [idx], [dz_one, full_first], scratch=[((half, D), f32)]
    )
    first_keep, first_low = call(
        pair_kernel, [unit, unit_low], [idx], [after(first_own, back_send), first_got]
    )
    first_low = after(first_low, taps_got, last_got)
    first_got = swap_x(first_low)

    span = H
    while span > 4:
        span //= 2
        fold = [(i + span, i) for i in range(span)]

        def folded(keep, got):
            total = keep + got.astype(f32)
            return total + along_h(total.astype(bf16), fold).astype(f32), jnp.zeros_like(got)

        first_keep, first_got = folded(first_keep, first_got)
        last_keep, last_got = folded(last_keep, last_got)
        taps_keep, taps_got = folded(taps_keep, taps_got)
    line = 4

    size_taps = (loc, INNER + TAIL)
    sum_taps, send_taps = call(
        taps_kernel, [((loc, 2 * INNER + TAIL), f32), (size_taps, bf16)], [idx], [taps_keep, taps_got]
    )
    got_taps = along_h(send_taps, [(i, i ^ 1) for i in range(line)])
    tail_low = ((loc, TAIL), bf16)
    part_unit, part_tail, *sends, tail_send = call(
        line_kernel,
        [unit, ((loc, TAIL), f32), unit_low, unit_low, unit_low, tail_low],
        [idx],
        [first_keep, first_got, last_keep, last_got, sum_taps, got_taps],
    )
    got_units = [along_h(v, pairs) for v, pairs in zip(sends, LINE)]
    got_tail = along_h(tail_send, LINE_TAIL)
    back_got = swap_y(back_send)
    def whole_block(shape):
        return pl.BlockSpec(shape, lambda i, idx: (0, 0))

    out_mine, out_send, squares = pl.pallas_call(
        output_kernel,
        out_shape=[
            jax.ShapeDtypeStruct((col, half), f32),
            jax.ShapeDtypeStruct((col, half), f32),
            jax.ShapeDtypeStruct((8, 128), f32),
        ],
        grid_spec=pltpu.PrefetchScalarGridSpec(
            num_scalar_prefetch=1,
            grid=(1,),
            in_specs=[
                whole_block((half, HALF_D)),
                whole_block((half, HALF_D)),
                pl.BlockSpec((half, HALF_D), lambda i, idx: (idx[0], idx[1])),
                whole_block((VECTOR // 128, 128)),
                whole_block((1, T)),
            ],
            out_specs=[whole_block((col, half)), whole_block((col, half)), whole_block((8, 128))],
            scratch_shapes=[pltpu.VMEM((HALF_D, half), f32)],
        ),
        compiler_params=pltpu.CompilerParams(vmem_limit_bytes=24 * MIB),
        cost_estimate=pl.CostEstimate(flops=1000, bytes_accessed=1000, transcendentals=0),
    )(idx, branch_own, branch_got, tokens, flat_params, valid)
    e_one, part_one, sums_one = call(
        token_kernel,
        [((half, HALF_D), f32), ((half, 128), f32), ((8, HALF_D), f32)],
        [idx],
        [back_own, back_got, slope_one, hat_one, gain_shift],
    )
    (part_one,) = call(flip_kernel, [((8, half), f32)], [], [part_one])
    (vector,) = call(
        vector_kernel, [((ROWS, INNER), f32)], [idx], [sums_two, sums_three, sums_one, cot_sums, squares]
    )
    (old_unit,) = call(own_kernel, [(size_taps, f32)], [idx], [m_first, m_taps, m_last])
    sum_unit, sum_tail, new_unit, cross = call(
        finish_kernel,
        [unit_low, tail_low, (size_taps, bf16), unit_low],
        [idx],
        [old_unit, part_unit, part_tail, *got_units, got_tail],
    )
    cross_got = swap_x(after(cross, squares, back_got))
    (block,) = call(block_kernel, [((loc, D), bf16)], [idx], [new_unit, cross_got])

    def far_along_z(unit, tail):
        return along_h(unit, [(i, i ^ 2) for i in range(4)]), along_h(tail, LINE_TAIL)

    sum_far, tail_far = far_along_z(sum_unit, sum_tail)
    block_sib, block_opp = swap_core(block), swap_y(block)
    block_diag = swap_core(after(block_opp, sum_far, tail_far, vector))

    def joined_with(unit, got, tail, tail_got):
        return call(
            join_kernel, [((loc, 2 * INNER + TAIL), bf16)], [idx], [unit, got, tail, tail_got]
        )[0]

    def next_along_z(joined):
        return along_h(joined, [(i, i ^ 1) for i in range(4)])

    def spread(parts):
        span = 4
        while span < H:
            pairs = [(i, i + span) for i in range(span)]
            parts = [jnp.where((h >= span) & (h < 2 * span), along_h(v, pairs), v) for v in parts]
            span *= 2
        return parts

    def apply(keep, rate_long, rate_tap, parts, first, taps, last):
        return call(
            functools.partial(apply_kernel, keep, rate_long, rate_tap),
            [((loc, D), f32), ((KERNEL_TAPS, loc, INNER), f32), ((loc, D), f32)],
            [idx],
            [*parts, first, taps, last],
            limit=32,
        )

    joined = joined_with(sum_unit, sum_far, sum_tail, tail_far)
    vector_x = swap_x(vector)
    mine, theirs = call(
        ortho_kernel,
        [((loc, D), bf16), ((loc, INNER), bf16)],
        [idx],
        [after(block, joined, vector_x), block_sib, block_opp, block_diag],
        scratch=[
            ((INNER, D), f32),
            ((INNER, D), bf16),
            ((INNER, INNER), bf16),
            ((INNER, INNER), f32),
            ((INNER, INNER), bf16),
            ((INNER, INNER), bf16),
        ],
        limit=32,
        flops=14 * 10**9,
    )
    joined_x = swap_x(joined)
    other = next_along_z(joined)
    part_got = swap_y(part_one)
    vector = vector + vector_x
    vector_core = swap_core(vector)
    theirs_got = swap_core(theirs)
    step_unit, step_tail = call(
        step_kernel, [unit_low, ((loc, TAIL), bf16)], [idx], [after(mine, joined_x, other, vector_core, part_got), theirs_got]
    )
    other_x = swap_x(after(other, step_unit))
    mom_parts = spread([joined, joined_x, other, other_x])

    vector = vector + vector_core
    vector = vector + swap_y(vector)
    step_far, tail_far = far_along_z(step_unit, step_tail)
    grad_mine, grad_send = call(
        token_back_kernel,
        [((col, half), f32), ((col, half), f32)],
        [idx],
        [after(e_one, step_unit), hat_one, scale_one, part_one, part_got],
        scratch=[((half, HALF_D), f32), ((HALF_D, half), f32)],
    )
    joined = joined_with(after(step_unit, vector, other_x, grad_send), step_far, step_tail, tail_far)
    joined_x = swap_x(joined)
    other = after(next_along_z(joined), joined_x)

    grad_got, out_got = swap_core(grad_send), swap_core(out_send)
    vector = vector + lax.ppermute(vector, "seq", [(i, i ^ 2) for i in range(S)])
    other, vector, grad_got, out_got = lax.optimization_barrier((other, vector, grad_got, out_got))
    other_x = swap_x(other)
    bit = 4
    while bit < S:
        vector = vector + lax.ppermute(vector, "seq", [(i, i ^ bit) for i in range(S)])
        bit *= 2
    (block_output,) = call(place_kernel, [((col, T), f32)], [idx], [out_mine, out_got])
    (tokens_grad,) = call(place_add_kernel, [((col, T), f32)], [idx], [grad_mine, grad_got, cot])
    vector_first, vector_second, vector_values, root = call(
        adam_kernel,
        [(flat, f32)] * 3 + [((8, 128), f32)],
        [],
        [vector, flat_params, vector_moment.reshape(flat), vector_square.reshape(flat)],
        scratch=[((12, INNER), f32)],
    )
    vector_first, vector_second, vector_values = (
        v.reshape(VECTOR) for v in (vector_first, vector_second, vector_values)
    )
    root_means = root[:2, 0]
    new_first, new_taps, new_last = apply(
        muon_keep, 1.0, 1.0, [after(mom_parts[0], other), *mom_parts[1:]], m_first, m_taps, m_last
    )
    keep_weight = 1.0 - muon_rate * decay_rate
    rate = muon_rate * muon_scale
    out_first, out_taps, out_last = apply(
        keep_weight,
        -rate * math.sqrt(D),
        -rate * math.sqrt(INNER),
        spread([joined, joined_x, other, other_x]),
        w_first,
        w_taps,
        w_last,
    )
    return (
        block_output.T,
        tokens_grad.T,
        out_first.T,
        jnp.swapaxes(out_taps, 1, 2),
        out_last,
        new_first.T,
        jnp.swapaxes(new_taps, 1, 2),
        new_last,
        vector_first,
        vector_second,
        vector_values,
        root_means,
    )


def solution(mesh):
    placed = (
        P("seq", None),
        P("seq", "ch"),
        P(),
        P("seq"),
        P(None, "ch"),
        P(None, None, "ch"),
        P("ch", None),
        P(None, "ch"),
        P(None, None, "ch"),
        P("ch", None),
        P(),
        P(),
        P(),
    )
    return jax.shard_map(
        body,
        mesh=mesh,
        in_specs=placed,
        out_specs=(
            P("seq", "ch"),
            P("seq", "ch"),
            P(None, "ch"),
            P(None, None, "ch"),
            P("ch", None),
            P(None, "ch"),
            P(None, None, "ch"),
            P("ch", None),
            P(),
            P(),
            P(),
            P(),
        ),
        check_vma=False,
    )
```

```python
import functools
import math

import jax
import jax.numpy as jnp
from jax import lax
from jax.experimental import pallas as pl
from jax.experimental.pallas import tpu as pltpu
from jax.sharding import PartitionSpec as P

D = 1280
INNER = 640
KERNEL_TAPS = 5
DILATION_SPAN = 128
STEP = 10

norm_eps = 1e-05
coef_first = 3.4445
coef_second = -4.775
coef_third = 2.0315
adam_rate = 0.4
adam_first = 0.9
adam_second = 0.999
adam_eps = 1e-08
decay_rate = 0.01
muon_rate = 0.1
muon_keep = 0.95
muon_scale = 0.2
REACH = KERNEL_TAPS // 2 * DILATION_SPAN
VECTOR = 3 * D + 6 * INNER
HALF_D = D // 2
MIB = 1024 * 1024

f32 = jnp.float32
bf16 = jnp.bfloat16
NN = (((1,), (0,)), ((), ()))
NT = (((1,), (1,)), ((), ()))
TN = (((0,), (0,)), ((), ()))


def mul(a, b, dims):
    return lax.dot_general(a, b, dims, preferred_element_type=f32)


def erf_parts(v):
    a = jnp.abs(v) * math.sqrt(0.5)
    t = pl.reciprocal(1.0 + 0.3275911 * a)
    e = jnp.exp(-a * a)
    p = t * (0.254829592 + t * (-0.284496736 + t * (1.421413741 + t * (-1.453152027 + t * 1.061405429))))
    tail = 0.5 * p * e
    return jnp.where(v >= 0, 1.0 - tail, tail), e


def gelu_pair(v):
    cdf, e = erf_parts(v)
    return v * cdf, cdf + v * e * (1.0 / math.sqrt(2.0 * math.pi))


VMEM = pl.BlockSpec(memory_space=pltpu.VMEM)
SMEM = pl.BlockSpec(memory_space=pltpu.SMEM)


def call(kernel, outs, scalars, arrays, scratch=(), limit=16, flops=1000):
    shapes = [jax.ShapeDtypeStruct(shape, dtype) for shape, dtype in outs]
    return pl.pallas_call(
        kernel,
        out_shape=shapes,
        in_specs=[SMEM] * len(scalars) + [VMEM] * len(arrays),
        out_specs=[VMEM] * len(outs),
        scratch_shapes=[pltpu.VMEM(shape, dtype) for shape, dtype in scratch],
        compiler_params=pltpu.CompilerParams(vmem_limit_bytes=limit * MIB),
        cost_estimate=pl.CostEstimate(flops=flops, bytes_accessed=1000, transcendentals=0),
    )(*scalars, *arrays)


def chunks(count, step):
    return [pl.ds(i, step) for i in range(0, count, step)]


def at(index, count, step=32):
    return pl.ds(pl.multiple_of(index * count, step), count)


def prep_kernel(idx, w_ref, cot_ref, wo_ref, all_ref, other_ref, sums_ref):
    half = other_ref.shape[1]
    for r in chunks(cot_ref.shape[0], 32):
        v = cot_ref[r, :]
        all_ref[r, :] = v.astype(bf16)
        other_ref[r, :] = cot_ref[r, at(1 - idx[0], half, 128)].astype(bf16)
        sums_ref[r, :] = jnp.broadcast_to(jnp.sum(v, axis=1, keepdims=True), (32, 128))
    for r in chunks(w_ref.shape[0], 32):
        wo_ref[r, :] = w_ref[r, :].astype(bf16)


def rest_kernel(last_ref, taps_ref, o_ref):
    for r in chunks(last_ref.shape[0], 32):
        o_ref[r, :D] = last_ref[r, :].astype(bf16)
        for j in range(KERNEL_TAPS):
            o_ref[r, D + j * INNER : D + (j + 1) * INNER] = taps_ref[j, r, :].astype(bf16)


def input_kernel(idx, tok_ref, gs_ref, hid_ref, hat_ref, slope_ref, scale_ref):
    for r in chunks(tok_ref.shape[0], 16):
        v = tok_ref[r, :]
        center = jnp.sum(v, axis=1, keepdims=True) * (1.0 / D)
        square = jnp.sum(v * v, axis=1, keepdims=True) * (1.0 / D)
        scale = lax.rsqrt(square - center * center + norm_eps)
        hat = (v - center) * scale
        hid, slope = gelu_pair(hat * gs_ref[0:1, :] + gs_ref[1:2, :])
        hid_ref[r, :] = hid.astype(bf16)
        hat_ref[r, :] = hat.astype(bf16)
        slope_ref[r, :] = slope.astype(bf16)
        scale_ref[r, :] = jnp.broadcast_to(scale, (16, 128))


def put_stats(ref, parts):
    for i, part in enumerate(parts):
        ref[i : i + 1, :] = part


def first_kernel(idx, own_ref, got_ref, hid_ref, cols_ref, w_ref, inner_ref, st_ref):
    k = idx[0]
    loc = own_ref.shape[0]
    w_ref[at(k, loc), :] = own_ref[...]
    w_ref[at(1 - k, loc), :] = got_ref[...]
    v = mul(w_ref[...], hid_ref[...], NT) + cols_ref[:, 0:1]
    inner_ref[...] = v
    put_stats(st_ref, (jnp.sum(v, axis=0, keepdims=True), jnp.sum(v * v, axis=0, keepdims=True)))


def center_scale(st_ref, got_ref):
    center = (st_ref[0:1, :] + got_ref[0:1, :]) * (1.0 / INNER)
    square = (st_ref[1:2, :] + got_ref[1:2, :]) * (1.0 / INNER)
    return center, lax.rsqrt(square - center * center + norm_eps)


def second_kernel(
    idx, inner_ref, st_ref, got_ref, cols_ref, valid_ref, in_ref, out_ref, hat_ref, slope_ref, hid_ref
):
    center, scale = center_scale(st_ref, got_ref)
    valid = valid_ref[:, at(idx[0], hid_ref.shape[1], 128)].astype(f32)
    for r in chunks(inner_ref.shape[0], 32):
        hat = (inner_ref[r, :] - center) * scale
        hid, slope = gelu_pair(hat * cols_ref[r, 1:2] + cols_ref[r, 2:3])
        hid_ref[r, :] = (hid * valid).astype(bf16)
        hat_ref[r, :] = hat
        slope_ref[r, :] = slope * valid
    slabs_of(idx[0], hid_ref, slice(None), in_ref, out_ref)


def slabs_of(k, v_ref, row, in_ref, out_ref):
    half = v_ref.shape[1]
    rows = v_ref.shape[0]
    in_ref[row, :] = v_ref[:, at(1 - k, half - REACH, 128)]
    out_ref[row, :] = v_ref[:, at(k, half - REACH, 128)]


def fill_reach(k, ext_ref, in_ref, out_ref, half):
    @pl.when(k == 0)
    def _():
        ext_ref[:, :REACH] = out_ref[...]
        ext_ref[:, REACH + half :] = in_ref[...]

    @pl.when(k == 1)
    def _():
        ext_ref[:, :REACH] = in_ref[...]
        ext_ref[:, REACH + half :] = out_ref[...]


def conv_kernel(
    total, idx, lengths, own_in, own_out, opp_in, opp_out, sib_in, sib_opp_in, seq_out, seq_opp_out,
    wo_ref, wg_ref, cols_ref, ext_ref, inner_ref, st_ref, last_ref, taps_ref, mask_ref, stack,
):
    k, y = idx[0], idx[1]
    wide, reach = own_in.shape
    half = 2 * reach
    loc = wo_ref.shape[0]
    for q in range(2):
        @pl.when(k == q)
        def _():
            for place, (mine, other) in enumerate(
                ((seq_out, seq_opp_out), (own_out, opp_out), (own_in, opp_in), (sib_in, sib_opp_in))
            ):
                place = 3 - place if q else place
                lanes = slice(place * reach, (place + 1) * reach)
                ext_ref[at(y, wide), lanes] = mine[...]
                ext_ref[at(1 - y, wide), lanes] = other[...]

    last_ref[at(k, loc), :] = wo_ref[:, :D]
    last_ref[at(1 - k, loc), :] = wg_ref[:, :D]
    taps_ref[at(k, loc), :] = wo_ref[:, D:]
    taps_ref[at(1 - k, loc), :] = wg_ref[:, D:]
    positions = idx[5] - REACH + lax.broadcasted_iota(jnp.int32, (1, half + 2 * REACH), 1)
    segment = jnp.zeros_like(positions)
    bound = jnp.int32(0)
    for i in range(lengths.shape[0]):
        bound = bound + lengths[i]
        segment = segment + (positions >= bound).astype(jnp.int32)
    segment = jnp.where((positions >= 0) & (positions < total), segment, -1)
    centre = segment[:, REACH : REACH + half]
    for j in range(KERNEL_TAPS):
        lanes = slice(j * DILATION_SPAN, j * DILATION_SPAN + half)
        mask = (segment[:, lanes] == centre).astype(f32)
        mask_ref[j : j + 1, :] = mask
        low = mask.astype(bf16)
        for i in range(0, INNER, 160):
            stack[j * INNER + i : j * INNER + i + 160, :] = ext_ref[i : i + 160, lanes] * low
    v = mul(taps_ref[...], stack[...], NN) + cols_ref[:, 3:4]
    inner_ref[...] = v
    put_stats(st_ref, (jnp.sum(v, axis=0, keepdims=True), jnp.sum(v * v, axis=0, keepdims=True)))


def cotangent_kernel(idx, last_ref, all_ref, sib_ref, opp_ref, diag_ref, gw_ref, g_ref):
    k, y = idx[0], idx[1]
    col, half = sib_ref.shape
    mine = at(k, half, 128)
    gw_ref[at(2 * y + k, col), :] = all_ref[:, mine]
    gw_ref[at(2 * y + 1 - k, col), :] = sib_ref[...]
    gw_ref[at(2 * (1 - y) + k, col), :] = opp_ref[:, mine]
    gw_ref[at(2 * (1 - y) + 1 - k, col), :] = diag_ref[...]
    g_ref[...] = mul(last_ref[...], gw_ref[...], NN)


def other_half_kernel(idx, all_ref, o_ref):
    o_ref[...] = all_ref[:, at(1 - idx[0], o_ref.shape[1], 128)]


def third_kernel(inner_ref, st_ref, got_ref, cols_ref, g_ref, hid_ref, e_ref, hat_ref, part_ref):
    center, scale = center_scale(st_ref, got_ref)
    plain = jnp.zeros_like(center)
    cross = jnp.zeros_like(center)
    for r in chunks(inner_ref.shape[0], 32):
        hat = (inner_ref[r, :] - center) * scale
        gain = cols_ref[r, 4:5]
        hid, slope = gelu_pair(hat * gain + cols_ref[r, 5:6])
        hid_ref[r, :] = hid.astype(bf16)
        hat_ref[r, :] = hat
        e = slope * g_ref[r, :]
        e_ref[r, :] = e
        eg = e * gain
        plain = plain + jnp.sum(eg, axis=0, keepdims=True)
        cross = cross + jnp.sum(eg * hat, axis=0, keepdims=True)
    put_stats(part_ref, (plain, cross, scale))


def norm_back(r, e_ref, hat_ref, part_ref, got_ref, scale, gain, sums_ref):
    plain = (part_ref[0:1, :] + got_ref[0:1, :]) * (1.0 / INNER)
    cross = (part_ref[1:2, :] + got_ref[1:2, :]) * (1.0 / INNER)
    e, hat = e_ref[r, :], hat_ref[r, :]
    grad = scale * (e * gain - plain - hat * cross)
    sums_ref[r, 0:1] = jnp.sum(e * hat, axis=1, keepdims=True)
    sums_ref[r, 1:2] = jnp.sum(e, axis=1, keepdims=True)
    sums_ref[r, 2:3] = jnp.sum(grad, axis=1, keepdims=True)
    return grad


def third_back_kernel(idx, e_ref, hat_ref, part_ref, got_ref, cols_ref, dz_ref, in_ref, out_ref, sums_ref):
    for r in chunks(e_ref.shape[0], 32):
        grad = norm_back(r, e_ref, hat_ref, part_ref, got_ref, part_ref[2:3, :], cols_ref[r, 4:5], sums_ref)
        dz_ref[r, :] = grad.astype(bf16)
    slabs_of(idx[0], dz_ref, slice(None), in_ref, out_ref)


def split_rows(k, full, own_ref, send_ref, lanes):
    loc = own_ref.shape[0]
    own_ref[:, lanes] = full[at(k, loc), lanes]
    send_ref[:, lanes] = full[at(1 - k, loc), lanes].astype(bf16)


def grads_kernel(idx, dz_ref, ext_ref, mask_ref, hid_ref, gw_ref, own_ref, send_ref, full):
    k = idx[0]
    half = dz_ref.shape[1]
    full[:, :D] = mul(hid_ref[...], gw_ref[...], NT)
    split_rows(k, full, own_ref, send_ref, slice(0, D))
    for j in range(KERNEL_TAPS):
        masked = dz_ref[...] * mask_ref[j : j + 1, :].astype(bf16)
        moved = ext_ref[:, j * DILATION_SPAN : j * DILATION_SPAN + half]
        lanes = slice(D + j * INNER, D + (j + 1) * INNER)
        full[:, lanes] = mul(masked, moved, NT)
        split_rows(k, full, own_ref, send_ref, lanes)


def conv_back_kernel(idx, dz_ref, in_ref, out_ref, mask_ref, taps_ref, own_ref, send_ref, ext, full):
    k, y = idx[0], idx[1]
    wide, half = dz_ref.shape
    ext[:, REACH : REACH + half] = dz_ref[...]
    fill_reach(k, ext, in_ref, out_ref, half)
    total = None
    for j in range(KERNEL_TAPS):
        begin = REACH - (j - KERNEL_TAPS // 2) * DILATION_SPAN
        mask = mask_ref[KERNEL_TAPS - 1 - j : KERNEL_TAPS - j, :].astype(bf16)
        part = mul(taps_ref[:, j * INNER : (j + 1) * INNER], ext[:, begin : begin + half] * mask, TN)
        total = part if total is None else total + part
    full[...] = total
    own_ref[...] = full[at(y, wide), :]
    send_ref[...] = full[at(1 - y, wide), :].astype(bf16)


def second_back_kernel(own_ref, got_ref, slope_ref, hat_ref, cols_ref, e_ref, part_ref):
    plain = jnp.zeros((1, own_ref.shape[1]), f32)
    cross = jnp.zeros_like(plain)
    for r in chunks(own_ref.shape[0], 32):
        e = slope_ref[r, :] * (own_ref[r, :] + got_ref[r, :].astype(f32))
        e_ref[r, :] = e
        eg = e * cols_ref[r, 1:2]
        plain = plain + jnp.sum(eg, axis=0, keepdims=True)
        cross = cross + jnp.sum(eg * hat_ref[r, :], axis=0, keepdims=True)
    put_stats(part_ref, (plain, cross))


def first_back_kernel(
    idx, e_ref, hat_ref, part_ref, got_ref, st_ref, stg_ref, cols_ref, hid_ref,
    dz_ref, own_ref, send_ref, sums_ref, full,
):
    _, scale = center_scale(st_ref, stg_ref)
    for r in chunks(e_ref.shape[0], 32):
        grad = norm_back(r, e_ref, hat_ref, part_ref, got_ref, scale, cols_ref[r, 1:2], sums_ref)
        dz_ref[r, :] = grad.astype(bf16)
    full[...] = mul(dz_ref[...], hid_ref[...], NN)
    split_rows(idx[0], full, own_ref, send_ref, slice(0, D))


def halves_kernel(idx, z_ref, w_ref, own_ref, send_ref, full):
    y = idx[1]
    full[...] = mul(z_ref[...], w_ref[...], TN)
    for r in chunks(full.shape[0], 64):
        own_ref[r, :] = full[r, at(y, HALF_D, 128)]
        send_ref[r, :] = full[r, at(1 - y, HALF_D, 128)].astype(bf16)


def column_halves(k, flipped, mine_ref, send_ref, full):
    col = mine_ref.shape[0]
    full[...] = flipped
    mine_ref[...] = full[at(k, col), :]
    send_ref[...] = full[at(1 - k, col), :]


def output_kernel(idx, own_ref, got_ref, tok_ref, flat_ref, valid_ref, mine_ref, send_ref, sq_ref, full):
    k, y = idx[0], idx[1]
    half = own_ref.shape[0]
    per = HALF_D // 128
    first = (2 * D + 6 * INNER) // 128 + per * y
    bias = jnp.concatenate([flat_ref[pl.ds(first + q, 1), :] for q in range(per)], axis=1)
    branch = own_ref[...] + got_ref[...].astype(f32) + bias
    out = tok_ref[...] + branch
    valid = valid_ref[:, at(k, half, 128)].astype(f32)
    sq_ref[0:1, :] = jnp.sum(valid * mul_rows(out), axis=1, keepdims=True) * jnp.ones((1, 128), f32)
    sq_ref[1:2, :] = jnp.sum(valid * mul_rows(branch), axis=1, keepdims=True) * jnp.ones((1, 128), f32)
    sq_ref[2:3, :] = jnp.sum(valid, axis=1, keepdims=True) * jnp.full((1, 128), 0.5, f32)
    sq_ref[3:8, :] = jnp.zeros((5, 128), f32)
    column_halves(k, out.T, mine_ref, send_ref, full)


def mul_rows(v):
    rows = jnp.sum(v * v, axis=1, keepdims=True)
    return jnp.broadcast_to(rows, (v.shape[0], 128)).T[0:1, :]


def token_kernel(idx, own_ref, got_ref, slope_ref, hat_ref, gs_ref, e_ref, part_ref, sums_ref):
    y = idx[1]
    cols = at(y, HALF_D, 128)
    gain = gs_ref[0:1, cols]
    sum_cross = jnp.zeros((1, HALF_D), f32)
    sum_plain = jnp.zeros((1, HALF_D), f32)
    for r in chunks(own_ref.shape[0], 32):
        e = slope_ref[r, cols].astype(f32) * (own_ref[r, :] + got_ref[r, :].astype(f32))
        hat = hat_ref[r, cols].astype(f32)
        eg = e * gain
        e_ref[r, :] = eg
        part_ref[r, 0:1] = jnp.sum(eg, axis=1, keepdims=True)
        part_ref[r, 1:2] = jnp.sum(eg * hat, axis=1, keepdims=True)
        sum_cross = sum_cross + jnp.sum(e * hat, axis=0, keepdims=True)
        sum_plain = sum_plain + jnp.sum(e, axis=0, keepdims=True)
    put_stats(sums_ref, (sum_cross, sum_plain))


def flip_kernel(part_ref, o_ref):
    o_ref[...] = part_ref[...].T[0:8, :]


def token_back_kernel(idx, e_ref, hat_ref, scale_ref, part_ref, got_ref, mine_ref, send_ref, rows, full):
    cols = at(idx[1], HALF_D, 128)
    means = ((part_ref[...] + got_ref[...]) * (1.0 / D)).T
    for r in range(0, e_ref.shape[0], 64):
        s = slice(r, r + 64)
        hat = hat_ref[s, cols].astype(f32)
        rows[s, :] = scale_ref[s, 0:1] * (e_ref[s, :] - means[s, 0:1] - hat * means[s, 1:2])
    column_halves(idx[0], rows[...].T, mine_ref, send_ref, full)


def place_kernel(idx, mine_ref, got_ref, o_ref):
    half = mine_ref.shape[1]
    o_ref[:, at(idx[0], half, 128)] = mine_ref[...]
    o_ref[:, at(1 - idx[0], half, 128)] = got_ref[...]


def place_add_kernel(idx, mine_ref, got_ref, base_ref, o_ref):
    half = mine_ref.shape[1]
    mine, other = at(idx[0], half, 128), at(1 - idx[0], half, 128)
    o_ref[:, mine] = base_ref[:, mine] + mine_ref[...]
    o_ref[:, other] = base_ref[:, other] + got_ref[...]


TAIL = INNER // 2


def tap_columns(b):
    return ((D + b * INNER, INNER), (D + (2 + b) * INNER, INNER), (D + 4 * INNER + b * TAIL, TAIL))


def pair_columns(own_ref, got_ref, keep_ref, send_ref, mine, other):
    to = 0
    for (m, count), (o, _n) in zip(mine, other):
        for r in chunks(own_ref.shape[0], 32):
            keep_ref[r, to : to + count] = own_ref[r, m : m + count] + got_ref[r, m : m + count].astype(f32)
            send_ref[r, to : to + count] = (
                own_ref[r, o : o + count] + got_ref[r, o : o + count].astype(f32)
            ).astype(bf16)
        to += count


def early_kernel(idx, own_ref, got_ref, keep_last, send_last, keep_taps, send_taps):
    for b in range(2):

        @pl.when(idx[2] == b)
        def _():
            pair_columns(own_ref, got_ref, keep_last, send_last, [(b * INNER, INNER)], [((1 - b) * INNER, INNER)])
            pair_columns(own_ref, got_ref, keep_taps, send_taps, tap_columns(b), tap_columns(1 - b))


def pair_kernel(idx, own_ref, got_ref, keep_ref, send_ref):
    for b in range(2):

        @pl.when(idx[2] == b)
        def _():
            pair_columns(own_ref, got_ref, keep_ref, send_ref, [(b * INNER, INNER)], [((1 - b) * INNER, INNER)])


def taps_kernel(idx, keep_ref, got_ref, sum_ref, send_ref):
    for r in chunks(keep_ref.shape[0], 32):
        sum_ref[r, :] = keep_ref[r, :] + got_ref[r, :].astype(f32)

    @pl.when(idx[3] % 2 == 0)
    def _():
        send_ref[...] = sum_ref[:, INNER:].astype(bf16)

    @pl.when(idx[3] % 2 == 1)
    def _():
        send_ref[:, :INNER] = sum_ref[:, :INNER].astype(bf16)
        send_ref[:, INNER:] = jnp.zeros_like(send_ref[:, INNER:])


LINE = (
    ((0, 0), (1, 3), (2, 1), (3, 2)),
    ((0, 2), (1, 0), (2, 3), (3, 1)),
    ((0, 1), (1, 2), (2, 0), (3, 3)),
)
LINE_TAIL = ((0, 0), (1, 3), (2, 2), (3, 1))


def line_kernel(
    idx, keep_f, got_f, keep_l, got_l, taps_ref, taps_got,
    part_ref, tail_part, one_ref, two_ref, three_ref, tail_ref,
):
    h = idx[3]
    first = keep_f[...] + got_f[...].astype(f32)
    last = keep_l[...] + got_l[...].astype(f32)
    even = taps_ref[:, :INNER] + taps_got[:, :INNER].astype(f32)
    odd = taps_ref[:, INNER : 2 * INNER] + taps_got[:, :INNER].astype(f32)
    tail = taps_ref[:, 2 * INNER :] + taps_got[:, INNER:].astype(f32)
    low_first, low_last = first.astype(bf16), last.astype(bf16)
    tail_part[...] = tail
    tail_ref[...] = tail.astype(bf16)

    @pl.when(h == 0)
    def _():
        part_ref[...] = even
        one_ref[...] = low_first
        two_ref[...] = low_last
        three_ref[...] = low_first

    @pl.when(h == 1)
    def _():
        part_ref[...] = first
        one_ref[...] = odd.astype(bf16)
        two_ref[...] = low_last
        three_ref[...] = low_last

    @pl.when(h == 2)
    def _():
        part_ref[...] = last
        one_ref[...] = low_first
        two_ref[...] = low_first
        three_ref[...] = even.astype(bf16)

    @pl.when(h >= 3)
    def _():
        part_ref[...] = odd
        one_ref[...] = low_last
        two_ref[...] = low_first
        three_ref[...] = low_last


def own_kernel(idx, first_ref, taps_ref, last_ref, unit_ref):
    h, b = idx[3], idx[2]
    unit_ref[:, INNER:] = jnp.zeros_like(unit_ref[:, INNER:])
    for i in range(2):

        @pl.when((h == 0) & (b == i))
        def _():
            unit_ref[:, :INNER] = taps_ref[i]

        @pl.when((h == 1) & (b == i))
        def _():
            unit_ref[:, :INNER] = first_ref[:, i * INNER : (i + 1) * INNER]

        @pl.when((h == 2) & (b == i))
        def _():
            unit_ref[:, :INNER] = last_ref[:, i * INNER : (i + 1) * INNER]

        @pl.when((h == 3) & (b == i))
        def _():
            unit_ref[:, :INNER] = taps_ref[2 + i]
            unit_ref[:, INNER:] = taps_ref[4, :, i * TAIL : (i + 1) * TAIL]

    @pl.when(h > 3)
    def _():
        unit_ref[...] = jnp.zeros_like(unit_ref)


def finish_kernel(
    idx, old_ref, part_ref, tail_part, one_got, two_got, three_got, tail_got,
    sum_ref, tail_ref, new_ref, cross_ref,
):
    h = idx[3]

    def put(v):
        sum_ref[...] = v.astype(bf16)
        new_ref[:, :INNER] = (muon_keep * old_ref[:, :INNER] + v).astype(bf16)

    @pl.when(h == 0)
    def _():
        put(part_ref[...] + three_got[...].astype(f32))

    @pl.when((h == 1) | (h == 2))
    def _():
        put(part_ref[...] + one_got[...].astype(f32) + two_got[...].astype(f32) + three_got[...].astype(f32))

    @pl.when(h >= 3)
    def _():
        put(part_ref[...] + one_got[...].astype(f32))

    tail = tail_part[...] + tail_got[...].astype(f32)
    tail_ref[...] = tail.astype(bf16)
    new_ref[:, INNER:] = (muon_keep * old_ref[:, INNER:] + tail).astype(bf16)

    @pl.when(h == 3)
    def _():
        cross_ref[:, :TAIL] = new_ref[:, INNER:]
        cross_ref[:, TAIL:] = new_ref[:, INNER:]

    @pl.when(h != 3)
    def _():
        cross_ref[...] = new_ref[:, :INNER]


def block_kernel(idx, new_ref, got_ref, o_ref):
    h, b = idx[3], idx[2]
    long = (h == 1) | (h == 2)
    for i in range(2):

        @pl.when(long & (b == i))
        def _():
            o_ref[:, i * INNER : (i + 1) * INNER] = new_ref[:, :INNER]
            o_ref[:, (1 - i) * INNER : (2 - i) * INNER] = got_ref[...]

        @pl.when(jnp.logical_not(long) & (b == i))
        def _():
            o_ref[:, :INNER] = new_ref[:, :INNER]
            o_ref[:, INNER + i * TAIL : INNER + (i + 1) * TAIL] = new_ref[:, INNER:]
            o_ref[:, INNER + (1 - i) * TAIL : INNER + (2 - i) * TAIL] = got_ref[:, :TAIL]


def sweep(X, Xh, Xl, A, Bh, Rh, width, low, last, carry):
    scale, squares = carry
    n = X.shape[0]
    alpha = squares * scale * scale * (1.0 / n)
    outer = scale * scale
    rest = coef_second + 2.0 * coef_third * alpha
    keep = (coef_first + coef_second * alpha + coef_third * alpha * alpha) * scale
    if low:
        Bl = mul(Xh[:, :width], Xl[:, :width], NT)
        A[...] = Bl + Bl.T
    blocks = [(i, min(i + 256, n)) for i in range(0, n, 256)]
    for i, e in blocks:
        a = mul(Xh[i:e, :width], Xh[i:, :width], NT)
        if low:
            a = a + A[i:e, i:]
        row = lax.broadcasted_iota(jnp.int32, a.shape, 0)
        col = lax.broadcasted_iota(jnp.int32, a.shape, 1)
        a = a * outer - jnp.where(row == col, alpha, 0.0)
        A[i:e, i:] = a
        Bh[i:e, i:] = a.astype(bf16)
        if e < n:
            Bh[e:, i:e] = a[:, e - i :].T.astype(bf16)
    for i, e in blocks:
        p = rest * A[i:e, i:] + coef_third * mul(Bh[i:e, :], Bh[:, i:], NN)
        Rh[i:e, i:] = p.astype(bf16)
        if e < n:
            Rh[e:, i:e] = p[:, e - i :].T.astype(bf16)
    total = jnp.zeros((8, 128), f32)
    for i in range(0, width, 256):
        c = slice(i, min(i + 256, width))
        v = keep * X[:, c] + scale * mul(Rh[...], Xh[:, c], NN)
        X[:, c] = v
        Xh[:, c] = v.astype(bf16)
        if last is not None:
            Xl[:, c] = (v - Xh[:, c].astype(f32)).astype(bf16)
        for q in range(0, c.stop - c.start, 128):
            w = v[:, q : q + 128]
            total = total + jnp.sum((w * w).reshape(n // 8, 8, 128), axis=0)
    return jnp.float32(1.0), jnp.sum(total)


def ortho_kernel(idx, own_ref, sib_ref, opp_ref, diag_ref, mine_ref, theirs_ref, X, Xh, Xl, A, Bh, Rh):
    n, C = X.shape
    k, y, h = idx[0], idx[1], idx[3]
    loc = own_ref.shape[0]
    long = (h == 1) | (h == 2)
    fifth = (h == 3) & (k == 1)
    blocks = (
        (2 * y + k, own_ref),
        (2 * y + 1 - k, sib_ref),
        (2 * (1 - y) + k, opp_ref),
        (2 * (1 - y) + 1 - k, diag_ref),
    )

    def load(first, count):
        total = jnp.zeros((8, count), f32)
        for place, ref in blocks:
            base = pl.multiple_of(place * loc, 32)
            for i in range(0, loc, 32):
                low = ref[i : i + 32, first : first + count]
                v = low.astype(f32)
                Xh[pl.ds(base + i, 32), :count] = low
                X[pl.ds(base + i, 32), :count] = v
                total = total + jnp.sum((v * v).reshape(4, 8, count), axis=0)
        squares = jnp.sum(total)
        return 1.0 / (jnp.sqrt(squares) + 1e-07), squares

    @pl.when(long)
    def _():
        carry = load(0, C)
        lax.fori_loop(0, 5, lambda i, c: sweep(X, Xh, Xl, A, Bh, Rh, C, False, None, c), carry)

    def taps(first):
        carry = load(first, INNER)
        carry = lax.fori_loop(0, 2, lambda i, c: sweep(X, Xh, Xl, A, Bh, Rh, INNER, False, True, c), carry)
        lax.fori_loop(0, 3, lambda i, c: sweep(X, Xh, Xl, A, Bh, Rh, INNER, True, True, c), carry)

    @pl.when(jnp.logical_not(long) & jnp.logical_not(fifth))
    def _():
        taps(0)

    @pl.when(fifth)
    def _():
        taps(INNER)

    mine_ref[...] = X[at(2 * y + k, loc), :].astype(bf16)
    theirs_ref[...] = X[at(2 * y + 1 - k, loc), :INNER].astype(bf16)


def step_kernel(idx, mine_ref, got_ref, o_ref, tail_ref):
    h, b, k = idx[3], idx[2], idx[0]

    @pl.when((h == 0) | ((h == 3) & (k == 0)) | (h > 3))
    def _():
        o_ref[...] = mine_ref[:, :INNER]

    @pl.when((h == 3) & (k == 1))
    def _():
        o_ref[...] = got_ref[...]

    for i in range(2):

        @pl.when(((h == 1) | (h == 2)) & (b == i))
        def _():
            o_ref[...] = mine_ref[:, i * INNER : (i + 1) * INNER]

        @pl.when((h == 3) & (k == 0) & (b == i))
        def _():
            tail_ref[...] = got_ref[:, i * TAIL : (i + 1) * TAIL]

        @pl.when((h == 3) & (k == 1) & (b == i))
        def _():
            tail_ref[...] = mine_ref[:, i * TAIL : (i + 1) * TAIL]

    @pl.when(h != 3)
    def _():
        tail_ref[...] = jnp.zeros_like(tail_ref)


def join_kernel(idx, own_ref, got_ref, tail_ref, tail_got, o_ref):
    h = idx[3]
    for q in range(2):

        @pl.when(h // 2 % 2 == q)
        def _():
            o_ref[:, q * INNER : (q + 1) * INNER] = own_ref[...]
            o_ref[:, (1 - q) * INNER : (2 - q) * INNER] = got_ref[...]
            o_ref[:, 2 * INNER :] = (tail_ref if q else tail_got)[...]


def apply_kernel(
    keep, rate_long, rate_tap, idx, own_ref, x_ref, z_ref, zx_ref, first_ref, taps_ref, last_ref,
    of_out, ot_out, ol_out, of_ref, ot_ref, ol_ref, sems,
):
    h, b = idx[3], idx[2]
    for odd in range(2):
        for i in range(2):

            @pl.when((h % 2 == odd) & (b == i))
            def _():
                even = (own_ref, x_ref) if odd == 0 else (z_ref, zx_ref)
                odds = (z_ref, zx_ref) if odd == 0 else (own_ref, x_ref)
                copies = []
                for n, r in enumerate(chunks(first_ref.shape[0], 32)):
                    for q in range(2):
                        e = even[q ^ i]
                        o = odds[q ^ i]
                        lanes = slice(q * INNER, (q + 1) * INNER)
                        tail = slice(q * TAIL, (q + 1) * TAIL)
                        of_ref[r, lanes] = keep * first_ref[r, lanes] + rate_long * o[r, :INNER].astype(f32)
                        ol_ref[r, lanes] = keep * last_ref[r, lanes] + rate_long * e[r, INNER : 2 * INNER].astype(f32)
                        ot_ref[q, r, :] = keep * taps_ref[q, r, :] + rate_tap * e[r, :INNER].astype(f32)
                        ot_ref[2 + q, r, :] = keep * taps_ref[2 + q, r, :] + rate_tap * o[
                            r, INNER : 2 * INNER
                        ].astype(f32)
                        ot_ref[4, r, tail] = keep * taps_ref[4, r, tail] + rate_tap * o[r, 2 * INNER :].astype(f32)
                    copies.append(pltpu.make_async_copy(of_ref.at[r], of_out.at[r], sems.at[0, n]))
                    copies.append(pltpu.make_async_copy(ot_ref.at[:, r], ot_out.at[:, r], sems.at[1, n]))
                    copies.append(pltpu.make_async_copy(ol_ref.at[r], ol_out.at[r], sems.at[2, n]))
                    for copy in copies[-3:]:
                        copy.start()
                for copy in copies:
                    copy.wait()


ROWS = 24


def vector_kernel(idx, two_ref, three_ref, one_ref, cot_ref, sq_ref, o_ref):
    y, c = idx[1], 2 * idx[1] + idx[0]
    o_ref[...] = jnp.zeros_like(o_ref)
    o_ref[pl.ds(y, 1), :] = one_ref[0:1, :]
    o_ref[pl.ds(2 + y, 1), :] = one_ref[1:2, :]
    two = two_ref[...].T
    three = three_ref[...].T
    wide = two_ref.shape[0]
    pieces = (two[2:3], two[0:1], two[1:2], three[2:3], three[0:1], three[1:2])
    for i, piece in enumerate(pieces):
        o_ref[pl.ds(4 + 6 * y + i, 1), :wide] = piece
    cot = cot_ref[...].T
    o_ref[pl.ds(16 + c, 1), : cot_ref.shape[0]] = cot[0:1]
    for i in range(3):
        o_ref[20 + i : 21 + i, :128] = sq_ref[i : i + 1, :]


def adam_kernel(v_ref, par_ref, mom_ref, sqr_ref, first_ref, second_ref, value_ref, root_ref, g):
    wide = INNER // 2
    g[0:4, :] = v_ref[0:4, :]
    for i in range(6):
        g[4 + i : 5 + i, :wide] = v_ref[4 + i : 5 + i, :wide]
        g[4 + i : 5 + i, wide:] = v_ref[10 + i : 11 + i, :wide]
    for i in range(2):
        g[10 + i : 11 + i, :wide] = v_ref[16 + 2 * i : 17 + 2 * i, :wide]
        g[10 + i : 11 + i, wide:] = v_ref[17 + 2 * i : 18 + 2 * i, :wide]
    per = INNER // 128
    for r in range(12):
        for q in range(per):
            at_row = slice(r * per + q, r * per + q + 1)
            grad = g[r : r + 1, q * 128 : (q + 1) * 128]
            par = par_ref[at_row, :]
            first = adam_first * mom_ref[at_row, :] + (1.0 - adam_first) * grad
            second = adam_second * sqr_ref[at_row, :] + (1.0 - adam_second) * grad * grad
            first_ref[at_row, :] = first
            second_ref[at_row, :] = second
            value_ref[at_row, :] = par - adam_rate * (
                (first / (1.0 - adam_first**STEP)) / (jnp.sqrt(second / (1.0 - adam_second**STEP)) + adam_eps)
                + decay_rate * par
            )
    count = v_ref[22:23, :128] * D
    root_ref[...] = jnp.zeros_like(root_ref)
    for i in range(2):
        root_ref[i : i + 1, :] = jnp.sqrt(v_ref[20 + i : 21 + i, :128] / count)


def after(value, *others):
    return lax.optimization_barrier((value, *others))[0]


def body(
    tokens,
    cotangent,
    lengths,
    valid_mask,
    weight_first,
    weight_dilated,
    weight_last,
    momentum_first,
    momentum_dilated,
    momentum_last,
    vector_params,
    vector_moment,
    vector_square,
):
    C = lax.axis_size("ch")
    S = lax.axis_size("seq")
    c = lax.axis_index("ch")
    s = lax.axis_index("seq")
    k = c % 2
    y = c // 2
    T = tokens.shape[0]
    half = T // 2
    loc = weight_first.shape[1]
    wide = 2 * loc
    col = D // C
    H = S // 2
    b = s % 2
    h = s // 2
    idx = jnp.stack([k, y, b, h, s, s * T + k * half]).astype(jnp.int32)

    sib = [(i, i ^ 1) for i in range(C)]
    opp = [(i, i ^ 2) for i in range(C)]
    xsw = [(i, i ^ 1) for i in range(S)]

    def swap_core(v):
        return lax.ppermute(v, "ch", sib)

    def swap_y(v):
        return lax.ppermute(v, "ch", opp)

    def swap_x(v):
        return lax.ppermute(v, "seq", xsw)

    def along_h(v, pairs):
        return lax.ppermute(v, "seq", [(2 * i + q, 2 * j + q) for i, j in pairs for q in range(2)])

    outer_pairs = []
    for i in range(S):
        for j in range(C):
            if j % 2 == 0 and i >= 1:
                outer_pairs.append((i * C + j, (i - 1) * C + (j ^ 1)))
            if j % 2 == 1 and i + 1 < S:
                outer_pairs.append((i * C + j, (i + 1) * C + (j ^ 1)))

    def swap_outer(v):
        return lax.ppermute(v, ("seq", "ch"), outer_pairs)

    w_first, w_taps, w_last = weight_first.T, jnp.swapaxes(weight_dilated, 1, 2), weight_last
    m_first, m_taps, m_last = momentum_first.T, jnp.swapaxes(momentum_dilated, 1, 2), momentum_last
    cot = cotangent.T
    valid = valid_mask.reshape(1, T)
    gain_shift = vector_params[: 2 * D].reshape(2, D)
    inner_rows = vector_params[2 * D : 2 * D + 6 * INNER].reshape(6, INNER)
    cols = lax.dynamic_slice_in_dim(inner_rows, y * wide, wide, 1).T
    flat = (VECTOR // 128, 128)
    flat_params = vector_params.reshape(flat)

    low_first, cot_all, cot_other, cot_sums = call(
        prep_kernel,
        [((loc, D), bf16), ((col, T), bf16), ((col, half), bf16), ((col, 128), f32)],
        [idx],
        [w_first, cot],
    )
    got_first = swap_core(low_first)
    cot_opp = swap_y(cot_all)
    cot_sib = swap_core(cot_other)

    rows = 128
    steps = half // rows
    hid_one, hat_one, slope_one, scale_one = pl.pallas_call(
        input_kernel,
        out_shape=[
            jax.ShapeDtypeStruct((half, D), bf16),
            jax.ShapeDtypeStruct((half, D), bf16),
            jax.ShapeDtypeStruct((half, D), bf16),
            jax.ShapeDtypeStruct((half, 128), f32),
        ],
        grid_spec=pltpu.PrefetchScalarGridSpec(
            num_scalar_prefetch=1,
            grid=(steps,),
            in_specs=[
                pl.BlockSpec((rows, D), lambda i, idx: (idx[0] * steps + i, 0)),
                pl.BlockSpec((2, D), lambda i, idx: (0, 0)),
            ],
            out_specs=[
                pl.BlockSpec((rows, D), lambda i, idx: (i, 0)),
                pl.BlockSpec((rows, D), lambda i, idx: (i, 0)),
                pl.BlockSpec((rows, D), lambda i, idx: (i, 0)),
                pl.BlockSpec((rows, 128), lambda i, idx: (i, 0)),
            ],
        ),
        compiler_params=pltpu.CompilerParams(vmem_limit_bytes=16 * MIB),
        cost_estimate=pl.CostEstimate(flops=5000000000, bytes_accessed=1000, transcendentals=0),
    )(after(idx, cot_all, low_first), tokens, gain_shift)

    (low_rest,) = call(
        rest_kernel, [((loc, D + KERNEL_TAPS * INNER), bf16)], [], [w_last, w_taps]
    )
    got_rest = swap_core(low_rest)

    full_first, inner_one, st_two = call(
        first_kernel,
        [((wide, D), bf16), ((wide, half), f32), ((8, half), f32)],
        [idx],
        [low_first, got_first, hid_one, cols],
    )
    st_two_got = after(swap_y(st_two), cot_sib, cot_opp)
    (cot_diag,) = call(other_half_kernel, [((col, half), bf16)], [idx], [cot_opp])
    cot_diag = swap_core(cot_diag)
    slab = ((wide, REACH), bf16)
    own_in, own_out, hat_two, slope_two = call(
        second_kernel,
        [slab, slab, ((wide, half), f32), ((wide, half), f32)],
        [idx],
        [inner_one, st_two, st_two_got, cols, valid],
        scratch=[((wide, half), bf16)],
    )
    opp_in, opp_out = swap_y(own_in), swap_y(own_out)
    sib_in, seq_out = swap_core(own_in), swap_outer(own_out)
    sib_opp_in, seq_opp_out = swap_core(opp_in), swap_y(seq_out)
    ext, inner_two, st_three, full_last, full_taps, masks = call(
        functools.partial(conv_kernel, S * T),
        [
            ((INNER, half + 2 * REACH), bf16),
            ((wide, half), f32),
            ((8, half), f32),
            ((wide, D), bf16),
            ((wide, KERNEL_TAPS * INNER), bf16),
            ((8, half), f32),
        ],
        [idx, lengths],
        [
            own_in, own_out, opp_in, opp_out, sib_in, sib_opp_in, seq_out, seq_opp_out,
            low_rest, got_rest, cols,
        ],
        scratch=[((KERNEL_TAPS * INNER, half), bf16)],
    )
    st_three_got = swap_y(st_three)
    gw, g_three = call(
        cotangent_kernel,
        [((D, half), bf16), ((wide, half), f32)],
        [idx],
        [full_last, cot_all, cot_sib, cot_opp, cot_diag],
    )
    hid_three, e_three, hat_three, part_three = call(
        third_kernel,
        [((wide, half), bf16), ((wide, half), f32), ((wide, half), f32), ((8, half), f32)],
        [],
        [inner_two, st_three, st_three_got, cols, g_three],
    )
    part_three_got = swap_y(part_three)
    dz_two, slab_in, slab_out, sums_three = call(
        third_back_kernel,
        [((wide, half), bf16), ((wide, REACH), bf16), ((wide, REACH), bf16), ((wide, 128), f32)],
        [idx],
        [e_three, hat_three, part_three, part_three_got, cols],
    )
    got_in, got_out = swap_core(slab_in), swap_outer(slab_out)
    back_own, back_send = call(
        conv_back_kernel,
        [((wide, half), f32), ((wide, half), bf16)],
        [idx],
        [dz_two, got_in, got_out, masks, full_taps],
        scratch=[((wide, half + 2 * REACH), bf16), ((INNER, half), f32)],
    )
    back_got = swap_y(back_send)
    early_size = D + KERNEL_TAPS * INNER
    early_own, early_send = call(
        grads_kernel,
        [((loc, early_size), f32), ((loc, early_size), bf16)],
        [idx],
        [after(dz_two, back_send), ext, masks, hid_three, gw],
        scratch=[((wide, early_size), f32)],
        limit=32,
    )
    early_got = swap_core(early_send)
    unit, unit_low = ((loc, INNER), f32), ((loc, INNER), bf16)
    last_keep, last_send, taps_keep, taps_send = call(
        early_kernel,
        [unit, unit_low, ((loc, 2 * INNER + TAIL), f32), ((loc, 2 * INNER + TAIL), bf16)],
        [idx],
        [early_own, early_got],
    )
    last_got, taps_got = swap_x(last_send), swap_x(taps_send)
    e_two, part_two = call(
        second_back_kernel,
        [((wide, half), f32), ((8, half), f32)],
        [],
        [after(back_own, taps_send), back_got, slope_two, hat_two, cols],
    )
    half_out = [((half, HALF_D), f32), ((half, HALF_D), bf16)]
    branch_own, branch_send = call(
        halves_kernel, half_out, [idx], [after(hid_three, back_send), full_last], scratch=[((half, D), f32)]
    )
    part_two_got = after(swap_y(part_two), branch_send)
    branch_got = swap_y(after(branch_send, part_two_got))
    dz_one, first_own, first_send, sums_two = call(
        first_back_kernel,
        [((wide, half), bf16), ((loc, D), f32), ((loc, D), bf16), ((wide, 128), f32)],
        [idx],
        [e_two, hat_two, part_two, part_two_got, st_two, st_two_got, cols, hid_one],
        scratch=[((wide, D), f32)],
    )
    first_got = swap_core(first_send)
    back_own, back_send = call(
        halves_kernel, half_out, [idx], [dz_one, full_first], scratch=[((half, D), f32)]
    )
    first_keep, first_low = call(
        pair_kernel, [unit, unit_low], [idx], [after(first_own, back_send), first_got]
    )
    first_low = after(first_low, taps_got, last_got)
    first_got = swap_x(first_low)

    span = H
    while span > 4:
        span //= 2
        fold = [(i + span, i) for i in range(span)]

        def folded(keep, got):
            total = keep + got.astype(f32)
            return total + along_h(total.astype(bf16), fold).astype(f32), jnp.zeros_like(got)

        first_keep, first_got = folded(first_keep, first_got)
        last_keep, last_got = folded(last_keep, last_got)
        taps_keep, taps_got = folded(taps_keep, taps_got)
    line = 4

    size_taps = (loc, INNER + TAIL)
    sum_taps, send_taps = call(
        taps_kernel, [((loc, 2 * INNER + TAIL), f32), (size_taps, bf16)], [idx], [taps_keep, taps_got]
    )
    got_taps = along_h(send_taps, [(i, i ^ 1) for i in range(line)])
    tail_low = ((loc, TAIL), bf16)
    part_unit, part_tail, *sends, tail_send = call(
        line_kernel,
        [unit, ((loc, TAIL), f32), unit_low, unit_low, unit_low, tail_low],
        [idx],
        [first_keep, first_got, last_keep, last_got, sum_taps, got_taps],
    )
    got_units = [along_h(v, pairs) for v, pairs in zip(sends, LINE)]
    got_tail = along_h(tail_send, LINE_TAIL)
    back_got = swap_y(back_send)
    def whole_block(shape):
        return pl.BlockSpec(shape, lambda i, idx: (0, 0))

    out_mine, out_send, squares = pl.pallas_call(
        output_kernel,
        out_shape=[
            jax.ShapeDtypeStruct((col, half), f32),
            jax.ShapeDtypeStruct((col, half), f32),
            jax.ShapeDtypeStruct((8, 128), f32),
        ],
        grid_spec=pltpu.PrefetchScalarGridSpec(
            num_scalar_prefetch=1,
            grid=(1,),
            in_specs=[
                whole_block((half, HALF_D)),
                whole_block((half, HALF_D)),
                pl.BlockSpec((half, HALF_D), lambda i, idx: (idx[0], idx[1])),
                whole_block((VECTOR // 128, 128)),
                whole_block((1, T)),
            ],
            out_specs=[whole_block((col, half)), whole_block((col, half)), whole_block((8, 128))],
            scratch_shapes=[pltpu.VMEM((HALF_D, half), f32)],
        ),
        compiler_params=pltpu.CompilerParams(vmem_limit_bytes=24 * MIB),
        cost_estimate=pl.CostEstimate(flops=1000, bytes_accessed=1000, transcendentals=0),
    )(idx, branch_own, branch_got, tokens, flat_params, valid)
    e_one, part_one, sums_one = call(
        token_kernel,
        [((half, HALF_D), f32), ((half, 128), f32), ((8, HALF_D), f32)],
        [idx],
        [back_own, back_got, slope_one, hat_one, gain_shift],
    )
    (part_one,) = call(flip_kernel, [((8, half), f32)], [], [part_one])
    (vector,) = call(
        vector_kernel, [((ROWS, INNER), f32)], [idx], [sums_two, sums_three, sums_one, cot_sums, squares]
    )
    (old_unit,) = call(own_kernel, [(size_taps, f32)], [idx], [m_first, m_taps, m_last])
    sum_unit, sum_tail, new_unit, cross = call(
        finish_kernel,
        [unit_low, tail_low, (size_taps, bf16), unit_low],
        [idx],
        [old_unit, part_unit, part_tail, *got_units, got_tail],
    )
    cross_got = swap_x(after(cross, squares, back_got))
    (block,) = call(block_kernel, [((loc, D), bf16)], [idx], [new_unit, cross_got])

    def far_along_z(unit, tail):
        return along_h(unit, [(i, i ^ 2) for i in range(4)]), along_h(tail, LINE_TAIL)

    sum_far, tail_far = far_along_z(sum_unit, sum_tail)
    block_sib, block_opp = swap_core(block), swap_y(block)
    block_diag = swap_core(after(block_opp, sum_far, tail_far, vector))

    def joined_with(unit, got, tail, tail_got):
        return call(
            join_kernel, [((loc, 2 * INNER + TAIL), bf16)], [idx], [unit, got, tail, tail_got]
        )[0]

    def next_along_z(joined):
        return along_h(joined, [(i, i ^ 1) for i in range(4)])

    def spread(parts):
        span = 4
        while span < H:
            pairs = [(i, i + span) for i in range(span)]
            parts = [jnp.where((h >= span) & (h < 2 * span), along_h(v, pairs), v) for v in parts]
            span *= 2
        return parts

    def apply(keep, rate_long, rate_tap, parts, first, taps, last):
        shapes = [(loc, D), (KERNEL_TAPS, loc, INNER), (loc, D)]
        return pl.pallas_call(
            functools.partial(apply_kernel, keep, rate_long, rate_tap),
            out_shape=[jax.ShapeDtypeStruct(shape, f32) for shape in shapes],
            in_specs=[SMEM] + [VMEM] * 7,
            out_specs=[pl.BlockSpec(memory_space=pl.ANY)] * 3,
            scratch_shapes=[pltpu.VMEM(shape, f32) for shape in shapes] + [pltpu.SemaphoreType.DMA((3, loc // 32))],
            compiler_params=pltpu.CompilerParams(vmem_limit_bytes=16 * MIB),
            cost_estimate=pl.CostEstimate(flops=1000, bytes_accessed=1000, transcendentals=0),
        )(idx, *parts, first, taps, last)

    joined = joined_with(sum_unit, sum_far, sum_tail, tail_far)
    vector_x = swap_x(vector)
    mine, theirs = call(
        ortho_kernel,
        [((loc, D), bf16), ((loc, INNER), bf16)],
        [idx],
        [after(block, joined, vector_x), block_sib, block_opp, block_diag],
        scratch=[
            ((INNER, D), f32),
            ((INNER, D), bf16),
            ((INNER, INNER), bf16),
            ((INNER, INNER), f32),
            ((INNER, INNER), bf16),
            ((INNER, INNER), bf16),
        ],
        limit=32,
        flops=14 * 10**9,
    )
    joined_x = swap_x(joined)
    other = next_along_z(joined)
    part_got = swap_y(part_one)
    vector = vector + vector_x
    vector_core = swap_core(vector)
    theirs_got = swap_core(theirs)
    step_unit, step_tail = call(
        step_kernel, [unit_low, ((loc, TAIL), bf16)], [idx], [after(mine, joined_x, other, vector_core, part_got), theirs_got]
    )
    other_x = swap_x(after(other, step_unit))
    mom_parts = spread([joined, joined_x, other, other_x])

    vector = vector + vector_core
    vector = vector + swap_y(vector)
    step_far, tail_far = far_along_z(step_unit, step_tail)
    grad_mine, grad_send = call(
        token_back_kernel,
        [((col, half), f32), ((col, half), f32)],
        [idx],
        [after(e_one, step_unit), hat_one, scale_one, part_one, part_got],
        scratch=[((half, HALF_D), f32), ((HALF_D, half), f32)],
    )
    joined = joined_with(after(step_unit, vector, other_x, grad_send), step_far, step_tail, tail_far)
    joined_x = swap_x(joined)
    other = after(next_along_z(joined), joined_x)

    grad_got, out_got = swap_core(grad_send), swap_core(out_send)
    vector = vector + lax.ppermute(vector, "seq", [(i, i ^ 2) for i in range(S)])
    other, vector, grad_got, out_got = lax.optimization_barrier((other, vector, grad_got, out_got))
    other_x = swap_x(other)
    bit = 4
    while bit < S:
        vector = vector + lax.ppermute(vector, "seq", [(i, i ^ bit) for i in range(S)])
        bit *= 2
    (block_output,) = call(place_kernel, [((col, T), f32)], [idx], [out_mine, out_got])
    (tokens_grad,) = call(place_add_kernel, [((col, T), f32)], [idx], [grad_mine, grad_got, cot])
    vector_first, vector_second, vector_values, root = call(
        adam_kernel,
        [(flat, f32)] * 3 + [((8, 128), f32)],
        [],
        [vector, flat_params, vector_moment.reshape(flat), vector_square.reshape(flat)],
        scratch=[((12, INNER), f32)],
    )
    vector_first, vector_second, vector_values = (
        v.reshape(VECTOR) for v in (vector_first, vector_second, vector_values)
    )
    root_means = root[:2, 0]
    new_first, new_taps, new_last = apply(
        muon_keep, 1.0, 1.0, [after(mom_parts[0], other), *mom_parts[1:]], m_first, m_taps, m_last
    )
    keep_weight = 1.0 - muon_rate * decay_rate
    rate = muon_rate * muon_scale
    out_first, out_taps, out_last = apply(
        keep_weight,
        -rate * math.sqrt(D),
        -rate * math.sqrt(INNER),
        spread([joined, joined_x, other, other_x]),
        w_first,
        w_taps,
        w_last,
    )
    return (
        block_output.T,
        tokens_grad.T,
        out_first.T,
        jnp.swapaxes(out_taps, 1, 2),
        out_last,
        new_first.T,
        jnp.swapaxes(new_taps, 1, 2),
        new_last,
        vector_first,
        vector_second,
        vector_values,
        root_means,
    )


def solution(mesh):
    placed = (
        P("seq", None),
        P("seq", "ch"),
        P(),
        P("seq"),
        P(None, "ch"),
        P(None, None, "ch"),
        P("ch", None),
        P(None, "ch"),
        P(None, None, "ch"),
        P("ch", None),
        P(),
        P(),
        P(),
    )
    return jax.shard_map(
        body,
        mesh=mesh,
        in_specs=placed,
        out_specs=(
            P("seq", "ch"),
            P("seq", "ch"),
            P(None, "ch"),
            P(None, None, "ch"),
            P("ch", None),
            P(None, "ch"),
            P(None, None, "ch"),
            P("ch", None),
            P(),
            P(),
            P(),
            P(),
        ),
        check_vma=False,
    )
```
